256 devices in a mesh: slide: 8 (over z), tile: 32 (over y, x, core).
Axes of the slice: x: 4, y: 4, z: 8, core: 2. Of those that a mesh axis runs over, the one named last changes fastest.
Arguments:
- features: bfloat16 [8, 448, 98, 384], P('slide', 'tile'), may hold values from -6 to 6
- cotangent: bfloat16 [8, 448, 98, 384], P('slide', 'tile'), may hold values from -6 to 6
- owner_slot: int32 [8, 64, 14], P('slide'), may hold values from -1 to 511, as said below
- dw_weight: float32 [7, 7, 384], replicated, may hold values from -0.875 to 0.875
- dw_bias: float32 [384], replicated, may hold values from -3 to 3
- ln_gain: float32 [384], replicated, may hold values from 0.1 to 1.9
- ln_bias: float32 [384], replicated, may hold values from -3 to 3
- w_in: bfloat16 [384, 1536], replicated, may hold values from -0.3125 to 0.3125
- b_in: float32 [1536], replicated, may hold values from -3 to 3
- w_out: bfloat16 [1536, 384], replicated, may hold values from -0.15625 to 0.15625
- b_out: float32 [384], replicated, may hold values from -3 to 3
- layer_scale: float32 [384], replicated, may hold values from 0.25 to 1
Outputs:
- mixed: bfloat16 [8, 448, 98, 384], P('slide', 'tile')
- grad_dw_weight: float32 [7, 7, 384], replicated
- grad_dw_bias: float32 [384], replicated
- grad_ln_gain: float32 [384], replicated
- grad_ln_bias: float32 [384], replicated
- grad_w_in: float32 [384, 1536], replicated
- grad_b_in: float32 [1536], replicated
- grad_w_out: float32 [1536, 384], replicated
- grad_b_out: float32 [384], replicated
- grad_layer_scale: float32 [384], replicated
The draws below stay inside these ranges and needn't reach their ends.
Inputs may be any that keep to these rules, and one draw needn't show every extreme that they name: `owner_slot`: -1 marks a background tile; every other value o names owner device o // 16; each value 0 to 511 appears exactly once in each slide, so every owner device holds 16 tissue tiles. Of the tissue tiles in the 2 rows of one device, at most 1 goes to any one owner device, and for some pair of sender and owner exactly 1 does. In each slide the 2 rows of one device are tissue in all 14 columns.
All inputs are finite; a program needn't handle non-finite values.
Results may differ from the reference program's by a relative error of at most 0.0071.
Values may be sent and summed in bfloat16 or wider, within the bound.
A program may use at most 128 MiB of HBM per device.

```python
import math
import jax
import jax.numpy as jnp
from jax import lax

C = 384
HID = 1536
K = 7
TP = 7
COLS = 14
RPD = 2
OWN = 16
NR = 64
SLIDES = 8
LIVE = 512


def draw_owner_slot(key, part):
    key = jax.random.fold_in(key, 7)
    device_count = NR // RPD

    def one_slide(slide_key):
        keys = jax.random.split(slide_key, 5)
        levels = jax.random.randint(keys[0], (device_count,), 0, 64)
        busiest = jax.random.randint(keys[1], (), 0, device_count)
        levels = jnp.where(jnp.arange(device_count) == busiest, 4096, levels)
        row_levels = jnp.repeat(levels, RPD)
        noise = jax.random.randint(keys[2], (NR, COLS), 0, 64)
        scores = (row_levels[:, None] + noise) * (NR * COLS) + jnp.arange(NR * COLS, dtype=jnp.int32).reshape(NR, COLS)
        unused, chosen = lax.top_k(scores.reshape(-1), LIVE)
        alive = jnp.zeros((NR * COLS,), jnp.int32).at[chosen].set(1)
        rank_all = jnp.cumsum(alive) - 1
        dev_perm = jax.random.permutation(keys[3], device_count)
        slot_perm = jax.random.permutation(keys[4], OWN)
        safe_rank = jnp.maximum(rank_all, 0)
        owners = dev_perm[safe_rank % device_count] * OWN + slot_perm[safe_rank // device_count]
        return jnp.where(alive == 1, owners, -1).reshape(NR, COLS).astype(jnp.int32)
    return jax.vmap(one_slide)(jax.random.split(key, SLIDES))


def level_of(own_key, shape, cuts, least, top_value):
    def one(axis_at, shards_of):
        steps = jax.random.uniform(jax.random.fold_in(jax.random.fold_in(own_key, 6), axis_at), (shards_of,), jnp.float32, least / len(cuts), top_value / len(cuts))
        return jnp.repeat(jnp.exp(steps), shape[axis_at] // shards_of).reshape((-1,) + (1,) * (len(shape) - axis_at - 1))

    loudness = one(*cuts[0])
    for cut in cuts[1:]:
        loudness = loudness * one(*cut)
    return loudness


def gaussian(own_key, shape, width, most, cuts=(), held_as=jnp.bfloat16):
    loudness = level_of(own_key, shape, cuts, -0.22, 0.18) if cuts else 1.0
    entries = jax.random.normal(own_key, shape, jnp.float32) * width * loudness
    return jnp.minimum(jnp.maximum(entries, -most), most).astype(held_as)


def setup_inputs(seed: int = 0) -> dict:
    arg_keys = jax.random.split(jax.random.key(seed), 13)
    features = gaussian(arg_keys[0], (SLIDES, NR * TP, COLS * TP, C), 1.0, 6.0, ((0, 8), (1, 32)))
    cotangent = gaussian(arg_keys[1], (SLIDES, NR * TP, COLS * TP, C), 1.0, 6.0, ((0, 8), (1, 32)))
    owner_slot = draw_owner_slot(jax.random.fold_in(arg_keys[12], 71), 0)
    dw_weight = gaussian(arg_keys[3], (K, K, C), (K * K) ** -0.5, 0.875, (), jnp.float32)
    dw_bias = gaussian(arg_keys[4], (C,), 0.5, 3.0, (), jnp.float32)
    ln_gain = jnp.clip(1.0 + 0.18 * jax.random.normal(arg_keys[5], (C,), jnp.float32), 0.1, 1.9)
    ln_bias = gaussian(arg_keys[6], (C,), 0.5, 3.0, (), jnp.float32)
    w_in = gaussian(arg_keys[7], (C, HID), C ** -0.5, 0.3125)
    b_in = gaussian(arg_keys[8], (HID,), 0.5, 3.0, (), jnp.float32)
    w_out = gaussian(arg_keys[9], (HID, C), HID ** -0.5, 0.15625)
    b_out = gaussian(arg_keys[10], (C,), 0.5, 3.0, (), jnp.float32)
    layer_scale = jnp.clip(jnp.exp(jax.random.uniform(arg_keys[11], (C,), jnp.float32, math.log(0.25), math.log(1.0))), 0.25, 1.0)
    return {"features": features, "cotangent": cotangent, "owner_slot": owner_slot, "dw_weight": dw_weight, "dw_bias": dw_bias, "ln_gain": ln_gain, "ln_bias": ln_bias, "w_in": w_in, "b_in": b_in, "w_out": w_out, "b_out": b_out, "layer_scale": layer_scale}


def gelu_parts(pre_act):
    prob_mass = 0.5 * (1.0 + jax.scipy.special.erf(pre_act * 0.7071067811865476))
    density = jnp.exp(-0.5 * pre_act * pre_act) * 0.3989422804014327
    return (pre_act * prob_mass, prob_mass + pre_act * density)

def depthwise(padded, weight, offset, height, breadth):
    summed = jnp.zeros((height, breadth, padded.shape[2]), jnp.float32) + offset
    for row_tap in range(K):
        for col_tap in range(K):
            summed = summed + padded[row_tap:row_tap + height, col_tap:col_tap + breadth, :].astype(jnp.float32) * weight[row_tap, col_tap]
    return summed

def conv_grad(padded, grad_conv, height, breadth):
    pieces = []
    for row_tap in range(K):
        for col_tap in range(K):
            window = padded[row_tap:row_tap + height, col_tap:col_tap + breadth, :].astype(jnp.float32)
            pieces.append(lax.optimization_barrier(jnp.sum(window * grad_conv, axis=(0, 1))))
    return jnp.stack(pieces).reshape(K, K, -1)

def normalize(conv_out, ln_gain, ln_bias):
    mean_val = lax.optimization_barrier(jnp.mean(conv_out, axis=-1, keepdims=True))
    shifted = conv_out - mean_val
    var_val = lax.optimization_barrier(jnp.mean(shifted * shifted, axis=-1, keepdims=True))
    inv_std = lax.rsqrt(var_val + 1e-06)
    centred = shifted * inv_std
    return (centred, inv_std, centred * ln_gain + ln_bias)

def mlp_block(normed, cot_rows, live_rows, w_in, b_in, w_out, b_out, layer_scale, loss_scale):
    pre_act = jnp.dot(normed, w_in, preferred_element_type=jnp.float32) + b_in
    activ, slope = gelu_parts(pre_act)
    hidden = activ.astype(jnp.bfloat16)
    branch = (jnp.dot(hidden, w_out, preferred_element_type=jnp.float32) + b_out).astype(jnp.bfloat16)
    grad_branch = loss_scale * layer_scale * cot_rows.astype(jnp.float32) * live_rows
    grad_branch_b = grad_branch.astype(jnp.bfloat16)
    grad_b_out = lax.optimization_barrier(jnp.sum(grad_branch, axis=0))
    grad_w_out = jnp.dot(hidden.T, grad_branch_b, preferred_element_type=jnp.float32)
    grad_pre = jnp.dot(grad_branch_b, w_out.T, preferred_element_type=jnp.float32) * slope
    grad_pre_b = grad_pre.astype(jnp.bfloat16)
    grad_b_in = lax.optimization_barrier(jnp.sum(grad_pre, axis=0))
    grad_w_in = jnp.dot(normed.T, grad_pre_b, preferred_element_type=jnp.float32)
    grad_xn = jnp.dot(grad_pre_b, w_in.T, preferred_element_type=jnp.float32).astype(jnp.bfloat16)
    return (branch, grad_xn, (grad_w_in, grad_b_in, grad_w_out, grad_b_out))

def to_tiles(spatial):
    return spatial.reshape(NR, TP, COLS, TP, C).transpose(0, 2, 1, 3, 4).reshape(NR * COLS, TP, TP, C)

def from_tiles(tiles):
    return tiles.reshape(NR, COLS, TP, TP, C).transpose(0, 2, 1, 3, 4).reshape(NR * TP, COLS * TP, C)

def reference(features, cotangent, owner_slot, dw_weight, dw_bias, ln_gain, ln_bias, w_in, b_in, w_out, b_out, layer_scale):
    loss_scale = 1.0 / math.sqrt(SLIDES * LIVE * TP * TP)
    reach = K // 2
    height = NR * TP
    breadth = COLS * TP

    def one_slide(inputs):
        slide_feat, slide_cot, owners = inputs
        tile_live = (owners >= 0).astype(jnp.float32)
        tissue = jnp.repeat(jnp.repeat(tile_live, TP, axis=0), TP, axis=1)[:, :, None]
        masked = (slide_feat.astype(jnp.float32) * tissue).astype(jnp.bfloat16)
        padded = jnp.pad(masked, ((reach, reach), (reach, reach), (0, 0)))
        conv_out = depthwise(padded, dw_weight, dw_bias, height, breadth)
        centred, inv_std, normed_f = normalize(conv_out, ln_gain, ln_bias)
        normed = normed_f.astype(jnp.bfloat16)
        flat_owner = owners.reshape(-1)
        target = jnp.where(flat_owner >= 0, flat_owner, LIVE).astype(jnp.int32)
        places = jnp.zeros((LIVE,), jnp.int32).at[target].set(jnp.arange(NR * COLS, dtype=jnp.int32), mode='drop')
        live_xn = to_tiles(normed)[places].reshape(LIVE * TP * TP, C)
        live_cot = to_tiles(slide_cot)[places].reshape(LIVE * TP * TP, C)
        branch_rows, grad_rows, weight_grads = mlp_block(live_xn, live_cot, 1.0, w_in, b_in, w_out, b_out, layer_scale, loss_scale)
        branch_tiles = jnp.zeros((NR * COLS, TP, TP, C), branch_rows.dtype).at[places].set(branch_rows.reshape(LIVE, TP, TP, C))
        grad_tiles = jnp.zeros((NR * COLS, TP, TP, C), grad_rows.dtype).at[places].set(grad_rows.reshape(LIVE, TP, TP, C))
        branch = from_tiles(branch_tiles).astype(jnp.float32)
        grad_xn = from_tiles(grad_tiles).astype(jnp.float32)
        cot_f = slide_cot.astype(jnp.float32)
        mixed = (tissue * (slide_feat.astype(jnp.float32) + layer_scale * branch)).astype(jnp.bfloat16)
        grad_scale = loss_scale * lax.optimization_barrier(jnp.sum(tissue * cot_f * branch, axis=(0, 1)))
        grad_gain = lax.optimization_barrier(jnp.sum(grad_xn * centred, axis=(0, 1)))
        grad_lnb = lax.optimization_barrier(jnp.sum(grad_xn, axis=(0, 1)))
        scaled = grad_xn * ln_gain
        grad_conv = inv_std * (scaled - lax.optimization_barrier(jnp.mean(scaled, axis=-1, keepdims=True)) - centred * lax.optimization_barrier(jnp.mean(scaled * centred, axis=-1, keepdims=True)))
        grad_dwb = lax.optimization_barrier(jnp.sum(grad_conv, axis=(0, 1)))
        grad_dw = conv_grad(padded, grad_conv, height, breadth)
        grad_w1, grad_b1, grad_w2, grad_b2 = weight_grads
        return (mixed, (grad_dw, grad_dwb, grad_gain, grad_lnb, grad_w1, grad_b1, grad_w2, grad_b2, grad_scale))
    mixed, grads = lax.map(one_slide, (features, cotangent, owner_slot))
    summed = [lax.optimization_barrier(jnp.sum(item, axis=0)) for item in grads]
    return (mixed, summed[0], summed[1], summed[2], summed[3], summed[4], summed[5], summed[6], summed[7], summed[8])
```

```python
import math

import jax
import jax.numpy as jnp
from jax import lax
from jax.sharding import PartitionSpec as P

C = 384
K = 7
TP = 7
COLS = 14
OWN = 16


def with_halo(block, sides, width):
    for axis, dim in sides:
        count = lax.axis_size(axis)
        forward = [(i, i + 1) for i in range(count - 1)]
        backward = [(target, source) for source, target in forward]
        low = lax.ppermute(
            lax.slice_in_dim(block, block.shape[dim] - width, None, axis=dim), axis, forward
        )
        high = lax.ppermute(lax.slice_in_dim(block, 0, width, axis=dim), axis, backward)
        block = jnp.concatenate([low, block, high], axis=dim)
    return block


def gelu_parts(pre_act):
    prob_mass = 0.5 * (1.0 + jax.scipy.special.erf(pre_act * 0.7071067811865476))
    density = jnp.exp(-0.5 * pre_act * pre_act) * 0.3989422804014327
    return (pre_act * prob_mass, prob_mass + pre_act * density)


def depthwise(padded, weight, offset, height, breadth):
    summed = jnp.zeros((height, breadth, padded.shape[2]), jnp.float32) + offset
    for row_tap in range(K):
        for col_tap in range(K):
            summed = (
                summed
                + padded[row_tap : row_tap + height, col_tap : col_tap + breadth, :].astype(
                    jnp.float32
                )
                * weight[row_tap, col_tap]
            )
    return summed


def conv_grad(padded, grad_conv, height, breadth):
    pieces = []
    for row_tap in range(K):
        for col_tap in range(K):
            window = padded[row_tap : row_tap + height, col_tap : col_tap + breadth, :].astype(
                jnp.float32
            )
            pieces.append(jnp.sum(window * grad_conv, axis=(0, 1)))
    return jnp.stack(pieces).reshape(K, K, -1)


def normalize(conv_out, ln_gain, ln_bias):
    mean_val = jnp.mean(conv_out, axis=-1, keepdims=True)
    shifted = conv_out - mean_val
    var_val = jnp.mean(shifted * shifted, axis=-1, keepdims=True)
    inv_std = lax.rsqrt(var_val + 1e-06)
    centred = shifted * inv_std
    return (centred, inv_std, centred * ln_gain + ln_bias)


def contract_rows(left, right):
    return lax.dot_general(
        left, right, (((0,), (0,)), ((), ())), preferred_element_type=jnp.float32
    )


def contract_cols(left, right):
    return lax.dot_general(
        left, right, (((1,), (1,)), ((), ())), preferred_element_type=jnp.float32
    )


def mlp_block(normed, cot_rows, live_rows, w_in, b_in, w_out, b_out, layer_scale, loss_scale):
    pre_act = jnp.dot(normed, w_in, preferred_element_type=jnp.float32) + b_in
    activ, slope = gelu_parts(pre_act)
    hidden = activ.astype(jnp.bfloat16)
    branch = (jnp.dot(hidden, w_out, preferred_element_type=jnp.float32) + b_out).astype(
        jnp.bfloat16
    )
    grad_branch = loss_scale * layer_scale * cot_rows.astype(jnp.float32) * live_rows
    grad_branch_b = grad_branch.astype(jnp.bfloat16)
    grad_b_out = jnp.sum(grad_branch, axis=0)
    grad_w_out = contract_rows(hidden, grad_branch_b)
    grad_pre = contract_cols(grad_branch_b, w_out) * slope
    grad_pre_b = grad_pre.astype(jnp.bfloat16)
    grad_b_in = jnp.sum(grad_pre, axis=0)
    grad_w_in = contract_rows(normed, grad_pre_b)
    grad_xn = contract_cols(grad_pre_b, w_in).astype(jnp.bfloat16)
    return (branch, grad_xn, (grad_w_in, grad_b_in, grad_w_out, grad_b_out))


def local(
    features,
    cotangent,
    owner_slot,
    dw_weight,
    dw_bias,
    ln_gain,
    ln_bias,
    w_in,
    b_in,
    w_out,
    b_out,
    layer_scale,
):
    reach = K // 2
    ntile = lax.axis_size("tile")
    nslide = lax.axis_size("slide")
    loss_scale = 1.0 / math.sqrt(nslide * OWN * ntile * TP * TP)
    my_index = lax.axis_index("tile")
    breadth = COLS * TP
    height = features.shape[1]
    rows_here = height // TP
    tiles_here = rows_here * COLS
    table = owner_slot[0]
    mine = lax.dynamic_slice_in_dim(table, my_index * rows_here, rows_here, 0)
    my_live = mine >= 0
    tile_mask = my_live.astype(jnp.float32)
    tissue = jnp.repeat(jnp.repeat(tile_mask, TP, axis=0), TP, axis=1)[:, :, None]
    slide_feat = features[0]
    slide_cot = cotangent[0]
    masked = slide_feat * tissue.astype(jnp.bfloat16)
    grown = with_halo(masked, (("tile", 0),), reach)
    padded = jnp.pad(grown, ((0, 0), (reach, reach), (0, 0)))
    conv_out = depthwise(padded, dw_weight, dw_bias, height, breadth)
    centred, inv_std, normed_f = normalize(conv_out, ln_gain, ln_bias)
    normed = normed_f.astype(jnp.bfloat16)
    live_rows = tissue.reshape(height * breadth, 1)
    branch_rows, grad_rows, weight_grads = mlp_block(
        normed.reshape(height * breadth, C),
        slide_cot.reshape(height * breadth, C),
        live_rows,
        w_in,
        b_in,
        w_out,
        b_out,
        layer_scale,
        loss_scale,
    )
    branch = branch_rows.reshape(height, breadth, C)
    grad_xn = grad_rows.reshape(height, breadth, C)
    branch_f = branch.astype(jnp.float32)
    grad_xf = grad_xn.astype(jnp.float32)
    mixed = (tissue * (slide_feat.astype(jnp.float32) + layer_scale * branch_f)).astype(
        jnp.bfloat16
    )
    grad_scale = loss_scale * jnp.sum(
        tissue * slide_cot.astype(jnp.float32) * branch_f, axis=(0, 1)
    )
    grad_gain = jnp.sum(grad_xf * centred, axis=(0, 1))
    grad_lnb = jnp.sum(grad_xf, axis=(0, 1))
    scaled = grad_xf * ln_gain
    grad_conv = inv_std * (
        scaled
        - jnp.mean(scaled, axis=-1, keepdims=True)
        - centred * jnp.mean(scaled * centred, axis=-1, keepdims=True)
    )
    grad_dwb = jnp.sum(grad_conv, axis=(0, 1))
    grad_dw = conv_grad(padded, grad_conv, height, breadth)
    grad_w1, grad_b1, grad_w2, grad_b2 = weight_grads
    small = (grad_dw, grad_dwb, grad_gain, grad_lnb, grad_b1, grad_b2, grad_scale)
    packed = jnp.concatenate([item.reshape(-1) for item in small]).reshape(-1, C)
    large = jnp.concatenate([grad_w1.reshape(-1, C), grad_w2], axis=0).astype(jnp.bfloat16)
    packed = lax.psum(packed, ("slide", "tile"))
    large = lax.psum(large, ("slide", "tile")).astype(jnp.float32)
    half = grad_w1.size // C
    sums = []
    start = 0
    for item in small:
        rows = item.size // C
        sums.append(packed[start : start + rows].reshape(item.shape))
        start += rows
    dw, dwb, gain, lnb, b1, b2, scale = sums
    return (
        mixed[None],
        dw,
        dwb,
        gain,
        lnb,
        large[:half].reshape(grad_w1.shape),
        b1,
        large[half:],
        b2,
        scale,
    )


def solution(mesh):
    placed = (
        P("slide", "tile", None, None),
        P("slide", "tile", None, None),
        P("slide", None, None),
        P(),
        P(),
        P(),
        P(),
        P(),
        P(),
        P(),
        P(),
        P(),
    )
    return jax.shard_map(
        local,
        mesh=mesh,
        in_specs=placed,
        out_specs=(P("slide", "tile", None, None), P(), P(), P(), P(), P(), P(), P(), P(), P()),
        check_vma=False,
    )
```

```python
import math

import jax
import jax.numpy as jnp
from jax import lax
from jax.experimental import pallas as pl
from jax.experimental.pallas import tpu as pltpu
from jax.sharding import PartitionSpec as P

C = 384
K = 7
TP = 7
COLS = 14
OWN = 16


CORES = 2
SIZES = {"x": 4, "y": 4, "z": 8}
LANES = 128
MESH = pl.DeviceIdType.MESH


def coordinates():
    tile = lax.axis_index("tile")
    return {
        "z": lax.axis_index("slide"),
        "y": tile // 8,
        "x": (tile // 2) % 4,
        "core": tile % 2,
    }


def device_at(where):
    return (where["z"], where["y"] * 8 + where["x"] * 2 + where["core"])


def peer_along(where, axis, distance):
    size = SIZES[axis]
    position = (where[axis] + distance) % size
    return position, device_at({**where, axis: position})


def enter(where):
    peers = [device_at({**where, "core": 1 - where["core"]})]
    for axis, size in SIZES.items():
        peers += [peer_along(where, axis, step)[1] for step in range(1, size)]
    barrier = pltpu.get_barrier_semaphore()
    for peer in peers:
        pl.semaphore_signal(barrier, inc=1, device_id=peer, device_id_type=MESH)
    pl.semaphore_wait(barrier, len(peers))


class Sum:
    def __init__(self, rows, dtype, scatter, exchange):
        self.rows, self.dtype = rows, dtype
        self.scatter, self.exchange = scatter, exchange
        self.heights = [rows]
        for axis in scatter:
            self.heights.append(self.heights[-1] // SIZES[axis])
        self.copies = 2 + 2 * sum(SIZES[a] - 1 for a in scatter) + sum(SIZES[a] - 1 for a in exchange)

    def scratch(self):
        shapes = [pltpu.VMEM((self.rows, LANES), self.dtype)]
        for axis, before, after in zip(self.scatter, self.heights, self.heights[1:]):
            shapes.append(pltpu.VMEM((before, LANES), jnp.float32))
            shapes.append(pltpu.VMEM((before, LANES), self.dtype))
            shapes.append(pltpu.VMEM((SIZES[axis] - 1, after, LANES), self.dtype))
        for axis in self.exchange:
            shapes.append(pltpu.VMEM((SIZES[axis], self.heights[-1], LANES), self.dtype))
        shapes.append(pltpu.SemaphoreType.DMA((self.copies,)))
        shapes.append(pltpu.SemaphoreType.DMA((self.copies,)))
        return shapes

    def bind(self, where, keep, send, result, refs):
        refs = list(refs)
        self.where, self.keep, self.send, self.result = where, keep, send, result
        self.landed = refs.pop(0)
        self.levels = [tuple(refs.pop(0) for _ in range(3)) for _ in self.scatter]
        self.slots = [refs.pop(0) for _ in self.exchange]
        self.send_sems, self.recv_sems = refs
        self.used = 0
        self.flying = []
        self.done = []
        self.phase = 0
        offset = 0
        self.offsets = [offset]
        for axis, height in zip(self.scatter, self.heights[1:]):
            offset = offset + where[axis] * height
            self.offsets.append(offset)
        return self

    def copy(self, source, target, device):
        made = pltpu.make_async_remote_copy(
            src_ref=source,
            dst_ref=target,
            send_sem=self.send_sems.at[self.used],
            recv_sem=self.recv_sems.at[self.used],
            device_id=device,
            device_id_type=MESH,
        )
        self.used += 1
        made.start()
        self.flying.append(made)

    def land(self):
        for made in self.flying:
            made.wait_recv()
        self.done += self.flying
        self.flying = []

    def rows_at(self, level):
        return pl.ds(pl.multiple_of(self.offsets[level], 16), self.heights[level])

    def start_core(self):
        other = device_at({**self.where, "core": 1 - self.where["core"]})
        self.copy(self.send, self.landed, other)

    def start_scatter(self, index, total):
        axis, height = self.scatter[index], self.heights[index + 1]
        held, outgoing, incoming = self.levels[index]
        held[...] = total
        outgoing[...] = total.astype(self.dtype)
        for step in range(1, SIZES[axis]):
            position, device = peer_along(self.where, axis, step)
            self.copy(
                outgoing.at[pl.ds(pl.multiple_of(position * height, 16), height), :],
                incoming.at[step - 1],
                device,
            )

    def finish_scatter(self, index):
        axis, height = self.scatter[index], self.heights[index + 1]
        held, _, incoming = self.levels[index]
        total = held[pl.ds(pl.multiple_of(self.where[axis] * height, 16), height), :]
        for step in range(SIZES[axis] - 1):
            total = total + incoming[step].astype(jnp.float32)
        return total

    def start_exchange(self, index, total):
        axis, slots = self.exchange[index], self.slots[index]
        me = self.where[axis]
        slots[me] = total.astype(self.dtype)
        for step in range(1, SIZES[axis]):
            _, device = peer_along(self.where, axis, step)
            self.copy(slots.at[me], slots.at[me], device)

    def finish_exchange(self, index):
        axis, slots = self.exchange[index], self.slots[index]
        total = slots[0].astype(jnp.float32)
        for place in range(1, SIZES[axis]):
            total = total + slots[place].astype(jnp.float32)
        return total

    def start_gather(self, index):
        axis, core = self.scatter[index], self.where["core"]
        block = self.result.at[core, self.rows_at(index + 1), :]
        for step in range(1, SIZES[axis]):
            _, device = peer_along(self.where, axis, step)
            self.copy(block, block, device)

    def advance(self):
        deep, wide = len(self.scatter), len(self.exchange)
        phase, core = self.phase, self.where["core"]
        self.phase += 1
        self.land()
        if phase == 0:
            self.start_core()
            return True
        if phase == 1:
            total = self.keep[...].astype(jnp.float32) + self.landed[...].astype(jnp.float32)
            self.start_scatter(0, total)
            return True
        if phase <= deep + wide:
            if phase <= deep:
                total = self.finish_scatter(phase - 2)
                self.start_scatter(phase - 1, total)
                return True
            index = phase - deep - 1
            total = self.finish_scatter(deep - 1) if index == 0 else self.finish_exchange(index - 1)
            self.start_exchange(index, total)
            return True
        step = phase - deep - wide - 1
        if step == 0:
            total = self.finish_exchange(wide - 1)
            self.result[core, self.rows_at(deep), :] = total.astype(self.dtype)
        if step < deep:
            self.start_gather(deep - 1 - step)
            return True
        if step == deep:
            other = device_at({**self.where, "core": 1 - core})
            self.copy(self.result.at[core], self.result.at[core], other)
            return True
        for made in self.done:
            made.wait_send()
        return False


def sums():
    large = [
        Sum(1536, jnp.bfloat16, scatter, exchange)
        for scatter, exchange in ((("x", "z"), ("y",)), (("y", "z"), ("x",)), (("z", "y"), ("x",)))
    ]
    return large + [Sum(128, jnp.float32, ("z",), ("x", "y"))]


def sum_kernel(large_ref, small_ref, large_out, small_out, large_held, small_held, out_sems, *refs):
    where = coordinates()
    enter(where)
    core = where["core"]
    refs = list(refs)
    running = []
    for index, item in enumerate(sums()):
        count = len(item.scratch())
        mine, refs = refs[:count], refs[count:]
        if index < 3:
            item.bind(
                where,
                large_ref.at[index, core],
                large_ref.at[index, 1 - core],
                large_held.at[index],
                mine,
            )
        else:
            item.bind(where, small_ref.at[core], small_ref.at[1 - core], small_held, mine)
        running.append(item)
    going = list(running)
    while going:
        going = [item for item in going if item.advance()]
    outs = [
        pltpu.make_async_copy(large_held, large_out, out_sems.at[0]),
        pltpu.make_async_copy(small_held, small_out, out_sems.at[1]),
    ]
    for made in outs:
        made.start()
    for made in outs:
        made.wait()


def sum_all(large, small):
    scratch = [
        pltpu.VMEM(large.shape, large.dtype),
        pltpu.VMEM(small.shape, small.dtype),
        pltpu.SemaphoreType.DMA((2,)),
    ]
    for item in sums():
        scratch += item.scratch()
    return pl.pallas_call(
        sum_kernel,
        out_shape=(
            jax.ShapeDtypeStruct(large.shape, large.dtype),
            jax.ShapeDtypeStruct(small.shape, small.dtype),
        ),
        in_specs=[pl.BlockSpec(memory_space=pltpu.VMEM)] * 2,
        out_specs=(pl.BlockSpec(memory_space=pl.ANY),) * 2,
        scratch_shapes=scratch,
        compiler_params=pltpu.CompilerParams(
            collective_id=0, has_side_effects=True, vmem_limit_bytes=50 * 1024 * 1024
        ),
    )(large, small)


def pack_large(grad_w1, grad_w2):
    first = grad_w1.reshape(C, 3, 4, LANES).transpose(1, 2, 0, 3).reshape(3, 1, 1536, LANES)
    second = grad_w2.reshape(3, 512, 3, LANES).transpose(0, 2, 1, 3).reshape(3, 1, 1536, LANES)
    return jnp.concatenate([first, second], axis=1).astype(jnp.bfloat16)


def unpack_large(summed):
    first = summed[:, 0].reshape(3, 4, C, LANES).transpose(2, 0, 1, 3).reshape(C, 1536)
    second = summed[:, 1].reshape(3, 3, 512, LANES).transpose(0, 2, 1, 3).reshape(1536, C)
    return first.astype(jnp.float32), second.astype(jnp.float32)


def with_halo(block, sides, width):
    for axis, dim in sides:
        count = lax.axis_size(axis)
        forward = [(i, i + 1) for i in range(count - 1)]
        backward = [(target, source) for source, target in forward]
        low = lax.ppermute(
            lax.slice_in_dim(block, block.shape[dim] - width, None, axis=dim), axis, forward
        )
        high = lax.ppermute(lax.slice_in_dim(block, 0, width, axis=dim), axis, backward)
        block = jnp.concatenate([low, block, high], axis=dim)
    return block


def gelu_parts(pre_act):
    prob_mass = 0.5 * (1.0 + jax.scipy.special.erf(pre_act * 0.7071067811865476))
    density = jnp.exp(-0.5 * pre_act * pre_act) * 0.3989422804014327
    return (pre_act * prob_mass, prob_mass + pre_act * density)


def depthwise(padded, weight, offset, height, breadth):
    summed = jnp.zeros((height, breadth, padded.shape[2]), jnp.float32) + offset
    for row_tap in range(K):
        for col_tap in range(K):
            summed = (
                summed
                + padded[row_tap : row_tap + height, col_tap : col_tap + breadth, :].astype(
                    jnp.float32
                )
                * weight[row_tap, col_tap]
            )
    return summed


def conv_grad(padded, grad_conv, height, breadth):
    pieces = []
    for row_tap in range(K):
        for col_tap in range(K):
            window = padded[row_tap : row_tap + height, col_tap : col_tap + breadth, :].astype(
                jnp.float32
            )
            pieces.append(jnp.sum(window * grad_conv, axis=(0, 1)))
    return jnp.stack(pieces).reshape(K, K, -1)


def normalize(conv_out, ln_gain, ln_bias):
    mean_val = jnp.mean(conv_out, axis=-1, keepdims=True)
    shifted = conv_out - mean_val
    var_val = jnp.mean(shifted * shifted, axis=-1, keepdims=True)
    inv_std = lax.rsqrt(var_val + 1e-06)
    centred = shifted * inv_std
    return (centred, inv_std, centred * ln_gain + ln_bias)


def contract_rows(left, right):
    return lax.dot_general(
        left, right, (((0,), (0,)), ((), ())), preferred_element_type=jnp.float32
    )


def contract_cols(left, right):
    return lax.dot_general(
        left, right, (((1,), (1,)), ((), ())), preferred_element_type=jnp.float32
    )


def mlp_block(normed, cot_rows, live_rows, w_in, b_in, w_out, b_out, layer_scale, loss_scale):
    pre_act = jnp.dot(normed, w_in, preferred_element_type=jnp.float32) + b_in
    activ, slope = gelu_parts(pre_act)
    hidden = activ.astype(jnp.bfloat16)
    branch = (jnp.dot(hidden, w_out, preferred_element_type=jnp.float32) + b_out).astype(
        jnp.bfloat16
    )
    grad_branch = loss_scale * layer_scale * cot_rows.astype(jnp.float32) * live_rows
    grad_branch_b = grad_branch.astype(jnp.bfloat16)
    grad_b_out = jnp.sum(grad_branch, axis=0)
    grad_w_out = contract_rows(hidden, grad_branch_b)
    grad_pre = contract_cols(grad_branch_b, w_out) * slope
    grad_pre_b = grad_pre.astype(jnp.bfloat16)
    grad_b_in = jnp.sum(grad_pre, axis=0)
    grad_w_in = contract_rows(normed, grad_pre_b)
    grad_xn = contract_cols(grad_pre_b, w_in).astype(jnp.bfloat16)
    return (branch, grad_xn, (grad_w_in, grad_b_in, grad_w_out, grad_b_out))


def local(
    features,
    cotangent,
    owner_slot,
    dw_weight,
    dw_bias,
    ln_gain,
    ln_bias,
    w_in,
    b_in,
    w_out,
    b_out,
    layer_scale,
):
    reach = K // 2
    ntile = lax.axis_size("tile")
    nslide = lax.axis_size("slide")
    loss_scale = 1.0 / math.sqrt(nslide * OWN * ntile * TP * TP)
    my_index = lax.axis_index("tile")
    breadth = COLS * TP
    height = features.shape[1]
    rows_here = height // TP
    tiles_here = rows_here * COLS
    table = owner_slot[0]
    mine = lax.dynamic_slice_in_dim(table, my_index * rows_here, rows_here, 0)
    my_live = mine >= 0
    tile_mask = my_live.astype(jnp.float32)
    tissue = jnp.repeat(jnp.repeat(tile_mask, TP, axis=0), TP, axis=1)[:, :, None]
    slide_feat = features[0]
    slide_cot = cotangent[0]
    masked = slide_feat * tissue.astype(jnp.bfloat16)
    grown = with_halo(masked, (("tile", 0),), reach)
    padded = jnp.pad(grown, ((0, 0), (reach, reach), (0, 0)))
    conv_out = depthwise(padded, dw_weight, dw_bias, height, breadth)
    centred, inv_std, normed_f = normalize(conv_out, ln_gain, ln_bias)
    normed = normed_f.astype(jnp.bfloat16)
    live_rows = tissue.reshape(height * breadth, 1)
    branch_rows, grad_rows, weight_grads = mlp_block(
        normed.reshape(height * breadth, C),
        slide_cot.reshape(height * breadth, C),
        live_rows,
        w_in,
        b_in,
        w_out,
        b_out,
        layer_scale,
        loss_scale,
    )
    branch = branch_rows.reshape(height, breadth, C)
    grad_xn = grad_rows.reshape(height, breadth, C)
    branch_f = branch.astype(jnp.float32)
    grad_xf = grad_xn.astype(jnp.float32)
    mixed = (tissue * (slide_feat.astype(jnp.float32) + layer_scale * branch_f)).astype(
        jnp.bfloat16
    )
    grad_scale = loss_scale * jnp.sum(
        tissue * slide_cot.astype(jnp.float32) * branch_f, axis=(0, 1)
    )
    grad_gain = jnp.sum(grad_xf * centred, axis=(0, 1))
    grad_lnb = jnp.sum(grad_xf, axis=(0, 1))
    scaled = grad_xf * ln_gain
    grad_conv = inv_std * (
        scaled
        - jnp.mean(scaled, axis=-1, keepdims=True)
        - centred * jnp.mean(scaled * centred, axis=-1, keepdims=True)
    )
    grad_dwb = jnp.sum(grad_conv, axis=(0, 1))
    grad_dw = conv_grad(padded, grad_conv, height, breadth)
    grad_w1, grad_b1, grad_w2, grad_b2 = weight_grads
    small = (grad_dw, grad_dwb, grad_gain, grad_lnb, grad_b1, grad_b2, grad_scale)
    packed = jnp.concatenate([item.reshape(-1) for item in small])
    packed = jnp.pad(packed, (0, 2 * LANES * LANES - packed.size)).reshape(2, LANES, LANES)
    large, packed = sum_all(pack_large(grad_w1, grad_w2), packed)
    packed = packed.reshape(-1)
    grad_w1, grad_w2 = unpack_large(large)
    parts = []
    start = 0
    for item in small:
        parts.append(packed[start : start + item.size].reshape(item.shape))
        start += item.size
    dw, dwb, gain, lnb, b1, b2, scale = parts
    return (
        mixed[None],
        dw,
        dwb,
        gain,
        lnb,
        grad_w1,
        b1,
        grad_w2,
        b2,
        scale,
    )


def solution(mesh):
    placed = (
        P("slide", "tile", None, None),
        P("slide", "tile", None, None),
        P("slide", None, None),
        P(),
        P(),
        P(),
        P(),
        P(),
        P(),
        P(),
        P(),
        P(),
    )
    return jax.shard_map(
        local,
        mesh=mesh,
        in_specs=placed,
        out_specs=(P("slide", "tile", None, None), P(), P(), P(), P(), P(), P(), P(), P(), P()),
        check_vma=False,
    )
```

```python
import math

import jax
import jax.numpy as jnp
from jax import lax
from jax.experimental import pallas as pl
from jax.experimental.pallas import tpu as pltpu
from jax.sharding import PartitionSpec as P

C = 384
HID = 1536
K = 7
TP = 7
COLS = 14
OWN = 16
ROWS = 14
BREADTH = 98
WIDE = 104
CELLS = ROWS * WIDE
PADDED = 1536
REACH = 3
CHUNK = 512
CHUNKS = HID // CHUNK
PAIR = 2 * WIDE
GROUPS = C // 128
LOSS_SCALE = 1.0 / math.sqrt(8 * 32 * OWN * TP * TP)

CORES = 2
SIZES = {"x": 4, "y": 4, "z": 8}
LANES = 128
MESH = pl.DeviceIdType.MESH


def coordinates():
    tile = lax.axis_index("tile")
    return {
        "z": lax.axis_index("slide"),
        "y": tile // 8,
        "x": (tile // 2) % 4,
        "core": tile % 2,
    }


def device_at(where):
    return (where["z"], where["y"] * 8 + where["x"] * 2 + where["core"])


def peer_along(where, axis, distance):
    size = SIZES[axis]
    position = (where[axis] + distance) % size
    return position, device_at({**where, axis: position})


def enter(where):
    tile = lax.axis_index("tile")
    peers = [device_at({**where, "core": 1 - where["core"]})]
    peers += [(where["z"], (tile + step) % 32) for step in (1, 31)]
    for axis, size in SIZES.items():
        peers += [peer_along(where, axis, step)[1] for step in range(1, size)]
    barrier = pltpu.get_barrier_semaphore()
    for peer in peers:
        pl.semaphore_signal(barrier, inc=1, device_id=peer, device_id_type=MESH)
    pl.semaphore_wait(barrier, len(peers))


class Sum:
    def __init__(self, rows, dtype, scatter, exchange):
        self.rows, self.dtype = rows, dtype
        self.scatter, self.exchange = scatter, exchange
        self.heights = [rows]
        for axis in scatter:
            self.heights.append(self.heights[-1] // SIZES[axis])
        self.copies = 2 + 2 * sum(SIZES[a] - 1 for a in scatter) + sum(SIZES[a] - 1 for a in exchange)

    def scratch(self):
        shapes = [pltpu.VMEM((self.rows, LANES), jnp.float32)]
        for axis, before, after in zip(self.scatter, self.heights, self.heights[1:]):
            shapes.append(pltpu.VMEM((before, LANES), jnp.float32))
            shapes.append(pltpu.VMEM((before, LANES), self.dtype))
            shapes.append(pltpu.VMEM((SIZES[axis] - 1, after, LANES), self.dtype))
        for axis in self.exchange:
            shapes.append(pltpu.VMEM((SIZES[axis], self.heights[-1], LANES), self.dtype))
        shapes.append(pltpu.SemaphoreType.DMA((self.copies,)))
        shapes.append(pltpu.SemaphoreType.DMA((self.copies,)))
        return shapes

    def bind(self, where, keep, send, result, refs):
        refs = list(refs)
        self.where, self.keep, self.send, self.result = where, keep, send, result
        self.landed = refs.pop(0)
        self.levels = [tuple(refs.pop(0) for _ in range(3)) for _ in self.scatter]
        self.slots = [refs.pop(0) for _ in self.exchange]
        self.send_sems, self.recv_sems = refs
        self.used = 0
        self.flying = []
        self.done = []
        self.phase = 0
        offset = 0
        self.offsets = [offset]
        for axis, height in zip(self.scatter, self.heights[1:]):
            offset = offset + where[axis] * height
            self.offsets.append(offset)
        return self

    def copy(self, source, target, device):
        made = pltpu.make_async_remote_copy(
            src_ref=source,
            dst_ref=target,
            send_sem=self.send_sems.at[self.used],
            recv_sem=self.recv_sems.at[self.used],
            device_id=device,
            device_id_type=MESH,
        )
        self.used += 1
        made.start()
        self.flying.append(made)

    def land(self):
        for made in self.flying:
            made.wait_recv()
        self.done += self.flying
        self.flying = []

    def rows_at(self, level):
        return pl.ds(pl.multiple_of(self.offsets[level], 16), self.heights[level])

    def start_core(self):
        other = device_at({**self.where, "core": 1 - self.where["core"]})
        self.copy(self.send, self.landed, other)

    def start_scatter(self, index, total):
        axis, height = self.scatter[index], self.heights[index + 1]
        held, outgoing, incoming = self.levels[index]
        held[...] = total
        outgoing[...] = total.astype(self.dtype)
        for step in range(1, SIZES[axis]):
            position, device = peer_along(self.where, axis, step)
            self.copy(
                outgoing.at[pl.ds(pl.multiple_of(position * height, 16), height), :],
                incoming.at[step - 1],
                device,
            )

    def finish_scatter(self, index):
        axis, height = self.scatter[index], self.heights[index + 1]
        held, _, incoming = self.levels[index]
        total = held[pl.ds(pl.multiple_of(self.where[axis] * height, 16), height), :]
        for step in range(SIZES[axis] - 1):
            total = total + incoming[step].astype(jnp.float32)
        return total

    def start_exchange(self, index, total):
        axis, slots = self.exchange[index], self.slots[index]
        me = self.where[axis]
        slots[me] = total.astype(self.dtype)
        for step in range(1, SIZES[axis]):
            _, device = peer_along(self.where, axis, step)
            self.copy(slots.at[me], slots.at[me], device)

    def finish_exchange(self, index):
        axis, slots = self.exchange[index], self.slots[index]
        total = slots[0].astype(jnp.float32)
        for place in range(1, SIZES[axis]):
            total = total + slots[place].astype(jnp.float32)
        return total

    def start_gather(self, index):
        axis, core = self.scatter[index], self.where["core"]
        block = self.result.at[core, self.rows_at(index + 1), :]
        for step in range(1, SIZES[axis]):
            _, device = peer_along(self.where, axis, step)
            self.copy(block, block, device)

    def advance(self):
        phase, core = self.phase, self.where["core"]
        deep, wide = len(self.scatter), len(self.exchange)
        if phase > 2 * deep + wide + 2:
            return False
        self.phase += 1
        self.land()
        if phase == 0:
            self.start_core()
            return True
        if phase == 1:
            total = self.keep[...] + self.landed[...]
            self.start_scatter(0, total)
            return True
        if phase <= deep + wide:
            if phase <= deep:
                total = self.finish_scatter(phase - 2)
                self.start_scatter(phase - 1, total)
                return True
            index = phase - deep - 1
            total = self.finish_scatter(deep - 1) if index == 0 else self.finish_exchange(index - 1)
            self.start_exchange(index, total)
            return True
        step = phase - deep - wide - 1
        if step == 0:
            total = self.finish_exchange(wide - 1)
            self.result[core, self.rows_at(deep), :] = total.astype(self.dtype)
        if step < deep:
            self.start_gather(deep - 1 - step)
            return True
        if step == deep:
            other = device_at({**self.where, "core": 1 - core})
            self.copy(self.result.at[core], self.result.at[core], other)
            return True
        for made in self.done:
            made.wait_send()
        return False


def lanes(group):
    return slice(group * LANES, (group + 1) * LANES)


def by_eight(value):
    return jnp.sum(value.reshape(-1, 8, LANES), axis=0)


def gelu_parts(pre_act):
    density = jnp.exp(-0.5 * pre_act * pre_act) * 0.3989422804014327
    t = pl.reciprocal(1.0 + 0.2316419 * jnp.abs(pre_act), approx=False)
    series = 1.781477937 + t * (-1.821255978 + t * 1.330274429)
    series = t * (0.319381530 + t * (-0.356563782 + t * series))
    tail = density * series
    mass = jnp.where(pre_act >= 0.0, 1.0 - tail, tail)
    return pre_act * mass, mass + pre_act * density


def fill(feat, cot, mask, padded, cot_masked):
    edge = jnp.zeros((3, ROWS + 2 * REACH, 8, LANES), jnp.float32)
    padded[:, :, 0:8, :] = edge
    padded[:, :, 104:112, :] = edge
    padded[:, :, 112:120, :] = edge
    cot_masked[:, :, 96:104, :] = jnp.zeros((3, ROWS, 8, LANES), jnp.float32)

    def row(i, carry):
        live = mask[1 + i // TP][:BREADTH]
        cells = feat[i].astype(jnp.float32)
        pull = cot[i].astype(jnp.float32)
        for group in range(GROUPS):
            padded[group, i + REACH, 8 : 8 + BREADTH, :] = cells[:, lanes(group)] * live
            cot_masked[group, i, 0:BREADTH, :] = pull[:, lanes(group)] * live
        return carry

    lax.fori_loop(0, ROWS, row, 0)


def fill_halo(halo, mask, padded):
    def row(i, carry):
        for side in range(2):
            live = mask[3 * side][:BREADTH]
            cells = halo[side, i].astype(jnp.float32)
            for group in range(GROUPS):
                padded[group, i + side * (ROWS + REACH), 8 : 8 + BREADTH, :] = (
                    cells[:, lanes(group)] * live
                )
        return carry

    lax.fori_loop(0, REACH, row, 0)


def spread_taps(weight, taps):
    for tap in range(K * K):
        for group in range(GROUPS):
            taps[group, tap] = jnp.broadcast_to(weight[tap : tap + 1, lanes(group)], (8, LANES))


def conv(padded, taps, bias, conv_out):
    def tile(step, carry):
        group, column = step // 13, step % 13
        total = jnp.zeros((ROWS, 8, LANES), jnp.float32) + bias[group]
        for col_tap in range(K):
            window = padded[group, :, pl.ds(8 * column + 5 + col_tap, 8), :]
            for row_tap in range(K):
                total = total + window[row_tap : row_tap + ROWS] * taps[group, row_tap * K + col_tap]
        conv_out[group, :, pl.ds(pl.multiple_of(8 * column, 8), 8), :] = total
        return carry

    lax.fori_loop(0, GROUPS * 13, tile, 0)


def conv_grad(first, last, padded, grad_conv, tap_sums):
    def tile(step, carry):
        group, column = step // 13, step % 13
        pull = grad_conv[group, :, pl.ds(pl.multiple_of(8 * column, 8), 8), :]
        for col_tap in range(K):
            window = padded[group, :, pl.ds(8 * column + 5 + col_tap, 8), :]
            for row_tap in range(K):
                tap = row_tap * K + col_tap
                tap_sums[group, tap] += jnp.sum(window[row_tap : row_tap + ROWS] * pull, axis=0)
        return carry

    lax.fori_loop(first, last, tile, 0)


def norm(conv_out, inv_std, gain, offset, normed):
    def pair(step, carry):
        rows = pl.ds(2 * step, 2)
        held = [conv_out[group, rows].reshape(PAIR, LANES) for group in range(GROUPS)]
        mean = jnp.sum(held[0] + held[1] + held[2], axis=-1, keepdims=True) * (1.0 / C)
        held = [item - mean for item in held]
        squares = held[0] * held[0] + held[1] * held[1] + held[2] * held[2]
        var = jnp.sum(squares, axis=-1, keepdims=True) * (1.0 / C)
        inv = jnp.broadcast_to(lax.rsqrt(var + 1e-06), (PAIR, LANES))
        inv_std[rows] = inv.reshape(2, WIDE, LANES)
        place = pl.ds(pl.multiple_of(step * PAIR, 16), PAIR)
        for group in range(GROUPS):
            centred = held[group] * inv
            conv_out[group, rows] = centred.reshape(2, WIDE, LANES)
            normed[place, lanes(group)] = (
                centred * gain[:, lanes(group)] + offset[:, lanes(group)]
            ).astype(jnp.bfloat16)
        return carry

    lax.fori_loop(0, ROWS // 2, pair, 0)


def branch_grad(cot_masked, scale, grad_branch, sums):
    def pair(step, carry):
        place = pl.ds(pl.multiple_of(step * PAIR, 16), PAIR)
        for group in range(GROUPS):
            pull = cot_masked[group, pl.ds(2 * step, 2)].reshape(PAIR, LANES)
            pull = pull * (scale[:, lanes(group)] * LOSS_SCALE)
            grad_branch[place, lanes(group)] = pull.astype(jnp.bfloat16)
            sums[group] += by_eight(pull)
        return carry

    lax.fori_loop(0, ROWS // 2, pair, 0)


def turn(rows, turned):
    def block(step, carry):
        place = pl.ds(pl.multiple_of(step * LANES, LANES), LANES)
        turned[:, place] = rows[place, :].T
        return carry

    lax.fori_loop(0, PADDED // LANES, block, 0)


def nt(left, right):
    return lax.dot_general(
        left, right, (((1,), (1,)), ((), ())), preferred_element_type=jnp.float32
    )


def mlp_rows(chunk, first, last, normed, grad_branch, w_in, b_in, w_out, b_out, work):
    hidden, grad_pre, branch, grad_xn, in_sums = work
    units = slice(chunk * CHUNK, (chunk + 1) * CHUNK)

    def block(step, carry):
        place = pl.ds(pl.multiple_of(step * PAIR, 16), PAIR)
        pre_act = jnp.dot(normed[place, :], w_in[:, units], preferred_element_type=jnp.float32)
        pre_act = pre_act + b_in[:, units]
        activ, slope = gelu_parts(pre_act)
        activ = activ.astype(jnp.bfloat16)
        hidden[place, :] = activ
        pull = nt(grad_branch[place, :], w_out[units, :]) * slope
        in_sums[:, units] += jnp.sum(pull.reshape(-1, 8, CHUNK), axis=0)
        pull = pull.astype(jnp.bfloat16)
        grad_pre[place, :] = pull
        out = jnp.dot(activ, w_out[units, :], preferred_element_type=jnp.float32)
        back = nt(pull, w_in[:, units])
        if chunk == 0:
            branch[place, :] = out + b_out[...]
            grad_xn[place, :] = back
        else:
            branch[place, :] += out
            grad_xn[place, :] += back
        return carry

    lax.fori_loop(first, last, block, 0)


def weight_grads(chunk, normed_t, grad_branch_t, hidden, grad_pre, large):
    first = jnp.dot(normed_t[...], grad_pre[...], preferred_element_type=jnp.float32)
    for group in range(CHUNK // LANES):
        large[chunk, 0, group * C : (group + 1) * C, :] = first[:, lanes(group)]
    second = jnp.dot(grad_branch_t[...], hidden[...], preferred_element_type=jnp.float32).T
    for group in range(GROUPS):
        large[chunk, 1, group * CHUNK : (group + 1) * CHUNK, :] = second[:, lanes(group)]


def after_mlp(branch, grad_xn, cot_masked, padded, centred, inv_std, mask, scale, gain, mixed, grad_conv, sums):
    def row(i, carry):
        place = pl.ds(pl.multiple_of(i * WIDE, 8), WIDE)
        live = mask[1 + i // TP]
        inv = inv_std[i]
        pulls, held = [], []
        for group in range(GROUPS):
            out = branch[place, lanes(group)].astype(jnp.bfloat16).astype(jnp.float32)
            sums[3 + group] += by_eight(cot_masked[group, i] * out)
            kept = padded[group, i + REACH, 8 : 8 + WIDE, :] + live * (scale[:, lanes(group)] * out)
            mixed[i, :, lanes(group)] = kept[:BREADTH].astype(jnp.bfloat16)
            pull = grad_xn[place, lanes(group)].astype(jnp.bfloat16).astype(jnp.float32)
            cen = centred[group, i]
            sums[6 + group] += by_eight(pull * cen)
            sums[9 + group] += by_eight(pull)
            pulls.append(pull * gain[:, lanes(group)])
            held.append(cen)
        mean = jnp.sum(pulls[0] + pulls[1] + pulls[2], axis=-1, keepdims=True) * (1.0 / C)
        along = pulls[0] * held[0] + pulls[1] * held[1] + pulls[2] * held[2]
        along = jnp.sum(along, axis=-1, keepdims=True) * (1.0 / C)
        for group in range(GROUPS):
            pull = inv * (pulls[group] - mean - held[group] * along)
            grad_conv[group, i] = pull
            sums[12 + group] += by_eight(pull)
        return carry

    lax.fori_loop(0, ROWS, row, 0)


def collect(tap_sums, sums, in_sums, small):
    def put(place, value):
        small[place // LANES, place % LANES : place % LANES + 1, :] = jnp.sum(
            value, axis=0, keepdims=True
        )

    small[1, 40:LANES, :] = jnp.zeros((LANES - 40, LANES), jnp.float32)
    for group in range(GROUPS):
        for tap in range(K * K):
            put(group * K * K + tap, tap_sums[group, tap])
    for index in range(15):
        value = sums[index]
        put(147 + index, value * LOSS_SCALE if 3 <= index < 6 else value)
    for group in range(HID // LANES):
        put(162 + group, in_sums[:, lanes(group)])


def plan():
    large = [
        Sum(1536, jnp.bfloat16, scatter, exchange)
        for scatter, exchange in ((("x", "z"), ("y",)), (("y", "z"), ("x",)), (("z", "y"), ("x",)))
    ]
    return large + [Sum(128, jnp.float32, ("z",), ("x", "y"))]


def work_scratch():
    def f32(*shape):
        return pltpu.VMEM(shape, jnp.float32)

    def b16(*shape):
        return pltpu.VMEM(shape, jnp.bfloat16)

    return [
        b16(2, REACH, BREADTH, C),
        pltpu.SemaphoreType.DMA((2,)),
        pltpu.SemaphoreType.DMA((2,)),
        f32(GROUPS, ROWS + 2 * REACH, 120, LANES),
        f32(GROUPS, ROWS, WIDE, LANES),
        f32(GROUPS, K * K, 8, LANES),
        f32(GROUPS, ROWS, WIDE, LANES),
        f32(ROWS, WIDE, LANES),
        b16(PADDED, C),
        b16(PADDED, C),
        b16(C, PADDED),
        b16(C, PADDED),
        b16(PADDED, CHUNK),
        b16(PADDED, CHUNK),
        f32(CELLS, C),
        f32(CELLS, C),
        f32(8, HID),
        f32(15, 8, LANES),
        f32(GROUPS, K * K, 8, LANES),
        f32(GROUPS, ROWS, WIDE, LANES),
        f32(CHUNKS, 2, 1536, LANES),
        f32(2, LANES, LANES),
        b16(CHUNKS, 2, 1536, LANES),
        f32(2, LANES, LANES),
        b16(ROWS, BREADTH, C),
        pltpu.SemaphoreType.DMA((3,)),
    ]


def block_kernel(
    feat, cot, mask, dw_weight, dw_bias, gain, offset, w_in, b_in, w_out, b_out, scale,
    mixed_out, large_out, small_out, *refs
):
    refs = list(refs)
    own = len(work_scratch())
    (
        halo, halo_send, halo_recv, padded, cot_masked, taps, centred, inv_std, normed, grad_branch,
        normed_t, grad_branch_t, hidden, grad_pre, branch, grad_xn, in_sums, sums, tap_sums,
        grad_conv, large, small, large_held, small_held, mixed, out_sems,
    ) = refs[:own]
    refs = refs[own:]
    where = coordinates()
    core, tile = where["core"], lax.axis_index("tile")
    enter(where)
    halves = []
    for side, step, first in ((0, 1, ROWS - REACH), (1, 31, 0)):
        made = pltpu.make_async_remote_copy(
            src_ref=feat.at[pl.ds(first, REACH)],
            dst_ref=halo.at[side],
            send_sem=halo_send.at[side],
            recv_sem=halo_recv.at[side],
            device_id=(where["z"], (tile + step) % 32),
            device_id_type=MESH,
        )
        made.start()
        halves.append(made)
    running = []
    for index, item in enumerate(plan()):
        count = len(item.scratch())
        mine, refs = refs[:count], refs[count:]
        if index < CHUNKS:
            keep, send = large.at[index, core], large.at[index, 1 - core]
            item.bind(where, keep, send, large_held.at[index], mine)
        else:
            item.bind(where, small.at[core], small.at[1 - core], small_held, mine)
        running.append(item)

    def advance(*which):
        for index in which:
            running[index].advance()

    fill(feat, cot, mask, padded, cot_masked)
    spread_taps(dw_weight, taps)
    sums[...] = jnp.zeros(sums.shape, jnp.float32)
    tap_sums[...] = jnp.zeros(tap_sums.shape, jnp.float32)
    in_sums[...] = jnp.zeros(in_sums.shape, jnp.float32)
    for rows in (normed, grad_branch, hidden, grad_pre):
        rows[CELLS:, :] = jnp.zeros((PADDED - CELLS, rows.shape[1]), jnp.bfloat16)
    branch_grad(cot_masked, scale, grad_branch, sums)
    turn(grad_branch, grad_branch_t)
    for made in halves:
        made.wait_recv()
    fill_halo(halo, mask, padded)
    conv(padded, taps, dw_bias, centred)
    norm(centred, inv_std, gain, offset, normed)
    turn(normed, normed_t)

    work = (hidden, grad_pre, branch, grad_xn, in_sums)
    weights = (normed, grad_branch, w_in, b_in, w_out, b_out, work)
    between = ((), (0,), (0, 1))
    for chunk in range(CHUNKS):
        mlp_rows(chunk, 0, 4, *weights)
        advance(*between[chunk])
        mlp_rows(chunk, 4, 7, *weights)
        weight_grads(chunk, normed_t, grad_branch_t, hidden, grad_pre, large)
        advance(*range(chunk + 1))
    after_mlp(
        branch, grad_xn, cot_masked, padded, centred, inv_std, mask, scale, gain, mixed, grad_conv, sums
    )
    mixed_copy = pltpu.make_async_copy(mixed, mixed_out, out_sems.at[0])
    mixed_copy.start()
    advance(0, 1, 2)
    steps = (0, 10, 20, 30, 39)
    for first, last in zip(steps, steps[1:]):
        conv_grad(first, last, padded, grad_conv, tap_sums)
        if last < 39:
            advance(0, 1, 2)
    collect(tap_sums, sums, in_sums, small)
    going = [running[3], running[0], running[1], running[2]]
    while going:
        going = [item for item in going if item.advance()]
    copies = [
        pltpu.make_async_copy(large_held, large_out, out_sems.at[1]),
        pltpu.make_async_copy(small_held, small_out, out_sems.at[2]),
    ]
    for made in copies:
        made.start()
    for made in copies + [mixed_copy]:
        made.wait()
    for made in halves:
        made.wait_send()


def run_block(*operands):
    scratch = work_scratch()
    for item in plan():
        scratch += item.scratch()
    return pl.pallas_call(
        block_kernel,
        out_shape=(
            jax.ShapeDtypeStruct((ROWS, BREADTH, C), jnp.bfloat16),
            jax.ShapeDtypeStruct((CHUNKS, 2, 1536, LANES), jnp.bfloat16),
            jax.ShapeDtypeStruct((2, LANES, LANES), jnp.float32),
        ),
        in_specs=[pl.BlockSpec(memory_space=pltpu.VMEM)] * len(operands),
        out_specs=(pl.BlockSpec(memory_space=pl.ANY),) * 3,
        scratch_shapes=scratch,
        compiler_params=pltpu.CompilerParams(
            collective_id=0, has_side_effects=True, vmem_limit_bytes=60 * 1024 * 1024
        ),
    )(*operands)


def finish_kernel(mixed_in, large, small, mixed, dw, dwb, ln_gain, ln_bias, w1, b1, w2, b2, scale):
    mixed[...] = mixed_in[...]
    for chunk in range(CHUNKS):
        for group in range(CHUNK // LANES):
            first = chunk * CHUNK + group * LANES
            w1[:, first : first + LANES] = large[chunk, 0, group * C : (group + 1) * C, :].astype(
                jnp.float32
            )
        for group in range(GROUPS):
            w2[chunk * CHUNK : (chunk + 1) * CHUNK, lanes(group)] = large[
                chunk, 1, group * CHUNK : (group + 1) * CHUNK, :
            ].astype(jnp.float32)

    def row(place):
        return small[place // LANES, place % LANES : place % LANES + 1, :]

    for group in range(GROUPS):
        for tap in range(K * K):
            dw[tap // K, tap % K : tap % K + 1, lanes(group)] = row(group * K * K + tap)
    for index, target in enumerate((b2, scale, ln_gain, ln_bias, dwb)):
        for group in range(GROUPS):
            target[:, lanes(group)] = row(147 + index * GROUPS + group)
    for group in range(HID // LANES):
        b1[:, lanes(group)] = row(162 + group)


def finish(mixed, large, small):
    def f32(*shape):
        return jax.ShapeDtypeStruct(shape, jnp.float32)

    vector = f32(1, C)
    return pl.pallas_call(
        finish_kernel,
        out_shape=(
            jax.ShapeDtypeStruct(mixed.shape, mixed.dtype), f32(K, K, C), vector, vector, vector,
            f32(C, HID), f32(1, HID), f32(HID, C), vector, vector,
        ),
        in_specs=[pl.BlockSpec(memory_space=pltpu.VMEM)] * 3,
        out_specs=(pl.BlockSpec(memory_space=pltpu.VMEM),) * 10,
        compiler_params=pltpu.CompilerParams(vmem_limit_bytes=40 * 1024 * 1024),
    )(mixed, large, small)


def tissue_rows(table):
    live = jnp.pad((table >= 0).astype(jnp.float32), ((1, 1), (0, 0)))
    mine = lax.dynamic_slice_in_dim(live, lax.axis_index("tile") * 2, 4, 0)
    cells = jnp.pad(jnp.repeat(mine, TP, axis=1), ((0, 0), (0, WIDE - BREADTH)))
    return jnp.broadcast_to(cells[:, :, None], (4, WIDE, LANES))


def local(
    features,
    cotangent,
    owner_slot,
    dw_weight,
    dw_bias,
    ln_gain,
    ln_bias,
    w_in,
    b_in,
    w_out,
    b_out,
    layer_scale,
):
    mixed, large, small = run_block(
        features[0],
        cotangent[0],
        tissue_rows(owner_slot[0]),
        dw_weight.reshape(K * K, C),
        dw_bias.reshape(GROUPS, 1, LANES),
        ln_gain.reshape(1, C),
        ln_bias.reshape(1, C),
        w_in,
        b_in.reshape(1, HID),
        w_out,
        b_out.reshape(1, C),
        layer_scale.reshape(1, C),
    )
    mixed, dw, dwb, gain, bias, w1, b1, w2, b2, scale = finish(mixed, large, small)
    return (
        mixed[None],
        dw,
        dwb.reshape(C),
        gain.reshape(C),
        bias.reshape(C),
        w1,
        b1.reshape(HID),
        w2,
        b2.reshape(C),
        scale.reshape(C),
    )


def solution(mesh):
    placed = (
        P("slide", "tile", None, None),
        P("slide", "tile", None, None),
        P("slide", None, None),
        P(),
        P(),
        P(),
        P(),
        P(),
        P(),
        P(),
        P(),
        P(),
    )
    return jax.shard_map(
        local,
        mesh=mesh,
        in_specs=placed,
        out_specs=(P("slide", "tile", None, None), P(), P(), P(), P(), P(), P(), P(), P(), P()),
        check_vma=False,
    )
```

```python
import math

import jax
import jax.numpy as jnp
from jax import lax
from jax.experimental import pallas as pl
from jax.experimental.pallas import tpu as pltpu
from jax.sharding import PartitionSpec as P

C = 384
HID = 1536
K = 7
TP = 7
COLS = 14
OWN = 16
ROWS = 14
BREADTH = 98
WIDE = 104
CELLS = ROWS * WIDE
PADDED = 1536
REACH = 3
CHUNK = 512
CHUNKS = HID // CHUNK
PAIR = 2 * WIDE
GROUPS = C // 128
LOSS_SCALE = 1.0 / math.sqrt(8 * 32 * OWN * TP * TP)

CORES = 2
SIZES = {"x": 4, "y": 4, "z": 8}
LANES = 128
MESH = pl.DeviceIdType.MESH


def coordinates():
    tile = lax.axis_index("tile")
    return {
        "z": lax.axis_index("slide"),
        "y": tile // 8,
        "x": (tile // 2) % 4,
        "core": tile % 2,
    }


def device_at(where):
    return (where["z"], where["y"] * 8 + where["x"] * 2 + where["core"])


def peer_along(where, axis, distance):
    size = SIZES[axis]
    position = (where[axis] + distance) % size
    return position, device_at({**where, axis: position})


def stack_peer(where, distance):
    place = (where["z"] * 2 + where["core"] + distance) % 16
    return place, device_at({**where, "z": place // 2, "core": place % 2})


def plane_peer(where, distance):
    place = (where["y"] * 4 + where["x"] + distance) % 16
    return place, device_at({**where, "y": place // 4, "x": place % 4})


def enter(where):
    tile = lax.axis_index("tile")
    peers = [(where["z"], (tile + step) % 32) for step in (1, 31)]
    for step in range(1, 16):
        peers += [stack_peer(where, step)[1], plane_peer(where, step)[1]]
    barrier = pltpu.get_barrier_semaphore()
    for peer in peers:
        pl.semaphore_signal(barrier, inc=1, device_id=peer, device_id_type=MESH)
    pl.semaphore_wait(barrier, len(peers))


class Sum:
    def __init__(self, rows, dtype, scatter, exchange):
        self.rows, self.dtype = rows, dtype
        self.scatter, self.exchange = scatter, exchange
        self.heights = [rows]
        for axis in scatter:
            self.heights.append(self.heights[-1] // SIZES[axis])
        self.phases = 2 * len(scatter) + len(exchange) + 3
        self.copies = 2 + 2 * sum(SIZES[a] - 1 for a in scatter) + sum(SIZES[a] - 1 for a in exchange)

    def scratch(self):
        shapes = [pltpu.VMEM((self.rows, LANES), jnp.float32)]
        for axis, before, after in zip(self.scatter, self.heights, self.heights[1:]):
            shapes.append(pltpu.VMEM((before, LANES), jnp.float32))
            shapes.append(pltpu.VMEM((before, LANES), self.dtype))
            shapes.append(pltpu.VMEM((SIZES[axis] - 1, after, LANES), self.dtype))
        for axis in self.exchange:
            shapes.append(pltpu.VMEM((SIZES[axis], self.heights[-1], LANES), self.dtype))
        shapes.append(pltpu.SemaphoreType.DMA((self.copies,)))
        shapes.append(pltpu.SemaphoreType.DMA((self.copies,)))
        return shapes

    def bind(self, where, keep, send, result, refs):
        refs = list(refs)
        self.where, self.keep, self.send, self.result = where, keep, send, result
        self.landed = refs.pop(0)
        self.levels = [tuple(refs.pop(0) for _ in range(3)) for _ in self.scatter]
        self.slots = [refs.pop(0) for _ in self.exchange]
        self.send_sems, self.recv_sems = refs
        self.used = 0
        self.flying = []
        self.done = []
        self.phase = 0
        offset = 0
        self.offsets = [offset]
        for axis, height in zip(self.scatter, self.heights[1:]):
            offset = offset + where[axis] * height
            self.offsets.append(offset)
        return self

    def copy(self, source, target, device):
        made = pltpu.make_async_remote_copy(
            src_ref=source,
            dst_ref=target,
            send_sem=self.send_sems.at[self.used],
            recv_sem=self.recv_sems.at[self.used],
            device_id=device,
            device_id_type=MESH,
        )
        self.used += 1
        made.start()
        self.flying.append(made)

    def land(self):
        for made in self.flying:
            made.wait_recv()
        self.done += self.flying
        self.flying = []

    def rows_at(self, level):
        return pl.ds(pl.multiple_of(self.offsets[level], 16), self.heights[level])

    def start_core(self):
        other = device_at({**self.where, "core": 1 - self.where["core"]})
        self.copy(self.send, self.landed, other)

    def start_scatter(self, index, total):
        axis, height = self.scatter[index], self.heights[index + 1]
        held, outgoing, incoming = self.levels[index]
        held[...] = total
        outgoing[...] = total.astype(self.dtype)
        for step in range(1, SIZES[axis]):
            position, device = peer_along(self.where, axis, step)
            self.copy(
                outgoing.at[pl.ds(pl.multiple_of(position * height, 16), height), :],
                incoming.at[step - 1],
                device,
            )

    def finish_scatter(self, index):
        axis, height = self.scatter[index], self.heights[index + 1]
        held, _, incoming = self.levels[index]
        total = held[pl.ds(pl.multiple_of(self.where[axis] * height, 16), height), :]
        for step in range(SIZES[axis] - 1):
            total = total + incoming[step].astype(jnp.float32)
        return total

    def start_exchange(self, index, total):
        axis, slots = self.exchange[index], self.slots[index]
        me = self.where[axis]
        slots[me] = total.astype(self.dtype)
        for step in range(1, SIZES[axis]):
            _, device = peer_along(self.where, axis, step)
            self.copy(slots.at[me], slots.at[me], device)

    def finish_exchange(self, index):
        axis, slots = self.exchange[index], self.slots[index]
        total = slots[0].astype(jnp.float32)
        for place in range(1, SIZES[axis]):
            total = total + slots[place].astype(jnp.float32)
        return total

    def start_gather(self, index):
        axis, core = self.scatter[index], self.where["core"]
        block = self.result.at[core, self.rows_at(index + 1), :]
        for step in range(1, SIZES[axis]):
            _, device = peer_along(self.where, axis, step)
            self.copy(block, block, device)

    def advance(self):
        phase, core = self.phase, self.where["core"]
        deep, wide = len(self.scatter), len(self.exchange)
        if phase >= self.phases:
            return False
        self.phase += 1
        self.land()
        if phase == 0:
            self.start_core()
            return True
        if phase == 1:
            total = self.keep[...] + self.landed[...]
            self.start_scatter(0, total)
            return True
        if phase <= deep + wide:
            if phase <= deep:
                total = self.finish_scatter(phase - 2)
                self.start_scatter(phase - 1, total)
                return True
            index = phase - deep - 1
            total = self.finish_scatter(deep - 1) if index == 0 else self.finish_exchange(index - 1)
            self.start_exchange(index, total)
            return True
        step = phase - deep - wide - 1
        if step == 0:
            total = self.finish_exchange(wide - 1)
            self.result[core, self.rows_at(deep), :] = total.astype(self.dtype)
        if step < deep:
            self.start_gather(deep - 1 - step)
            return True
        if step == deep:
            other = device_at({**self.where, "core": 1 - core})
            self.copy(self.result.at[core], self.result.at[core], other)
            return True
        for made in self.done:
            made.wait_send()
        return False


class Spread:
    ROWS = 16
    phases = 4

    def scratch(self):
        return [
            pltpu.VMEM((15, self.ROWS, LANES), jnp.float32),
            pltpu.VMEM((16, self.ROWS, LANES), jnp.float32),
            pltpu.SemaphoreType.DMA((45,)),
            pltpu.SemaphoreType.DMA((45,)),
        ]

    def bind(self, where, source, result, refs):
        self.where, self.source, self.result = where, source, result
        self.landed, self.slots, self.send_sems, self.recv_sems = refs
        self.used, self.phase = 0, 0
        self.flying, self.done = [], []
        return self

    copy = Sum.copy
    land = Sum.land

    def advance(self):
        phase, where, rows = self.phase, self.where, self.ROWS
        if phase >= self.phases:
            return False
        self.phase += 1
        self.land()
        place, flat = where["z"] * 2 + where["core"], where["y"] * 4 + where["x"]
        mine = pl.ds(pl.multiple_of(place * rows, rows), rows)
        if phase == 0:
            for step in range(1, 16):
                other, device = stack_peer(where, step)
                block = self.source.at[pl.ds(pl.multiple_of(other * rows, rows), rows), :]
                self.copy(block, self.landed.at[step - 1], device)
        elif phase == 1:
            total = self.source[mine, :]
            for step in range(15):
                total = total + self.landed[step]
            self.slots[flat] = total
            for step in range(1, 16):
                _, device = plane_peer(where, step)
                self.copy(self.slots.at[flat], self.slots.at[flat], device)
        elif phase == 2:
            total = self.slots[0]
            for index in range(1, 16):
                total = total + self.slots[index]
            self.result[mine, :] = total
            block = self.result.at[mine, :]
            for step in range(1, 16):
                _, device = stack_peer(where, step)
                self.copy(block, block, device)
        else:
            for made in self.done:
                made.wait_send()
            return False
        return True


def lanes(group):
    return slice(group * LANES, (group + 1) * LANES)


def line(vector, group):
    return vector[lanes(group)].reshape(1, LANES)


def by_eight(value):
    return jnp.sum(value.reshape(-1, 8, LANES), axis=0)


def gelu_parts(pre_act):
    density = jnp.exp(-0.5 * pre_act * pre_act) * 0.3989422804014327
    t = pl.reciprocal(1.0 + 0.2316419 * jnp.abs(pre_act), approx=False)
    series = 1.781477937 + t * (-1.821255978 + t * 1.330274429)
    series = t * (0.319381530 + t * (-0.356563782 + t * series))
    tail = density * series
    mass = jnp.where(pre_act >= 0.0, 1.0 - tail, tail)
    return pre_act * mass, mass + pre_act * density


def spread_tissue(table, mask):
    tile = lax.axis_index("tile")
    mask[:, 96:WIDE, :] = jnp.zeros((4, WIDE - 96, LANES), jnp.float32)
    for place in range(4):
        row = jnp.clip(2 * tile - 1 + place, 0, 63)
        inside = 1.0
        if place == 0:
            inside = jnp.where(tile > 0, 1.0, 0.0)
        if place == 3:
            inside = jnp.where(tile < 31, 1.0, 0.0)
        for column in range(COLS):
            live = jnp.where(table[row, column] >= 0, 1.0, 0.0) * inside
            mask[place, column * TP : (column + 1) * TP, :] = jnp.full((TP, LANES), live, jnp.float32)


def fill(feat, cot, mask, padded, cot_masked):
    edge = jnp.zeros((3, ROWS + 2 * REACH, 8, LANES), jnp.float32)
    padded[:, :, 0:8, :] = edge
    padded[:, :, 104:112, :] = edge
    padded[:, :, 112:120, :] = edge
    cot_masked[:, :, 96:104, :] = jnp.zeros((3, ROWS, 8, LANES), jnp.float32)

    def row(i, carry):
        live = mask[1 + i // TP][:BREADTH]
        cells = feat[i].astype(jnp.float32)
        pull = cot[i].astype(jnp.float32)
        for group in range(GROUPS):
            padded[group, i + REACH, 8 : 8 + BREADTH, :] = cells[:, lanes(group)] * live
            cot_masked[group, i, 0:BREADTH, :] = pull[:, lanes(group)] * live
        return carry

    lax.fori_loop(0, ROWS, row, 0)


def fill_halo(halo, mask, padded):
    def row(i, carry):
        for side in range(2):
            live = mask[3 * side][:BREADTH]
            cells = halo[side, i].astype(jnp.float32)
            for group in range(GROUPS):
                padded[group, i + side * (ROWS + REACH), 8 : 8 + BREADTH, :] = (
                    cells[:, lanes(group)] * live
                )
        return carry

    lax.fori_loop(0, REACH, row, 0)


def spread_taps(weight, taps, bias, bias_rows):
    for group in range(GROUPS):
        bias_rows[group] = jnp.broadcast_to(line(bias, group), (8, LANES))
    for tap in range(K * K):
        for group in range(GROUPS):
            taps[group, tap] = jnp.broadcast_to(weight[tap // K, tap % K : tap % K + 1, lanes(group)], (8, LANES))


def conv(padded, taps, bias_rows, conv_out):
    def tile(step, carry):
        group, column = step // 13, step % 13
        total = jnp.zeros((ROWS, 8, LANES), jnp.float32) + bias_rows[group]
        for col_tap in range(K):
            window = padded[group, :, pl.ds(8 * column + 5 + col_tap, 8), :]
            for row_tap in range(K):
                total = total + window[row_tap : row_tap + ROWS] * taps[group, row_tap * K + col_tap]
        conv_out[group, :, pl.ds(pl.multiple_of(8 * column, 8), 8), :] = total
        return carry

    lax.fori_loop(0, GROUPS * 13, tile, 0)


def conv_grad(first, last, padded, grad_conv, tap_sums):
    def tile(step, carry):
        group, column = step // 13, step % 13
        pull = grad_conv[group, :, pl.ds(pl.multiple_of(8 * column, 8), 8), :]
        for col_tap in range(K):
            window = padded[group, :, pl.ds(8 * column + 5 + col_tap, 8), :]
            for row_tap in range(K):
                tap = row_tap * K + col_tap
                tap_sums[group, tap] += jnp.sum(window[row_tap : row_tap + ROWS] * pull, axis=0)
        return carry

    lax.fori_loop(first, last, tile, 0)


def norm(conv_out, inv_std, gain, offset, normed):
    def pair(step, carry):
        rows = pl.ds(2 * step, 2)
        held = [conv_out[group, rows].reshape(PAIR, LANES) for group in range(GROUPS)]
        mean = jnp.sum(held[0] + held[1] + held[2], axis=-1, keepdims=True) * (1.0 / C)
        held = [item - mean for item in held]
        squares = held[0] * held[0] + held[1] * held[1] + held[2] * held[2]
        var = jnp.sum(squares, axis=-1, keepdims=True) * (1.0 / C)
        inv = jnp.broadcast_to(lax.rsqrt(var + 1e-06), (PAIR, LANES))
        inv_std[rows] = inv.reshape(2, WIDE, LANES)
        place = pl.ds(pl.multiple_of(step * PAIR, 16), PAIR)
        for group in range(GROUPS):
            centred = held[group] * inv
            conv_out[group, rows] = centred.reshape(2, WIDE, LANES)
            normed[place, lanes(group)] = (
                centred * line(gain, group) + line(offset, group)
            ).astype(jnp.bfloat16)
        return carry

    lax.fori_loop(0, ROWS // 2, pair, 0)


def branch_grad(cot_masked, scale, grad_branch, sums):
    def pair(step, carry):
        place = pl.ds(pl.multiple_of(step * PAIR, 16), PAIR)
        for group in range(GROUPS):
            pull = cot_masked[group, pl.ds(2 * step, 2)].reshape(PAIR, LANES)
            pull = pull * (line(scale, group) * LOSS_SCALE)
            grad_branch[place, lanes(group)] = pull.astype(jnp.bfloat16)
            sums[group] += by_eight(pull)
        return carry

    lax.fori_loop(0, ROWS // 2, pair, 0)


def turn(rows, turned):
    def block(step, carry):
        place = pl.ds(pl.multiple_of(step * LANES, LANES), LANES)
        turned[:, place] = rows[place, :].T
        return carry

    lax.fori_loop(0, PADDED // LANES, block, 0)


def nt(left, right):
    return lax.dot_general(
        left, right, (((1,), (1,)), ((), ())), preferred_element_type=jnp.float32
    )


def mlp_rows(chunk, first, last, normed, grad_branch, w_in, b_in, w_out, b_out, work):
    hidden, grad_pre, branch, grad_xn, in_sums = work
    units = slice(chunk * CHUNK, (chunk + 1) * CHUNK)

    def block(step, carry):
        place = pl.ds(pl.multiple_of(step * PAIR, 16), PAIR)
        pre_act = jnp.dot(normed[place, :], w_in[:, units], preferred_element_type=jnp.float32)
        pre_act = pre_act + b_in[units].reshape(1, CHUNK)
        activ, slope = gelu_parts(pre_act)
        activ = activ.astype(jnp.bfloat16)
        hidden[place, :] = activ
        pull = nt(grad_branch[place, :], w_out[units, :]) * slope
        in_sums[:, units] += jnp.sum(pull.reshape(-1, 8, CHUNK), axis=0)
        pull = pull.astype(jnp.bfloat16)
        grad_pre[place, :] = pull
        out = jnp.dot(activ, w_out[units, :], preferred_element_type=jnp.float32)
        back = nt(pull, w_in[:, units])
        if chunk == 0:
            branch[place, :] = out + b_out[...].reshape(1, C)
            grad_xn[place, :] = back
        else:
            branch[place, :] += out
            grad_xn[place, :] += back
        return carry

    lax.fori_loop(first, last, block, 0)


def weight_grads(chunk, normed_t, grad_branch_t, hidden, grad_pre, large):
    first = jnp.dot(normed_t[...], grad_pre[...], preferred_element_type=jnp.float32)
    for group in range(CHUNK // LANES):
        large[chunk, 0, group * C : (group + 1) * C, :] = first[:, lanes(group)]
    second = jnp.dot(grad_branch_t[...], hidden[...], preferred_element_type=jnp.float32).T
    for group in range(GROUPS):
        large[chunk, 1, group * CHUNK : (group + 1) * CHUNK, :] = second[:, lanes(group)]


def after_mlp(first, last, branch, grad_xn, cot_masked, padded, centred, inv_std, mask, scale, gain, mixed, grad_conv, sums):
    def row(i, carry):
        place = pl.ds(pl.multiple_of(i * WIDE, 8), WIDE)
        live = mask[1 + i // TP]
        inv = inv_std[i]
        pulls, held = [], []
        for group in range(GROUPS):
            out = branch[place, lanes(group)].astype(jnp.bfloat16).astype(jnp.float32)
            sums[3 + group] += by_eight(cot_masked[group, i] * out)
            kept = padded[group, i + REACH, 8 : 8 + WIDE, :] + live * (line(scale, group) * out)
            mixed[i, :, lanes(group)] = kept[:BREADTH].astype(jnp.bfloat16)
            pull = grad_xn[place, lanes(group)].astype(jnp.bfloat16).astype(jnp.float32)
            cen = centred[group, i]
            sums[6 + group] += by_eight(pull * cen)
            sums[9 + group] += by_eight(pull)
            pulls.append(pull * line(gain, group))
            held.append(cen)
        mean = jnp.sum(pulls[0] + pulls[1] + pulls[2], axis=-1, keepdims=True) * (1.0 / C)
        along = pulls[0] * held[0] + pulls[1] * held[1] + pulls[2] * held[2]
        along = jnp.sum(along, axis=-1, keepdims=True) * (1.0 / C)
        for group in range(GROUPS):
            pull = inv * (pulls[group] - mean - held[group] * along)
            grad_conv[group, i] = pull
            sums[12 + group] += by_eight(pull)
        return carry

    lax.fori_loop(first, last, row, 0)


def collect(tap_sums, sums, in_sums, small):
    def put(place, value):
        small[place : place + 1, :] = jnp.sum(value, axis=0, keepdims=True)

    small[168:, :] = jnp.zeros((2 * LANES - 168, LANES), jnp.float32)
    for group in range(GROUPS):
        for tap in range(K * K):
            put(group * K * K + tap, tap_sums[group, tap])
    for index in range(15):
        value = sums[index]
        put(147 + index, value * LOSS_SCALE if 3 <= index < 6 else value)
    for group in range(HID // LANES):
        put(162 + group, in_sums[:, lanes(group)])


def plan():
    large = [
        Sum(1536, jnp.bfloat16, scatter, exchange)
        for scatter, exchange in ((("z", "y"), ("x",)), (("y", "z"), ("x",)), (("x", "z"), ("y",)))
    ]
    return large + [Spread()]


def work_scratch():
    def f32(*shape):
        return pltpu.VMEM(shape, jnp.float32)

    def b16(*shape):
        return pltpu.VMEM(shape, jnp.bfloat16)

    return [
        b16(2, REACH, BREADTH, C),
        pltpu.SemaphoreType.DMA((2,)),
        pltpu.SemaphoreType.DMA((2,)),
        f32(GROUPS, ROWS + 2 * REACH, 120, LANES),
        f32(GROUPS, ROWS, WIDE, LANES),
        f32(GROUPS, K * K, 8, LANES),
        f32(GROUPS, ROWS, WIDE, LANES),
        f32(ROWS, WIDE, LANES),
        b16(PADDED, C),
        b16(PADDED, C),
        b16(C, PADDED),
        b16(C, PADDED),
        b16(PADDED, CHUNK),
        b16(PADDED, CHUNK),
        f32(CELLS, C),
        f32(CELLS, C),
        f32(8, HID),
        f32(15, 8, LANES),
        f32(GROUPS, K * K, 8, LANES),
        f32(GROUPS, ROWS, WIDE, LANES),
        f32(CHUNKS, 2, 1536, LANES),
        f32(2 * LANES, LANES),
        b16(CHUNKS, 2, 1536, LANES),
        f32(2 * LANES, LANES),
        b16(ROWS, BREADTH, C),
        pltpu.SemaphoreType.DMA((5,)),
        f32(4, WIDE, LANES),
        f32(GROUPS, 8, LANES),
        b16(ROWS, BREADTH, C),
        b16(C, HID),
        b16(HID, C),
        pltpu.SemaphoreType.DMA((3,)),
    ]


def block_kernel(
    feat, cot_in, table, dw_weight, dw_bias, gain, offset, w_in_in, b_in, w_out_in, b_out, scale,
    mixed_out, large_out, small_out, *refs
):
    refs = list(refs)
    own = len(work_scratch())
    (
        halo, halo_send, halo_recv, padded, cot_masked, taps, centred, inv_std, normed, grad_branch,
        normed_t, grad_branch_t, hidden, grad_pre, branch, grad_xn, in_sums, sums, tap_sums,
        grad_conv, large, small, large_held, small_held, mixed, out_sems,
        mask, bias_rows, cot, w_in, w_out, in_sems,
    ) = refs[:own]
    refs = refs[own:]
    where = coordinates()
    core, tile = where["core"], lax.axis_index("tile")
    loads = [
        pltpu.make_async_copy(source, target, in_sems.at[index])
        for index, (source, target) in enumerate(((cot_in, cot), (w_in_in, w_in), (w_out_in, w_out)))
    ]
    for made in loads:
        made.start()
    enter(where)
    halves = []
    for side, step, first in ((0, 1, ROWS - REACH), (1, 31, 0)):
        made = pltpu.make_async_remote_copy(
            src_ref=feat.at[pl.ds(first, REACH)],
            dst_ref=halo.at[side],
            send_sem=halo_send.at[side],
            recv_sem=halo_recv.at[side],
            device_id=(where["z"], (tile + step) % 32),
            device_id_type=MESH,
        )
        made.start()
        halves.append(made)
    running = []
    for index, item in enumerate(plan()):
        count = len(item.scratch())
        mine, refs = refs[:count], refs[count:]
        if index < CHUNKS:
            keep, send = large.at[index, core], large.at[index, 1 - core]
            item.bind(where, keep, send, large_held.at[index], mine)
        else:
            item.bind(where, small, small_held, mine)
        running.append(item)

    copies = []

    def store(source, target):
        made = pltpu.make_async_copy(source, target, out_sems.at[len(copies)])
        made.start()
        copies.append(made)

    def advance(*which):
        for index in which:
            item = running[index]
            before = item.phase
            if not item.advance() and item.phase > before:
                if index < CHUNKS:
                    store(large_held.at[index], large_out.at[index])
                else:
                    store(small_held, small_out)

    spread_tissue(table, mask)
    spread_taps(dw_weight, taps, dw_bias, bias_rows)
    sums[...] = jnp.zeros(sums.shape, jnp.float32)
    tap_sums[...] = jnp.zeros(tap_sums.shape, jnp.float32)
    in_sums[...] = jnp.zeros(in_sums.shape, jnp.float32)
    for rows in (normed, grad_branch, hidden, grad_pre):
        rows[CELLS:, :] = jnp.zeros((PADDED - CELLS, rows.shape[1]), jnp.bfloat16)
    loads[0].wait()
    fill(feat, cot, mask, padded, cot_masked)
    branch_grad(cot_masked, scale, grad_branch, sums)
    turn(grad_branch, grad_branch_t)
    for made in halves:
        made.wait_recv()
    fill_halo(halo, mask, padded)
    conv(padded, taps, bias_rows, centred)
    norm(centred, inv_std, gain, offset, normed)
    turn(normed, normed_t)
    loads[1].wait()
    loads[2].wait()

    work = (hidden, grad_pre, branch, grad_xn, in_sums)
    weights = (normed, grad_branch, w_in, b_in, w_out, b_out, work)
    between = (((7, ()),), ((2, (0,)), (7, ())), ((2, (1,)), (5, (0,)), (7, ())))
    ends = ((0,), (1,), (0, 1, 2))
    for chunk in range(CHUNKS):
        first = 0
        for last, which in between[chunk]:
            mlp_rows(chunk, first, last, *weights)
            advance(*which)
            first = last
        weight_grads(chunk, normed_t, grad_branch_t, hidden, grad_pre, large)
        advance(*ends[chunk])
    first = 0
    for last, which in ((7, (2, 0)), (14, (0, 1))):
        after_mlp(
            first, last, branch, grad_xn, cot_masked, padded, centred, inv_std, mask, scale, gain, mixed,
            grad_conv, sums,
        )
        advance(*which)
        first = last
    store(mixed, mixed_out)
    first = 0
    for last, which in ((7, (1,)), (12, (2,)), (16, (0,)), (20, (1,)), (26, (2,)), (30, (0, 2)), (35, (1, 2)), (39, ())):
        conv_grad(first, last, padded, grad_conv, tap_sums)
        advance(*which)
        first = last
    collect(tap_sums, sums, in_sums, small)
    advance(3)
    while any(item.phase < item.phases for item in running):
        advance(2, 3, 0, 1)
    for made in copies:
        made.wait()
    for made in halves:
        made.wait_send()


def run_block(*operands):
    scratch = work_scratch()
    spaces = [pltpu.VMEM] * len(operands)
    spaces[1] = spaces[7] = spaces[9] = pl.ANY
    spaces[2] = pltpu.SMEM
    for item in plan():
        scratch += item.scratch()
    return pl.pallas_call(
        block_kernel,
        out_shape=(
            jax.ShapeDtypeStruct((ROWS, BREADTH, C), jnp.bfloat16),
            jax.ShapeDtypeStruct((CHUNKS, 2, 1536, LANES), jnp.bfloat16),
            jax.ShapeDtypeStruct((2 * LANES, LANES), jnp.float32),
        ),
        in_specs=[pl.BlockSpec(memory_space=space) for space in spaces],
        out_specs=(pl.BlockSpec(memory_space=pl.ANY),) * 3,
        scratch_shapes=scratch,
        compiler_params=pltpu.CompilerParams(
            collective_id=0, has_side_effects=True, vmem_limit_bytes=60 * 1024 * 1024
        ),
    )(*operands)


def finish_kernel(
    mixed_in, large_in, small_in, mixed, dw, dwb, ln_gain, ln_bias, w1_out, b1, w2_out, b2, scale,
    large, small, w1, w2, in_sems, out_sems
):
    across = pltpu.make_async_copy(mixed_in, mixed, out_sems.at[2 * CHUNKS])
    little = pltpu.make_async_copy(small_in, small, in_sems.at[2 * CHUNKS])
    pieces = [(chunk, half) for chunk in range(CHUNKS) for half in range(2)]
    loads = [
        pltpu.make_async_copy(large_in.at[piece], large.at[piece], in_sems.at[index])
        for index, piece in enumerate(pieces)
    ]
    for made in [little] + loads + [across]:
        made.start()
    little.wait()

    def row(place):
        return small[place : place + 1, :]

    for group in range(GROUPS):
        for tap in range(K * K):
            dw[tap // K, tap % K : tap % K + 1, lanes(group)] = row(group * K * K + tap)
    for index, target in enumerate((b2, scale, ln_gain, ln_bias, dwb)):
        for group in range(GROUPS):
            target[lanes(group)] = row(147 + index * GROUPS + group).reshape(LANES)
    for group in range(HID // LANES):
        b1[lanes(group)] = row(162 + group).reshape(LANES)

    stores = []
    for index, (chunk, half) in enumerate(pieces):
        loads[index].wait()
        units = slice(chunk * CHUNK, (chunk + 1) * CHUNK)
        if half == 0:
            for group in range(CHUNK // LANES):
                first = chunk * CHUNK + group * LANES
                w1[:, first : first + LANES] = large[
                    chunk, 0, group * C : (group + 1) * C, :
                ].astype(jnp.float32)
            made = pltpu.make_async_copy(w1.at[:, units], w1_out.at[:, units], out_sems.at[index])
        else:
            for group in range(GROUPS):
                w2[units, lanes(group)] = large[
                    chunk, 1, group * CHUNK : (group + 1) * CHUNK, :
                ].astype(jnp.float32)
            made = pltpu.make_async_copy(w2.at[units, :], w2_out.at[units, :], out_sems.at[index])
        made.start()
        stores.append(made)
    for made in stores + [across]:
        made.wait()


def finish(mixed, large, small):
    def f32(*shape):
        return jax.ShapeDtypeStruct(shape, jnp.float32)

    vector = f32(C)
    spaces = [pltpu.VMEM] * 10
    spaces[0] = spaces[5] = spaces[7] = pl.ANY
    return pl.pallas_call(
        finish_kernel,
        out_shape=(
            jax.ShapeDtypeStruct(mixed.shape, mixed.dtype), f32(K, K, C), vector, vector, vector,
            f32(C, HID), f32(HID), f32(HID, C), vector, vector,
        ),
        in_specs=[pl.BlockSpec(memory_space=pl.ANY)] * 3,
        out_specs=tuple(pl.BlockSpec(memory_space=space) for space in spaces),
        scratch_shapes=[
            pltpu.VMEM(large.shape, large.dtype),
            pltpu.VMEM(small.shape, small.dtype),
            pltpu.VMEM((C, HID), jnp.float32),
            pltpu.VMEM((HID, C), jnp.float32),
            pltpu.SemaphoreType.DMA((2 * CHUNKS + 1,)),
            pltpu.SemaphoreType.DMA((2 * CHUNKS + 1,)),
        ],
        compiler_params=pltpu.CompilerParams(vmem_limit_bytes=60 * 1024 * 1024),
    )(mixed, large, small)


def local(
    features,
    cotangent,
    owner_slot,
    dw_weight,
    dw_bias,
    ln_gain,
    ln_bias,
    w_in,
    b_in,
    w_out,
    b_out,
    layer_scale,
):
    mixed, large, small = run_block(
        features[0],
        cotangent[0],
        owner_slot[0],
        dw_weight,
        dw_bias,
        ln_gain,
        ln_bias,
        w_in,
        b_in,
        w_out,
        b_out,
        layer_scale,
    )
    outs = finish(mixed, large, small)
    return (outs[0][None],) + tuple(outs[1:])


def solution(mesh):
    placed = (
        P("slide", "tile", None, None),
        P("slide", "tile", None, None),
        P("slide", None, None),
        P(),
        P(),
        P(),
        P(),
        P(),
        P(),
        P(),
        P(),
        P(),
    )
    return jax.shard_map(
        local,
        mesh=mesh,
        in_specs=placed,
        out_specs=(P("slide", "tile", None, None), P(), P(), P(), P(), P(), P(), P(), P(), P()),
        check_vma=False,
    )
```

```python
import math

import jax
import jax.numpy as jnp
from jax import lax
from jax.experimental import pallas as pl
from jax.experimental.pallas import tpu as pltpu
from jax.sharding import PartitionSpec as P

C = 384
HID = 1536
K = 7
TP = 7
COLS = 14
OWN = 16
ROWS = 14
BREADTH = 98
WIDE = 104
CELLS = ROWS * WIDE
PADDED = 1536
REACH = 3
CHUNK = 512
CHUNKS = HID // CHUNK
PAIR = 2 * WIDE
BLOCKS = CELLS // PAIR
NORM_ROWS = 112
STRIP = 16
GROUPS = C // 128
LOSS_SCALE = 1.0 / math.sqrt(8 * 32 * OWN * TP * TP)

CORES = 2
SIZES = {"x": 4, "y": 4, "z": 8}
LANES = 128
MESH = pl.DeviceIdType.MESH


def coordinates():
    tile = lax.axis_index("tile")
    return {
        "z": lax.axis_index("slide"),
        "y": tile // 8,
        "x": (tile // 2) % 4,
        "core": tile % 2,
    }


def device_at(where):
    return (where["z"], where["y"] * 8 + where["x"] * 2 + where["core"])


def peer_along(where, axis, distance):
    size = SIZES[axis]
    position = (where[axis] + distance) % size
    return position, device_at({**where, axis: position})


def stack_peer(where, distance):
    place = (where["z"] * 2 + where["core"] + distance) % 16
    return place, device_at({**where, "z": place // 2, "core": place % 2})


def plane_peer(where, distance):
    place = (where["y"] * 4 + where["x"] + distance) % 16
    return place, device_at({**where, "y": place // 4, "x": place % 4})


def enter(where):
    tile = lax.axis_index("tile")
    peers = [(where["z"], (tile + step) % 32) for step in (1, 31)]
    for step in range(1, 16):
        peers += [stack_peer(where, step)[1], plane_peer(where, step)[1]]
    barrier = pltpu.get_barrier_semaphore()
    for peer in peers:
        pl.semaphore_signal(barrier, inc=1, device_id=peer, device_id_type=MESH)
    pl.semaphore_wait(barrier, len(peers))


class Sum:
    def __init__(self, rows, dtype, scatter, exchange):
        self.rows, self.dtype = rows, dtype
        self.scatter, self.exchange = scatter, exchange
        self.heights = [rows]
        for axis in scatter:
            self.heights.append(self.heights[-1] // SIZES[axis])
        self.phases = 2 * len(scatter) + len(exchange) + 3
        self.copies = 2 + 2 * sum(SIZES[a] - 1 for a in scatter) + sum(SIZES[a] - 1 for a in exchange)

    def scratch(self):
        shapes = [pltpu.VMEM((self.rows, LANES), jnp.float32)]
        for axis, before, after in zip(self.scatter, self.heights, self.heights[1:]):
            shapes.append(pltpu.VMEM((before, LANES), jnp.float32))
            shapes.append(pltpu.VMEM((before, LANES), self.dtype))
            shapes.append(pltpu.VMEM((SIZES[axis] - 1, after, LANES), self.dtype))
        for axis in self.exchange:
            shapes.append(pltpu.VMEM((SIZES[axis], self.heights[-1], LANES), self.dtype))
        shapes.append(pltpu.SemaphoreType.DMA((self.copies,)))
        shapes.append(pltpu.SemaphoreType.DMA((self.copies,)))
        return shapes

    def bind(self, where, keep, send, result, refs):
        refs = list(refs)
        self.where, self.keep, self.send, self.result = where, keep, send, result
        self.landed = refs.pop(0)
        self.levels = [tuple(refs.pop(0) for _ in range(3)) for _ in self.scatter]
        self.slots = [refs.pop(0) for _ in self.exchange]
        self.send_sems, self.recv_sems = refs
        self.used = 0
        self.flying = []
        self.done = []
        self.phase = 0
        offset = 0
        self.offsets = [offset]
        for axis, height in zip(self.scatter, self.heights[1:]):
            offset = offset + where[axis] * height
            self.offsets.append(offset)
        return self

    def copy(self, source, target, device):
        made = pltpu.make_async_remote_copy(
            src_ref=source,
            dst_ref=target,
            send_sem=self.send_sems.at[self.used],
            recv_sem=self.recv_sems.at[self.used],
            device_id=device,
            device_id_type=MESH,
        )
        self.used += 1
        made.start()
        self.flying.append(made)

    def land(self):
        for made in self.flying:
            made.wait_recv()
        self.done += self.flying
        self.flying = []

    def rows_at(self, level):
        return pl.ds(pl.multiple_of(self.offsets[level], 16), self.heights[level])

    def start_core(self):
        other = device_at({**self.where, "core": 1 - self.where["core"]})
        self.copy(self.send, self.landed, other)

    def start_scatter(self, index, total):
        axis, height = self.scatter[index], self.heights[index + 1]
        held, outgoing, incoming = self.levels[index]
        held[...] = total
        outgoing[...] = total.astype(self.dtype)
        for step in range(1, SIZES[axis]):
            position, device = peer_along(self.where, axis, step)
            self.copy(
                outgoing.at[pl.ds(pl.multiple_of(position * height, 16), height), :],
                incoming.at[step - 1],
                device,
            )

    def finish_scatter(self, index):
        axis, height = self.scatter[index], self.heights[index + 1]
        held, _, incoming = self.levels[index]
        total = held[pl.ds(pl.multiple_of(self.where[axis] * height, 16), height), :]
        for step in range(SIZES[axis] - 1):
            total = total + incoming[step].astype(jnp.float32)
        return total

    def start_exchange(self, index, total):
        axis, slots = self.exchange[index], self.slots[index]
        me = self.where[axis]
        slots[me] = total.astype(self.dtype)
        for step in range(1, SIZES[axis]):
            _, device = peer_along(self.where, axis, step)
            self.copy(slots.at[me], slots.at[me], device)

    def finish_exchange(self, index):
        axis, slots = self.exchange[index], self.slots[index]
        total = slots[0].astype(jnp.float32)
        for place in range(1, SIZES[axis]):
            total = total + slots[place].astype(jnp.float32)
        return total

    def start_gather(self, index):
        axis, core = self.scatter[index], self.where["core"]
        block = self.result.at[core, self.rows_at(index + 1), :]
        for step in range(1, SIZES[axis]):
            _, device = peer_along(self.where, axis, step)
            self.copy(block, block, device)

    def advance(self):
        phase, core = self.phase, self.where["core"]
        deep, wide = len(self.scatter), len(self.exchange)
        if phase >= self.phases:
            return False
        self.phase += 1
        self.land()
        if phase == 0:
            self.start_core()
            return True
        if phase == 1:
            total = self.keep[...] + self.landed[...]
            self.start_scatter(0, total)
            return True
        if phase <= deep + wide:
            if phase <= deep:
                total = self.finish_scatter(phase - 2)
                self.start_scatter(phase - 1, total)
                return True
            index = phase - deep - 1
            total = self.finish_scatter(deep - 1) if index == 0 else self.finish_exchange(index - 1)
            self.start_exchange(index, total)
            return True
        step = phase - deep - wide - 1
        if step == 0:
            total = self.finish_exchange(wide - 1)
            self.result[core, self.rows_at(deep), :] = total.astype(self.dtype)
        if step < deep:
            self.start_gather(deep - 1 - step)
            return True
        if step == deep:
            other = device_at({**self.where, "core": 1 - core})
            self.copy(self.result.at[core], self.result.at[core], other)
            return True
        for made in self.done:
            made.wait_send()
        return False


class Spread:
    ROWS = 16
    phases = 4

    def scratch(self):
        return [
            pltpu.VMEM((15, self.ROWS, LANES), jnp.float32),
            pltpu.VMEM((16, self.ROWS, LANES), jnp.float32),
            pltpu.SemaphoreType.DMA((45,)),
            pltpu.SemaphoreType.DMA((45,)),
        ]

    def bind(self, where, source, result, refs):
        self.where, self.source, self.result = where, source, result
        self.landed, self.slots, self.send_sems, self.recv_sems = refs
        self.used, self.phase = 0, 0
        self.flying, self.done = [], []
        return self

    copy = Sum.copy
    land = Sum.land

    def advance(self):
        phase, where, rows = self.phase, self.where, self.ROWS
        if phase >= self.phases:
            return False
        self.phase += 1
        self.land()
        place, flat = where["z"] * 2 + where["core"], where["y"] * 4 + where["x"]
        mine = pl.ds(pl.multiple_of(place * rows, rows), rows)
        if phase == 0:
            for step in range(1, 16):
                other, device = stack_peer(where, step)
                block = self.source.at[pl.ds(pl.multiple_of(other * rows, rows), rows), :]
                self.copy(block, self.landed.at[step - 1], device)
        elif phase == 1:
            total = self.source[mine, :]
            for step in range(15):
                total = total + self.landed[step]
            self.slots[flat] = total
            for step in range(1, 16):
                _, device = plane_peer(where, step)
                self.copy(self.slots.at[flat], self.slots.at[flat], device)
        elif phase == 2:
            total = self.slots[0]
            for index in range(1, 16):
                total = total + self.slots[index]
            self.result[mine, :] = total
            block = self.result.at[mine, :]
            for step in range(1, 16):
                _, device = stack_peer(where, step)
                self.copy(block, block, device)
        else:
            for made in self.done:
                made.wait_send()
            return False
        return True


def lanes(group):
    return slice(group * LANES, (group + 1) * LANES)


def line(vector, group):
    return vector[lanes(group)].reshape(1, LANES)


def by_eight(value):
    return jnp.sum(value.reshape(-1, 8, LANES), axis=0)


def gelu_parts(pre_act):
    density = jnp.exp(-0.5 * pre_act * pre_act) * 0.3989422804014327
    t = pl.reciprocal(1.0 + 0.2316419 * jnp.abs(pre_act), approx=False)
    series = 1.781477937 + t * (-1.821255978 + t * 1.330274429)
    series = t * (0.319381530 + t * (-0.356563782 + t * series))
    tail = density * series
    mass = jnp.where(pre_act >= 0.0, 1.0 - tail, tail)
    return pre_act * mass, mass + pre_act * density


def spread_tissue(table, mask):
    tile = lax.axis_index("tile")
    mask[:, 96:WIDE, :] = jnp.zeros((4, WIDE - 96, LANES), jnp.float32)
    for place in range(4):
        row = jnp.clip(2 * tile - 1 + place, 0, 63)
        inside = 1.0
        if place == 0:
            inside = jnp.where(tile > 0, 1.0, 0.0)
        if place == 3:
            inside = jnp.where(tile < 31, 1.0, 0.0)
        for column in range(COLS):
            live = jnp.where(table[row, column] >= 0, 1.0, 0.0) * inside
            mask[place, column * TP : (column + 1) * TP, :] = jnp.full((TP, LANES), live, jnp.float32)


def fill(feat, cot, mask, padded, cot_masked):
    edge = jnp.zeros((3, ROWS + 2 * REACH, 8, LANES), jnp.float32)
    padded[:, :, 0:8, :] = edge
    padded[:, :, 104:112, :] = edge
    padded[:, :, 112:120, :] = edge

    def row(i, carry):
        live = mask[1 + i // TP][:BREADTH]
        cells = feat[i].astype(jnp.float32)
        pull = cot[i].astype(jnp.float32)
        for group in range(GROUPS):
            padded[group, i + REACH, 8 : 8 + BREADTH, :] = cells[:, lanes(group)] * live
            end = pl.ds(pl.multiple_of(i * WIDE + WIDE - 8, 8), 8)
            cot_masked[group, end, :] = jnp.zeros((8, LANES), jnp.float32)
            place = pl.ds(pl.multiple_of(i * WIDE, 8), BREADTH)
            cot_masked[group, place, :] = pull[:, lanes(group)] * live
        return carry

    lax.fori_loop(0, ROWS, row, 0)


def fill_halo(halo, mask, padded):
    def row(i, carry):
        for side in range(2):
            live = mask[3 * side][:BREADTH]
            cells = halo[side, i].astype(jnp.float32)
            for group in range(GROUPS):
                padded[group, i + side * (ROWS + REACH), 8 : 8 + BREADTH, :] = (
                    cells[:, lanes(group)] * live
                )
        return carry

    lax.fori_loop(0, REACH, row, 0)


def spread_taps(weight, taps, bias, bias_rows):
    for group in range(GROUPS):
        bias_rows[group] = jnp.broadcast_to(line(bias, group), (8, LANES))
    for tap in range(K * K):
        for group in range(GROUPS):
            taps[group, tap] = jnp.broadcast_to(weight[tap // K, tap % K : tap % K + 1, lanes(group)], (8, LANES))


def conv(padded, taps, bias_rows, conv_out):
    def tile(step, carry):
        group, column = step // 13, step % 13
        total = jnp.zeros((ROWS, 8, LANES), jnp.float32) + bias_rows[group]
        for col_tap in range(K):
            window = padded[group, :, pl.ds(8 * column + 5 + col_tap, 8), :]
            for row_tap in range(K):
                total = total + window[row_tap : row_tap + ROWS] * taps[group, row_tap * K + col_tap]
        for i in range(ROWS):
            conv_out[group, pl.ds(pl.multiple_of(i * WIDE + 8 * column, 8), 8), :] = total[i]
        return carry

    lax.fori_loop(0, GROUPS * 13, tile, 0)


def conv_grad(first, last, padded, grad_conv, tap_sums):
    def tile(step, carry):
        group, column = step // 13, step % 13
        pull = jnp.stack(
            [
                grad_conv[group, pl.ds(pl.multiple_of(i * WIDE + 8 * column, 8), 8), :]
                for i in range(ROWS)
            ]
        )
        for col_tap in range(K):
            window = padded[group, :, pl.ds(8 * column + 5 + col_tap, 8), :]
            for row_tap in range(K):
                tap = row_tap * K + col_tap
                tap_sums[group, tap] += jnp.sum(window[row_tap : row_tap + ROWS] * pull, axis=0)
        return carry

    lax.fori_loop(first, last, tile, 0)


def norm(conv_out, inv_std, gain, offset, normed):
    def block(step, carry):
        place = pl.ds(pl.multiple_of(step * NORM_ROWS, 16), NORM_ROWS)
        held = [conv_out[group, place, :] for group in range(GROUPS)]
        mean = jnp.sum(held[0] + held[1] + held[2], axis=-1, keepdims=True) * (1.0 / C)
        held = [item - mean for item in held]
        squares = held[0] * held[0] + held[1] * held[1] + held[2] * held[2]
        var = jnp.sum(squares, axis=-1, keepdims=True) * (1.0 / C)
        inv = jnp.broadcast_to(lax.rsqrt(var + 1e-06), (NORM_ROWS, LANES))
        inv_std[place, :] = inv
        for group in range(GROUPS):
            centred = held[group] * inv
            conv_out[group, place, :] = centred
            normed[place, lanes(group)] = (
                centred * line(gain, group) + line(offset, group)
            ).astype(jnp.bfloat16)
        return carry

    lax.fori_loop(0, CELLS // NORM_ROWS, block, 0)


def branch_grad(cot_masked, scale, grad_branch, sums):
    def block(step, carry):
        place = pl.ds(pl.multiple_of(step * NORM_ROWS, 16), NORM_ROWS)
        for group in range(GROUPS):
            pull = cot_masked[group, place, :] * (line(scale, group) * LOSS_SCALE)
            grad_branch[place, lanes(group)] = pull.astype(jnp.bfloat16)
            sums[group] += by_eight(pull)
        return carry

    lax.fori_loop(0, CELLS // NORM_ROWS, block, 0)


def turn(rows, turned):
    def block(step, carry):
        place = pl.ds(pl.multiple_of(step * LANES, LANES), LANES)
        turned[:, place] = rows[place, :].T
        return carry

    lax.fori_loop(0, PADDED // LANES, block, 0)


def nt(left, right):
    return lax.dot_general(
        left, right, (((1,), (1,)), ((), ())), preferred_element_type=jnp.float32
    )


def rows_of(block):
    return slice(block * PAIR, (block + 1) * PAIR)


def mlp_enter(chunk, block, normed, grad_branch, w_in, w_out, pre_act, pull):
    units = slice(chunk * CHUNK, (chunk + 1) * CHUNK)
    place = rows_of(block)
    pre_act[...] = jnp.dot(normed[place, :], w_in[:, units], preferred_element_type=jnp.float32)
    pull[...] = nt(grad_branch[place, :], w_out[units, :])


def mlp_strips(chunk, block, b_in, pre_act, pull, hidden, grad_pre, in_sums):
    units = slice(chunk * CHUNK, (chunk + 1) * CHUNK)
    bias = b_in[units].reshape(1, CHUNK)
    total = in_sums[:, units]
    for first in range(0, PAIR, STRIP):
        strip = slice(first, first + STRIP)
        place = slice(block * PAIR + first, block * PAIR + first + STRIP)
        activ, slope = gelu_parts(pre_act[strip, :] + bias)
        hidden[place, :] = activ.astype(jnp.bfloat16)
        back = pull[strip, :] * slope
        total = total + back[:8] + back[8:]
        grad_pre[place, :] = back.astype(jnp.bfloat16)
    in_sums[:, units] = total


def mlp_leave(chunk, block, hidden, grad_pre, w_in, w_out, b_out, branch, grad_xn):
    units = slice(chunk * CHUNK, (chunk + 1) * CHUNK)
    place = rows_of(block)
    out = jnp.dot(hidden[place, :], w_out[units, :], preferred_element_type=jnp.float32)
    back = nt(grad_pre[place, :], w_in[:, units])
    if chunk == 0:
        branch[place, :] = out + b_out[...].reshape(1, C)
        grad_xn[place, :] = back
    else:
        branch[place, :] += out
        grad_xn[place, :] += back


def weight_grads(chunk, normed_t, grad_branch_t, hidden, grad_pre, large):
    first = jnp.dot(normed_t[...], grad_pre[...], preferred_element_type=jnp.float32)
    for group in range(CHUNK // LANES):
        large[chunk, 0, group * C : (group + 1) * C, :] = first[:, lanes(group)]
    second = jnp.dot(grad_branch_t[...], hidden[...], preferred_element_type=jnp.float32).T
    for group in range(GROUPS):
        large[chunk, 1, group * CHUNK : (group + 1) * CHUNK, :] = second[:, lanes(group)]


def after_mlp(first, last, branch, grad_xn, cot_masked, padded, centred, inv_std, mask, scale, gain, mixed, grad_conv, sums):
    def part(i, start, size):
        place = pl.ds(pl.multiple_of(i * WIDE + start, 8), size)
        live = mask[1 + i // TP, start : start + size]
        used = min(BREADTH - start, size)
        pulls, held = [], []
        for group in range(GROUPS):
            out = branch[place, lanes(group)].astype(jnp.bfloat16).astype(jnp.float32)
            sums[3 + group] += by_eight(cot_masked[group, place, :] * out)
            kept = padded[group, i + REACH, 8 + start : 8 + start + size, :]
            kept = kept + live * (line(scale, group) * out)
            mixed[i, start : start + used, lanes(group)] = kept[:used].astype(jnp.bfloat16)
        for group in range(GROUPS):
            pull = grad_xn[place, lanes(group)].astype(jnp.bfloat16).astype(jnp.float32)
            cen = centred[group, place, :]
            sums[6 + group] += by_eight(pull * cen)
            sums[9 + group] += by_eight(pull)
            pulls.append(pull * line(gain, group))
            held.append(cen)
        mean = jnp.sum(pulls[0] + pulls[1] + pulls[2], axis=-1, keepdims=True) * (1.0 / C)
        along = pulls[0] * held[0] + pulls[1] * held[1] + pulls[2] * held[2]
        along = jnp.sum(along, axis=-1, keepdims=True) * (1.0 / C)
        inv = inv_std[place, :]
        for group in range(GROUPS):
            pull = inv * (pulls[group] - mean - held[group] * along)
            grad_conv[group, place, :] = pull
            sums[12 + group] += by_eight(pull)

    def row(i, carry):
        part(i, 0, 48)
        part(i, 48, 56)
        return carry

    lax.fori_loop(first, last, row, 0)


def collect(tap_sums, sums, in_sums, small):
    def put(place, value):
        small[place : place + 1, :] = jnp.sum(value, axis=0, keepdims=True)

    small[168:, :] = jnp.zeros((2 * LANES - 168, LANES), jnp.float32)
    for group in range(GROUPS):
        for tap in range(K * K):
            put(group * K * K + tap, tap_sums[group, tap])
    for index in range(15):
        value = sums[index]
        put(147 + index, value * LOSS_SCALE if 3 <= index < 6 else value)
    for group in range(HID // LANES):
        put(162 + group, in_sums[:, lanes(group)])


def plan():
    large = [
        Sum(1536, jnp.bfloat16, scatter, exchange)
        for scatter, exchange in ((("z", "y"), ("x",)), (("y", "z"), ("x",)), (("x", "z"), ("y",)))
    ]
    return large + [Spread()]


def work_scratch():
    def f32(*shape):
        return pltpu.VMEM(shape, jnp.float32)

    def b16(*shape):
        return pltpu.VMEM(shape, jnp.bfloat16)

    return [
        b16(2, REACH, BREADTH, C),
        pltpu.SemaphoreType.DMA((2,)),
        pltpu.SemaphoreType.DMA((2,)),
        f32(GROUPS, ROWS + 2 * REACH, 120, LANES),
        f32(GROUPS, CELLS, LANES),
        f32(GROUPS, K * K, 8, LANES),
        f32(GROUPS, CELLS, LANES),
        f32(CELLS, LANES),
        b16(PADDED, C),
        b16(PADDED, C),
        b16(C, PADDED),
        b16(C, PADDED),
        b16(2, PADDED, CHUNK),
        b16(2, PADDED, CHUNK),
        f32(CELLS, C),
        f32(CELLS, C),
        f32(8, HID),
        f32(15, 8, LANES),
        f32(GROUPS, K * K, 8, LANES),
        f32(GROUPS, CELLS, LANES),
        f32(CHUNKS, 2, 1536, LANES),
        f32(2 * LANES, LANES),
        b16(CHUNKS, 2, 1536, LANES),
        f32(2 * LANES, LANES),
        b16(ROWS, BREADTH, C),
        pltpu.SemaphoreType.DMA((5,)),
        f32(4, WIDE, LANES),
        f32(GROUPS, 8, LANES),
        b16(ROWS, BREADTH, C),
        b16(C, HID),
        b16(HID, C),
        pltpu.SemaphoreType.DMA((3,)),
        f32(2, PAIR, CHUNK),
        f32(2, PAIR, CHUNK),
    ]


def block_kernel(
    feat, cot_in, table, dw_weight, dw_bias, gain, offset, w_in_in, b_in, w_out_in, b_out, scale,
    mixed_out, large_out, small_out, *refs
):
    refs = list(refs)
    own = len(work_scratch())
    (
        halo, halo_send, halo_recv, padded, cot_masked, taps, centred, inv_std, normed, grad_branch,
        normed_t, grad_branch_t, hidden, grad_pre, branch, grad_xn, in_sums, sums, tap_sums,
        grad_conv, large, small, large_held, small_held, mixed, out_sems,
        mask, bias_rows, cot, w_in, w_out, in_sems, pre_act, pull,
    ) = refs[:own]
    refs = refs[own:]
    where = coordinates()
    core, tile = where["core"], lax.axis_index("tile")
    loads = [
        pltpu.make_async_copy(source, target, in_sems.at[index])
        for index, (source, target) in enumerate(((cot_in, cot), (w_in_in, w_in), (w_out_in, w_out)))
    ]
    for made in loads:
        made.start()
    enter(where)
    halves = []
    for side, step, first in ((0, 1, ROWS - REACH), (1, 31, 0)):
        made = pltpu.make_async_remote_copy(
            src_ref=feat.at[pl.ds(first, REACH)],
            dst_ref=halo.at[side],
            send_sem=halo_send.at[side],
            recv_sem=halo_recv.at[side],
            device_id=(where["z"], (tile + step) % 32),
            device_id_type=MESH,
        )
        made.start()
        halves.append(made)
    running = []
    for index, item in enumerate(plan()):
        count = len(item.scratch())
        mine, refs = refs[:count], refs[count:]
        if index < CHUNKS:
            keep, send = large.at[index, core], large.at[index, 1 - core]
            item.bind(where, keep, send, large_held.at[index], mine)
        else:
            item.bind(where, small, small_held, mine)
        running.append(item)

    copies = []

    def store(source, target):
        made = pltpu.make_async_copy(source, target, out_sems.at[len(copies)])
        made.start()
        copies.append(made)

    def advance(*which):
        for index in which:
            item = running[index]
            before = item.phase
            if not item.advance() and item.phase > before:
                if index < CHUNKS:
                    store(large_held.at[index], large_out.at[index])
                else:
                    store(small_held, small_out)

    spread_tissue(table, mask)
    spread_taps(dw_weight, taps, dw_bias, bias_rows)
    sums[...] = jnp.zeros(sums.shape, jnp.float32)
    tap_sums[...] = jnp.zeros(tap_sums.shape, jnp.float32)
    in_sums[...] = jnp.zeros(in_sums.shape, jnp.float32)
    for rows in (normed, grad_branch, hidden.at[0], hidden.at[1], grad_pre.at[0], grad_pre.at[1]):
        rows[CELLS:, :] = jnp.zeros((PADDED - CELLS, rows.shape[1]), jnp.bfloat16)
    loads[0].wait()
    fill(feat, cot, mask, padded, cot_masked)
    branch_grad(cot_masked, scale, grad_branch, sums)
    turn(grad_branch, grad_branch_t)
    for made in halves:
        made.wait_recv()
    fill_halo(halo, mask, padded)
    conv(padded, taps, bias_rows, centred)
    norm(centred, inv_std, gain, offset, normed)
    turn(normed, normed_t)
    loads[1].wait()
    loads[2].wait()

    steps = [(chunk, block) for chunk in range(CHUNKS) for block in range(BLOCKS)]

    def enter_step(place):
        if place < len(steps):
            chunk, block = steps[place]
            side = place % 2
            mlp_enter(
                chunk, block, normed, grad_branch, w_in, w_out, pre_act.at[side], pull.at[side]
            )

    def leave_step(place):
        chunk, block = steps[place]
        half = chunk % 2
        mlp_leave(
            chunk, block, hidden.at[half], grad_pre.at[half], w_in, w_out, b_out, branch, grad_xn
        )

    def finish_chunk(chunk):
        half = chunk % 2
        weight_grads(chunk, normed_t, grad_branch_t, hidden.at[half], grad_pre.at[half], large)

    after_block = {
        (1, 1): (0,), (1, 4): (0,), (2, 1): (0, 1), (2, 4): (1,), (2, 6): (0,)
    }
    enter_step(0)
    for place, (chunk, block) in enumerate(steps):
        half, side = chunk % 2, place % 2
        enter_step(place + 1)
        mlp_strips(
            chunk, block, b_in, pre_act.at[side], pull.at[side], hidden.at[half], grad_pre.at[half],
            in_sums,
        )
        if place > 0:
            leave_step(place - 1)
        if block == 0 and chunk > 0:
            finish_chunk(chunk - 1)
        advance(*after_block.get((chunk, block), ()))
    leave_step(len(steps) - 1)
    finish_chunk(CHUNKS - 1)
    advance(2, 1)
    first = 0
    for last, which in ((7, (2, 0)), (14, (0, 1))):
        after_mlp(
            first, last, branch, grad_xn, cot_masked, padded, centred, inv_std, mask, scale, gain, mixed,
            grad_conv, sums,
        )
        advance(*which)
        first = last
    store(mixed, mixed_out)
    first = 0
    for last, which in ((7, (1,)), (12, (2,)), (16, (0,)), (20, (1,)), (26, (2,)), (30, (0, 2)), (35, (1, 2)), (39, ())):
        conv_grad(first, last, padded, grad_conv, tap_sums)
        advance(*which)
        first = last
    collect(tap_sums, sums, in_sums, small)
    advance(3)
    while any(item.phase < item.phases for item in running):
        advance(2, 3, 0, 1)
    for made in copies:
        made.wait()
    for made in halves:
        made.wait_send()


def run_block(*operands):
    scratch = work_scratch()
    spaces = [pltpu.VMEM] * len(operands)
    spaces[1] = spaces[7] = spaces[9] = pl.ANY
    spaces[2] = pltpu.SMEM
    for item in plan():
        scratch += item.scratch()
    return pl.pallas_call(
        block_kernel,
        out_shape=(
            jax.ShapeDtypeStruct((ROWS, BREADTH, C), jnp.bfloat16),
            jax.ShapeDtypeStruct((CHUNKS, 2, 1536, LANES), jnp.bfloat16),
            jax.ShapeDtypeStruct((2 * LANES, LANES), jnp.float32),
        ),
        in_specs=[pl.BlockSpec(memory_space=space) for space in spaces],
        out_specs=(pl.BlockSpec(memory_space=pl.ANY),) * 3,
        scratch_shapes=scratch,
        compiler_params=pltpu.CompilerParams(
            collective_id=0, has_side_effects=True, vmem_limit_bytes=60 * 1024 * 1024
        ),
    )(*operands)


def finish_kernel(
    mixed_in, large_in, small_in, mixed, dw, dwb, ln_gain, ln_bias, w1_out, b1, w2_out, b2, scale,
    large, small, w1, w2, held, in_sems, out_sems
):
    arrive = pltpu.make_async_copy(mixed_in, held, in_sems.at[2 * CHUNKS + 1])
    leave = pltpu.make_async_copy(held, mixed, out_sems.at[2 * CHUNKS])
    little = pltpu.make_async_copy(small_in, small, in_sems.at[2 * CHUNKS])
    pieces = [(chunk, half) for chunk in range(CHUNKS) for half in range(2)]
    loads = [
        pltpu.make_async_copy(large_in.at[piece], large.at[piece], in_sems.at[index])
        for index, piece in enumerate(pieces)
    ]
    for made in [little, arrive] + loads:
        made.start()
    little.wait()

    def row(place):
        return small[place : place + 1, :]

    for group in range(GROUPS):
        for tap in range(K * K):
            dw[tap // K, tap % K : tap % K + 1, lanes(group)] = row(group * K * K + tap)
    for index, target in enumerate((b2, scale, ln_gain, ln_bias, dwb)):
        for group in range(GROUPS):
            target[lanes(group)] = row(147 + index * GROUPS + group).reshape(LANES)
    for group in range(HID // LANES):
        b1[lanes(group)] = row(162 + group).reshape(LANES)

    arrive.wait()
    leave.start()
    stores = []
    for index, (chunk, half) in enumerate(pieces):
        loads[index].wait()
        units = slice(chunk * CHUNK, (chunk + 1) * CHUNK)
        if half == 0:
            for group in range(CHUNK // LANES):
                first = chunk * CHUNK + group * LANES
                w1[:, first : first + LANES] = large[
                    chunk, 0, group * C : (group + 1) * C, :
                ].astype(jnp.float32)
            made = pltpu.make_async_copy(w1.at[:, units], w1_out.at[:, units], out_sems.at[index])
        else:
            for group in range(GROUPS):
                w2[units, lanes(group)] = large[
                    chunk, 1, group * CHUNK : (group + 1) * CHUNK, :
                ].astype(jnp.float32)
            made = pltpu.make_async_copy(w2.at[units, :], w2_out.at[units, :], out_sems.at[index])
        made.start()
        stores.append(made)
    for made in stores + [leave]:
        made.wait()


def finish(mixed, large, small):
    def f32(*shape):
        return jax.ShapeDtypeStruct(shape, jnp.float32)

    vector = f32(C)
    spaces = [pltpu.VMEM] * 10
    spaces[0] = spaces[5] = spaces[7] = pl.ANY
    return pl.pallas_call(
        finish_kernel,
        out_shape=(
            jax.ShapeDtypeStruct(mixed.shape, mixed.dtype), f32(K, K, C), vector, vector, vector,
            f32(C, HID), f32(HID), f32(HID, C), vector, vector,
        ),
        in_specs=[pl.BlockSpec(memory_space=pl.ANY)] * 3,
        out_specs=tuple(pl.BlockSpec(memory_space=space) for space in spaces),
        scratch_shapes=[
            pltpu.VMEM(large.shape, large.dtype),
            pltpu.VMEM(small.shape, small.dtype),
            pltpu.VMEM((C, HID), jnp.float32),
            pltpu.VMEM((HID, C), jnp.float32),
            pltpu.VMEM(mixed.shape, mixed.dtype),
            pltpu.SemaphoreType.DMA((2 * CHUNKS + 2,)),
            pltpu.SemaphoreType.DMA((2 * CHUNKS + 1,)),
        ],
        compiler_params=pltpu.CompilerParams(vmem_limit_bytes=60 * 1024 * 1024),
    )(mixed, large, small)


def local(
    features,
    cotangent,
    owner_slot,
    dw_weight,
    dw_bias,
    ln_gain,
    ln_bias,
    w_in,
    b_in,
    w_out,
    b_out,
    layer_scale,
):
    mixed, large, small = run_block(
        features[0],
        cotangent[0],
        owner_slot[0],
        dw_weight,
        dw_bias,
        ln_gain,
        ln_bias,
        w_in,
        b_in,
        w_out,
        b_out,
        layer_scale,
    )
    outs = finish(mixed, large, small)
    return (outs[0][None],) + tuple(outs[1:])


def solution(mesh):
    placed = (
        P("slide", "tile", None, None),
        P("slide", "tile", None, None),
        P("slide", None, None),
        P(),
        P(),
        P(),
        P(),
        P(),
        P(),
        P(),
        P(),
        P(),
    )
    return jax.shard_map(
        local,
        mesh=mesh,
        in_specs=placed,
        out_specs=(P("slide", "tile", None, None), P(), P(), P(), P(), P(), P(), P(), P(), P()),
        check_vma=False,
    )
```

```python
import math

import jax
import jax.numpy as jnp
from jax import lax
from jax.experimental import pallas as pl
from jax.experimental.pallas import tpu as pltpu
from jax.sharding import PartitionSpec as P

C = 384
HID = 1536
K = 7
TP = 7
COLS = 14
OWN = 16
ROWS = 14
BREADTH = 98
WIDE = 104
CELLS = ROWS * WIDE
PADDED = 1536
REACH = 3
CHUNK = 512
CHUNKS = HID // CHUNK
PAIR = 2 * WIDE
BLOCKS = CELLS // PAIR
NORM_ROWS = 112
STRIP = 16
GROUPS = C // 128
LOSS_SCALE = 1.0 / math.sqrt(8 * 32 * OWN * TP * TP)

CORES = 2
SIZES = {"x": 4, "y": 4, "z": 8}
LANES = 128
MESH = pl.DeviceIdType.MESH


def coordinates():
    tile = lax.axis_index("tile")
    return {
        "z": lax.axis_index("slide"),
        "y": tile // 8,
        "x": (tile // 2) % 4,
        "core": tile % 2,
    }


def device_at(where):
    return (where["z"], where["y"] * 8 + where["x"] * 2 + where["core"])


def peer_along(where, axis, distance):
    size = SIZES[axis]
    position = (where[axis] + distance) % size
    return position, device_at({**where, axis: position})


def stack_peer(where, distance):
    place = (where["z"] * 2 + where["core"] + distance) % 16
    return place, device_at({**where, "z": place // 2, "core": place % 2})


def plane_peer(where, distance):
    place = (where["y"] * 4 + where["x"] + distance) % 16
    return place, device_at({**where, "y": place // 4, "x": place % 4})


def enter(where):
    tile = lax.axis_index("tile")
    peers = [(where["z"], (tile + step) % 32) for step in (1, 31)]
    for step in range(1, 16):
        peers += [stack_peer(where, step)[1], plane_peer(where, step)[1]]
    barrier = pltpu.get_barrier_semaphore()
    for peer in peers:
        pl.semaphore_signal(barrier, inc=1, device_id=peer, device_id_type=MESH)
    pl.semaphore_wait(barrier, len(peers))


class Sum:
    def __init__(self, rows, dtype, scatter, exchange):
        self.rows, self.dtype = rows, dtype
        self.scatter, self.exchange = scatter, exchange
        self.heights = [rows]
        for axis in scatter:
            self.heights.append(self.heights[-1] // SIZES[axis])
        self.phases = 2 * len(scatter) + len(exchange) + 3
        self.copies = 2 + 2 * sum(SIZES[a] - 1 for a in scatter) + sum(SIZES[a] - 1 for a in exchange)

    def scratch(self):
        shapes = [pltpu.VMEM((self.rows, LANES), jnp.float32)]
        for axis, before, after in zip(self.scatter, self.heights, self.heights[1:]):
            shapes.append(pltpu.VMEM((before, LANES), jnp.float32))
            shapes.append(pltpu.VMEM((before, LANES), self.dtype))
            shapes.append(pltpu.VMEM((SIZES[axis] - 1, after, LANES), self.dtype))
        for axis in self.exchange:
            shapes.append(pltpu.VMEM((SIZES[axis], self.heights[-1], LANES), self.dtype))
        shapes.append(pltpu.SemaphoreType.DMA((self.copies,)))
        shapes.append(pltpu.SemaphoreType.DMA((self.copies,)))
        return shapes

    def bind(self, where, keep, send, result, refs):
        refs = list(refs)
        self.where, self.keep, self.send, self.result = where, keep, send, result
        self.landed = refs.pop(0)
        self.levels = [tuple(refs.pop(0) for _ in range(3)) for _ in self.scatter]
        self.slots = [refs.pop(0) for _ in self.exchange]
        self.send_sems, self.recv_sems = refs
        self.used = 0
        self.flying = []
        self.done = []
        self.phase = 0
        offset = 0
        self.offsets = [offset]
        for axis, height in zip(self.scatter, self.heights[1:]):
            offset = offset + where[axis] * height
            self.offsets.append(offset)
        return self

    def copy(self, source, target, device):
        made = pltpu.make_async_remote_copy(
            src_ref=source,
            dst_ref=target,
            send_sem=self.send_sems.at[self.used],
            recv_sem=self.recv_sems.at[self.used],
            device_id=device,
            device_id_type=MESH,
        )
        self.used += 1
        made.start()
        self.flying.append(made)

    def land(self):
        for made in self.flying:
            made.wait_recv()
        self.done += self.flying
        self.flying = []

    def rows_at(self, level):
        return pl.ds(pl.multiple_of(self.offsets[level], 16), self.heights[level])

    def start_core(self):
        other = device_at({**self.where, "core": 1 - self.where["core"]})
        self.copy(self.send, self.landed, other)

    def start_scatter(self, index, total):
        axis, height = self.scatter[index], self.heights[index + 1]
        held, outgoing, incoming = self.levels[index]
        held[...] = total
        outgoing[...] = total.astype(self.dtype)
        for step in range(1, SIZES[axis]):
            position, device = peer_along(self.where, axis, step)
            self.copy(
                outgoing.at[pl.ds(pl.multiple_of(position * height, 16), height), :],
                incoming.at[step - 1],
                device,
            )

    def finish_scatter(self, index):
        axis, height = self.scatter[index], self.heights[index + 1]
        held, _, incoming = self.levels[index]
        total = held[pl.ds(pl.multiple_of(self.where[axis] * height, 16), height), :]
        for step in range(SIZES[axis] - 1):
            total = total + incoming[step].astype(jnp.float32)
        return total

    def start_exchange(self, index, total):
        axis, slots = self.exchange[index], self.slots[index]
        me = self.where[axis]
        slots[me] = total.astype(self.dtype)
        for step in range(1, SIZES[axis]):
            _, device = peer_along(self.where, axis, step)
            self.copy(slots.at[me], slots.at[me], device)

    def finish_exchange(self, index):
        axis, slots = self.exchange[index], self.slots[index]
        total = slots[0].astype(jnp.float32)
        for place in range(1, SIZES[axis]):
            total = total + slots[place].astype(jnp.float32)
        return total

    def start_gather(self, index):
        axis, core = self.scatter[index], self.where["core"]
        block = self.result.at[core, self.rows_at(index + 1), :]
        for step in range(1, SIZES[axis]):
            _, device = peer_along(self.where, axis, step)
            self.copy(block, block, device)

    def advance(self):
        phase, core = self.phase, self.where["core"]
        deep, wide = len(self.scatter), len(self.exchange)
        if phase >= self.phases:
            return False
        self.phase += 1
        self.land()
        if phase == 0:
            self.start_core()
            return True
        if phase == 1:
            total = self.keep[...] + self.landed[...]
            self.start_scatter(0, total)
            return True
        if phase <= deep + wide:
            if phase <= deep:
                total = self.finish_scatter(phase - 2)
                self.start_scatter(phase - 1, total)
                return True
            index = phase - deep - 1
            total = self.finish_scatter(deep - 1) if index == 0 else self.finish_exchange(index - 1)
            self.start_exchange(index, total)
            return True
        step = phase - deep - wide - 1
        if step == 0:
            total = self.finish_exchange(wide - 1)
            self.result[core, self.rows_at(deep), :] = total.astype(self.dtype)
        if step < deep:
            self.start_gather(deep - 1 - step)
            return True
        if step == deep:
            other = device_at({**self.where, "core": 1 - core})
            self.copy(self.result.at[core], self.result.at[core], other)
            return True
        for made in self.done:
            made.wait_send()
        return False


class Spread:
    ROWS = 16
    phases = 4

    def scratch(self):
        return [
            pltpu.VMEM((15, self.ROWS, LANES), jnp.float32),
            pltpu.VMEM((16, self.ROWS, LANES), jnp.float32),
            pltpu.SemaphoreType.DMA((45,)),
            pltpu.SemaphoreType.DMA((45,)),
        ]

    def bind(self, where, source, result, refs):
        self.where, self.source, self.result = where, source, result
        self.landed, self.slots, self.send_sems, self.recv_sems = refs
        self.used, self.phase = 0, 0
        self.flying, self.done = [], []
        return self

    copy = Sum.copy
    land = Sum.land

    def advance(self):
        phase, where, rows = self.phase, self.where, self.ROWS
        if phase >= self.phases:
            return False
        self.phase += 1
        self.land()
        place, flat = where["z"] * 2 + where["core"], where["y"] * 4 + where["x"]
        mine = pl.ds(pl.multiple_of(place * rows, rows), rows)
        if phase == 0:
            for step in range(1, 16):
                other, device = stack_peer(where, step)
                block = self.source.at[pl.ds(pl.multiple_of(other * rows, rows), rows), :]
                self.copy(block, self.landed.at[step - 1], device)
        elif phase == 1:
            total = self.source[mine, :]
            for step in range(15):
                total = total + self.landed[step]
            self.slots[flat] = total
            for step in range(1, 16):
                _, device = plane_peer(where, step)
                self.copy(self.slots.at[flat], self.slots.at[flat], device)
        elif phase == 2:
            total = self.slots[0]
            for index in range(1, 16):
                total = total + self.slots[index]
            self.result[mine, :] = total
            block = self.result.at[mine, :]
            for step in range(1, 16):
                _, device = stack_peer(where, step)
                self.copy(block, block, device)
        else:
            for made in self.done:
                made.wait_send()
            return False
        return True


def lanes(group):
    return slice(group * LANES, (group + 1) * LANES)


def line(vector, group):
    return vector[lanes(group)].reshape(1, LANES)


def by_eight(value):
    return jnp.sum(value.reshape(-1, 8, LANES), axis=0)


def gelu_parts(pre_act):
    density = jnp.exp(-0.5 * pre_act * pre_act) * 0.3989422804014327
    t = pl.reciprocal(1.0 + 0.2316419 * jnp.abs(pre_act), approx=False)
    series = 1.781477937 + t * (-1.821255978 + t * 1.330274429)
    series = t * (0.319381530 + t * (-0.356563782 + t * series))
    tail = density * series
    mass = jnp.where(pre_act >= 0.0, 1.0 - tail, tail)
    return pre_act * mass, mass + pre_act * density


def spread_tissue(table, mask):
    tile = lax.axis_index("tile")
    mask[:, 96:WIDE, :] = jnp.zeros((4, WIDE - 96, LANES), jnp.float32)
    for place in range(4):
        row = jnp.clip(2 * tile - 1 + place, 0, 63)
        inside = 1.0
        if place == 0:
            inside = jnp.where(tile > 0, 1.0, 0.0)
        if place == 3:
            inside = jnp.where(tile < 31, 1.0, 0.0)
        for column in range(COLS):
            live = jnp.where(table[row, column] >= 0, 1.0, 0.0) * inside
            mask[place, column * TP : (column + 1) * TP, :] = jnp.full((TP, LANES), live, jnp.float32)


def fill(feat, cot, mask, padded, cot_masked):
    edge = jnp.zeros((3, ROWS + 2 * REACH, 8, LANES), jnp.float32)
    padded[:, :, 0:8, :] = edge
    padded[:, :, 104:112, :] = edge
    padded[:, :, 112:120, :] = edge

    def row(i, carry):
        live = mask[1 + i // TP][:BREADTH]
        cells = feat[i].astype(jnp.float32)
        pull = cot[i].astype(jnp.float32)
        for group in range(GROUPS):
            padded[group, i + REACH, 8 : 8 + BREADTH, :] = cells[:, lanes(group)] * live
            end = pl.ds(pl.multiple_of(i * WIDE + WIDE - 8, 8), 8)
            cot_masked[group, end, :] = jnp.zeros((8, LANES), jnp.float32)
            place = pl.ds(pl.multiple_of(i * WIDE, 8), BREADTH)
            cot_masked[group, place, :] = pull[:, lanes(group)] * live
        return carry

    lax.fori_loop(0, ROWS, row, 0)


def fill_halo(halo, mask, padded):
    def row(i, carry):
        for side in range(2):
            live = mask[3 * side][:BREADTH]
            cells = halo[side, i].astype(jnp.float32)
            for group in range(GROUPS):
                padded[group, i + side * (ROWS + REACH), 8 : 8 + BREADTH, :] = (
                    cells[:, lanes(group)] * live
                )
        return carry

    lax.fori_loop(0, REACH, row, 0)


def spread_taps(weight, taps, bias, bias_rows):
    for group in range(GROUPS):
        bias_rows[group] = jnp.broadcast_to(line(bias, group), (8, LANES))
    for tap in range(K * K):
        for group in range(GROUPS):
            taps[group, tap] = jnp.broadcast_to(weight[tap // K, tap % K : tap % K + 1, lanes(group)], (8, LANES))


def conv(padded, taps, bias_rows, conv_out):
    def tile(step, carry):
        group, column = step // 13, step % 13
        total = jnp.zeros((ROWS, 8, LANES), jnp.float32) + bias_rows[group]
        for col_tap in range(K):
            window = padded[group, :, pl.ds(8 * column + 5 + col_tap, 8), :]
            for row_tap in range(K):
                total = total + window[row_tap : row_tap + ROWS] * taps[group, row_tap * K + col_tap]
        for i in range(ROWS):
            conv_out[group, pl.ds(pl.multiple_of(i * WIDE + 8 * column, 8), 8), :] = total[i]
        return carry

    lax.fori_loop(0, GROUPS * 13, tile, 0)


def conv_grad(first, last, padded, grad_conv, tap_sums):
    def tile(step, carry):
        group, column = step // 13, step % 13
        pull = jnp.stack(
            [
                grad_conv[group, pl.ds(pl.multiple_of(i * WIDE + 8 * column, 8), 8), :]
                for i in range(ROWS)
            ]
        )
        for col_tap in range(K):
            window = padded[group, :, pl.ds(8 * column + 5 + col_tap, 8), :]
            for row_tap in range(K):
                tap = row_tap * K + col_tap
                tap_sums[group, tap] += jnp.sum(window[row_tap : row_tap + ROWS] * pull, axis=0)
        return carry

    lax.fori_loop(first, last, tile, 0)


def norm(conv_out, inv_std, gain, offset, normed):
    def block(step, carry):
        place = pl.ds(pl.multiple_of(step * NORM_ROWS, 16), NORM_ROWS)
        held = [conv_out[group, place, :] for group in range(GROUPS)]
        mean = jnp.sum(held[0] + held[1] + held[2], axis=-1, keepdims=True) * (1.0 / C)
        held = [item - mean for item in held]
        squares = held[0] * held[0] + held[1] * held[1] + held[2] * held[2]
        var = jnp.sum(squares, axis=-1, keepdims=True) * (1.0 / C)
        inv = jnp.broadcast_to(lax.rsqrt(var + 1e-06), (NORM_ROWS, LANES))
        inv_std[place, :] = inv
        for group in range(GROUPS):
            centred = held[group] * inv
            conv_out[group, place, :] = centred
            normed[place, lanes(group)] = (
                centred * line(gain, group) + line(offset, group)
            ).astype(jnp.bfloat16)
        return carry

    lax.fori_loop(0, CELLS // NORM_ROWS, block, 0)


def branch_grad(cot_masked, scale, grad_branch, sums):
    def block(step, carry):
        place = pl.ds(pl.multiple_of(step * NORM_ROWS, 16), NORM_ROWS)
        for group in range(GROUPS):
            pull = cot_masked[group, place, :] * (line(scale, group) * LOSS_SCALE)
            grad_branch[place, lanes(group)] = pull.astype(jnp.bfloat16)
            sums[group] += by_eight(pull)
        return carry

    lax.fori_loop(0, CELLS // NORM_ROWS, block, 0)


def turn(rows, turned):
    def block(step, carry):
        place = pl.ds(pl.multiple_of(step * LANES, LANES), LANES)
        turned[:, place] = rows[place, :].T
        return carry

    lax.fori_loop(0, PADDED // LANES, block, 0)


def nt(left, right):
    return lax.dot_general(
        left, right, (((1,), (1,)), ((), ())), preferred_element_type=jnp.float32
    )


def rows_of(block):
    return slice(block * PAIR, (block + 1) * PAIR)


def mlp_enter(chunk, block, normed, grad_branch, w_in, w_out, pre_act, pull):
    units = slice(chunk * CHUNK, (chunk + 1) * CHUNK)
    place = rows_of(block)
    pre_act[...] = jnp.dot(normed[place, :], w_in[:, units], preferred_element_type=jnp.float32)
    pull[...] = nt(grad_branch[place, :], w_out[units, :])


def mlp_strips(chunk, block, b_in, pre_act, pull, hidden, grad_pre, in_sums):
    units = slice(chunk * CHUNK, (chunk + 1) * CHUNK)
    bias = b_in[units].reshape(1, CHUNK)
    total = in_sums[:, units]
    for first in range(0, PAIR, STRIP):
        strip = slice(first, first + STRIP)
        place = slice(block * PAIR + first, block * PAIR + first + STRIP)
        activ, slope = gelu_parts(pre_act[strip, :] + bias)
        hidden[place, :] = activ.astype(jnp.bfloat16)
        back = pull[strip, :] * slope
        total = total + back[:8] + back[8:]
        grad_pre[place, :] = back.astype(jnp.bfloat16)
    in_sums[:, units] = total


def mlp_leave(chunk, block, hidden, grad_pre, w_in, w_out, b_out, branch, grad_xn):
    units = slice(chunk * CHUNK, (chunk + 1) * CHUNK)
    place = rows_of(block)
    out = jnp.dot(hidden[place, :], w_out[units, :], preferred_element_type=jnp.float32)
    back = nt(grad_pre[place, :], w_in[:, units])
    if chunk == 0:
        branch[place, :] = out + b_out[...].reshape(1, C)
        grad_xn[place, :] = back
    else:
        branch[place, :] += out
        grad_xn[place, :] += back


def weight_grads(chunk, normed_t, grad_branch_t, hidden, grad_pre, large):
    first = jnp.dot(normed_t[...], grad_pre[...], preferred_element_type=jnp.float32)
    for group in range(CHUNK // LANES):
        large[chunk, 0, group * C : (group + 1) * C, :] = first[:, lanes(group)]
    second = jnp.dot(grad_branch_t[...], hidden[...], preferred_element_type=jnp.float32).T
    for group in range(GROUPS):
        large[chunk, 1, group * CHUNK : (group + 1) * CHUNK, :] = second[:, lanes(group)]


def after_mlp(first, last, branch, grad_xn, cot_masked, padded, centred, inv_std, mask, scale, gain, mixed, grad_conv, sums):
    def part(i, start, size):
        place = pl.ds(pl.multiple_of(i * WIDE + start, 8), size)
        live = mask[1 + i // TP, start : start + size]
        used = min(BREADTH - start, size)
        pulls, held = [], []
        for group in range(GROUPS):
            out = branch[place, lanes(group)].astype(jnp.bfloat16).astype(jnp.float32)
            sums[3 + group] += by_eight(cot_masked[group, place, :] * out)
            kept = padded[group, i + REACH, 8 + start : 8 + start + size, :]
            kept = kept + live * (line(scale, group) * out)
            mixed[i, start : start + used, lanes(group)] = kept[:used].astype(jnp.bfloat16)
        for group in range(GROUPS):
            pull = grad_xn[place, lanes(group)].astype(jnp.bfloat16).astype(jnp.float32)
            cen = centred[group, place, :]
            sums[6 + group] += by_eight(pull * cen)
            sums[9 + group] += by_eight(pull)
            pulls.append(pull * line(gain, group))
            held.append(cen)
        mean = jnp.sum(pulls[0] + pulls[1] + pulls[2], axis=-1, keepdims=True) * (1.0 / C)
        along = pulls[0] * held[0] + pulls[1] * held[1] + pulls[2] * held[2]
        along = jnp.sum(along, axis=-1, keepdims=True) * (1.0 / C)
        inv = inv_std[place, :]
        for group in range(GROUPS):
            pull = inv * (pulls[group] - mean - held[group] * along)
            grad_conv[group, place, :] = pull
            sums[12 + group] += by_eight(pull)

    def row(i, carry):
        part(i, 0, 48)
        part(i, 48, 56)
        return carry

    lax.fori_loop(first, last, row, 0)


def collect(tap_sums, sums, in_sums, small):
    def put(place, value):
        small[place : place + 1, :] = jnp.sum(value, axis=0, keepdims=True)

    small[168:, :] = jnp.zeros((2 * LANES - 168, LANES), jnp.float32)
    for group in range(GROUPS):
        for tap in range(K * K):
            put(group * K * K + tap, tap_sums[group, tap])
    for index in range(15):
        value = sums[index]
        put(147 + index, value * LOSS_SCALE if 3 <= index < 6 else value)
    for group in range(HID // LANES):
        put(162 + group, in_sums[:, lanes(group)])


def plan():
    large = [
        Sum(1536, jnp.bfloat16, scatter, exchange)
        for scatter, exchange in ((("z", "y"), ("x",)), (("y", "z"), ("x",)), (("x", "z"), ("y",)))
    ]
    return large + [Spread()]


F32, B16 = jnp.float32, jnp.bfloat16
FORWARD = (
    ((GROUPS, ROWS + 2 * REACH, 120, LANES), F32),
    ((GROUPS, CELLS, LANES), F32),
    ((GROUPS, CELLS, LANES), F32),
    ((CELLS, LANES), F32),
    ((PADDED, C), B16),
    ((PADDED, C), B16),
    ((C, PADDED), B16),
    ((C, PADDED), B16),
    ((15, 8, LANES), F32),
    ((4, WIDE, LANES), F32),
)
MIDDLE = (
    ((CHUNKS, 2, 1536, LANES), F32),
    ((CELLS, C), F32),
    ((CELLS, C), F32),
    ((8, HID), F32),
)
LAST = (
    ((ROWS, BREADTH, C), B16),
    ((CHUNKS, 2, 1536, LANES), B16),
    ((2 * LANES, LANES), F32),
)


def shapes_of(layout):
    return tuple(jax.ShapeDtypeStruct(shape, dtype) for shape, dtype in layout)


def vmem(layout):
    return [pltpu.VMEM(shape, dtype) for shape, dtype in layout]


def enter_forward(where):
    tile = lax.axis_index("tile")
    barrier = pltpu.get_barrier_semaphore()
    for step in (1, 31):
        peer = (where["z"], (tile + step) % 32)
        pl.semaphore_signal(barrier, inc=1, device_id=peer, device_id_type=MESH)
    pl.semaphore_wait(barrier, 2)


def forward_kernel(
    feat, cot, table, dw_weight, dw_bias, gain, offset, scale,
    padded, cot_masked, centred, inv_std, normed, grad_branch, normed_t, grad_branch_t, sums, mask,
    halo, halo_send, halo_recv, taps, bias_rows,
):
    where = coordinates()
    tile = lax.axis_index("tile")
    enter_forward(where)
    halves = []
    for side, step, first in ((0, 1, ROWS - REACH), (1, 31, 0)):
        made = pltpu.make_async_remote_copy(
            src_ref=feat.at[pl.ds(first, REACH)],
            dst_ref=halo.at[side],
            send_sem=halo_send.at[side],
            recv_sem=halo_recv.at[side],
            device_id=(where["z"], (tile + step) % 32),
            device_id_type=MESH,
        )
        made.start()
        halves.append(made)
    spread_tissue(table, mask)
    spread_taps(dw_weight, taps, dw_bias, bias_rows)
    sums[...] = jnp.zeros(sums.shape, jnp.float32)
    for rows in (normed, grad_branch):
        rows[CELLS:, :] = jnp.zeros((PADDED - CELLS, rows.shape[1]), jnp.bfloat16)
    fill(feat, cot, mask, padded, cot_masked)
    branch_grad(cot_masked, scale, grad_branch, sums)
    turn(grad_branch, grad_branch_t)
    for made in halves:
        made.wait_recv()
    fill_halo(halo, mask, padded)
    conv(padded, taps, bias_rows, centred)
    norm(centred, inv_std, gain, offset, normed)
    turn(normed, normed_t)
    for made in halves:
        made.wait_send()


def mlp_kernel(
    normed, grad_branch, normed_t, grad_branch_t, w_in, b_in, w_out, b_out,
    large, branch, grad_xn, in_sums,
    hidden, grad_pre, pre_act, pull,
):
    in_sums[...] = jnp.zeros(in_sums.shape, jnp.float32)
    for rows in (hidden.at[0], hidden.at[1], grad_pre.at[0], grad_pre.at[1]):
        rows[CELLS:, :] = jnp.zeros((PADDED - CELLS, rows.shape[1]), jnp.bfloat16)
    steps = [(chunk, block) for chunk in range(CHUNKS) for block in range(BLOCKS)]

    def enter_step(place):
        if place < len(steps):
            chunk, block = steps[place]
            side = place % 2
            mlp_enter(
                chunk, block, normed, grad_branch, w_in, w_out, pre_act.at[side], pull.at[side]
            )

    def leave_step(place):
        chunk, block = steps[place]
        half = chunk % 2
        mlp_leave(
            chunk, block, hidden.at[half], grad_pre.at[half], w_in, w_out, b_out, branch, grad_xn
        )

    def finish_chunk(chunk):
        half = chunk % 2
        weight_grads(chunk, normed_t, grad_branch_t, hidden.at[half], grad_pre.at[half], large)

    enter_step(0)
    for place, (chunk, block) in enumerate(steps):
        half, side = chunk % 2, place % 2
        enter_step(place + 1)
        mlp_strips(
            chunk, block, b_in, pre_act.at[side], pull.at[side], hidden.at[half], grad_pre.at[half],
            in_sums,
        )
        if place > 0:
            leave_step(place - 1)
        if block == 0 and chunk > 0:
            finish_chunk(chunk - 1)
    leave_step(len(steps) - 1)
    finish_chunk(CHUNKS - 1)


def tail_kernel(
    padded, cot_masked, centred, inv_std, first_sums, mask, large, branch, grad_xn, in_sums, gain, scale,
    mixed_out, large_out, small_out,
    mixed, large_held, small_held, sums, tap_sums, grad_conv, small, out_sems, *refs
):
    refs = list(refs)
    where = coordinates()
    core = where["core"]
    enter(where)
    running = []
    for index, item in enumerate(plan()):
        count = len(item.scratch())
        mine, refs = refs[:count], refs[count:]
        if index < CHUNKS:
            keep, send = large.at[index, core], large.at[index, 1 - core]
            item.bind(where, keep, send, large_held.at[index], mine)
        else:
            item.bind(where, small, small_held, mine)
        running.append(item)
    copies = []

    def store(source, target):
        made = pltpu.make_async_copy(source, target, out_sems.at[len(copies)])
        made.start()
        copies.append(made)

    def advance(*which):
        for index in which:
            item = running[index]
            before = item.phase
            if not item.advance() and item.phase > before:
                if index < CHUNKS:
                    store(large_held.at[index], large_out.at[index])
                else:
                    store(small_held, small_out)

    advance(0, 1, 2)
    sums[...] = first_sums[...]
    tap_sums[...] = jnp.zeros(tap_sums.shape, jnp.float32)
    advance(0, 1, 2)
    first = 0
    for last, which in ((7, ()), (14, (0, 1, 2))):
        after_mlp(
            first, last, branch, grad_xn, cot_masked, padded, centred, inv_std, mask, scale, gain, mixed,
            grad_conv, sums,
        )
        advance(*which)
        first = last
    store(mixed, mixed_out)
    first = 0
    for last, which in ((10, (0, 1, 2)), (18, (0, 1, 2)), (28, (0, 1, 2)), (39, ())):
        conv_grad(first, last, padded, grad_conv, tap_sums)
        advance(*which)
        first = last
    collect(tap_sums, sums, in_sums, small)
    advance(3)
    while any(item.phase < item.phases for item in running):
        advance(2, 3, 0, 1)
    for made in copies:
        made.wait()


def call(kernel, outs, out_spaces, spaces, scratch, collective, operands):
    remote = {} if collective is None else {"collective_id": collective, "has_side_effects": True}
    return pl.pallas_call(
        kernel,
        out_shape=outs,
        in_specs=[pl.BlockSpec(memory_space=space) for space in spaces],
        out_specs=tuple(pl.BlockSpec(memory_space=space) for space in out_spaces),
        scratch_shapes=scratch,
        compiler_params=pltpu.CompilerParams(vmem_limit_bytes=60 * 1024 * 1024, **remote),
    )(*operands)


def run_block(
    feat, cot, table, dw_weight, dw_bias, gain, offset, w_in, b_in, w_out, b_out, scale
):
    spaces = [pltpu.VMEM] * 8
    spaces[2] = pltpu.SMEM
    padded, cot_masked, centred, inv_std, normed, grad_branch, normed_t, grad_branch_t, sums, mask = call(
        forward_kernel, shapes_of(FORWARD), [pltpu.VMEM] * len(FORWARD), spaces,
        [
            pltpu.VMEM((2, REACH, BREADTH, C), B16),
            pltpu.SemaphoreType.DMA((2,)),
            pltpu.SemaphoreType.DMA((2,)),
            pltpu.VMEM((GROUPS, K * K, 8, LANES), F32),
            pltpu.VMEM((GROUPS, 8, LANES), F32),
        ],
        1, (feat, cot, table, dw_weight, dw_bias, gain, offset, scale),
    )
    large, branch, grad_xn, in_sums = call(
        mlp_kernel, shapes_of(MIDDLE), [pltpu.VMEM] * len(MIDDLE), [pltpu.VMEM] * 8,
        [
            pltpu.VMEM((2, PADDED, CHUNK), B16),
            pltpu.VMEM((2, PADDED, CHUNK), B16),
            pltpu.VMEM((2, PAIR, CHUNK), F32),
            pltpu.VMEM((2, PAIR, CHUNK), F32),
        ],
        None, (normed, grad_branch, normed_t, grad_branch_t, w_in, b_in, w_out, b_out),
    )
    scratch = vmem(LAST) + [
        pltpu.VMEM((15, 8, LANES), F32),
        pltpu.VMEM((GROUPS, K * K, 8, LANES), F32),
        pltpu.VMEM((GROUPS, CELLS, LANES), F32),
        pltpu.VMEM((2 * LANES, LANES), F32),
        pltpu.SemaphoreType.DMA((5,)),
    ]
    for item in plan():
        scratch += item.scratch()
    operands = (
        padded, cot_masked, centred, inv_std, sums, mask, large, branch, grad_xn, in_sums, gain, scale
    )
    return call(
        tail_kernel, shapes_of(LAST), [pl.ANY] * len(LAST), [pltpu.VMEM] * len(operands), scratch, 0,
        operands,
    )


def finish_kernel(
    mixed_in, large_in, small_in, mixed, dw, dwb, ln_gain, ln_bias, w1_out, b1, w2_out, b2, scale,
    large, small, w1, w2, held, in_sems, out_sems
):
    arrive = pltpu.make_async_copy(mixed_in, held, in_sems.at[2 * CHUNKS + 1])
    leave = pltpu.make_async_copy(held, mixed, out_sems.at[2 * CHUNKS])
    little = pltpu.make_async_copy(small_in, small, in_sems.at[2 * CHUNKS])
    pieces = [(chunk, half) for chunk in range(CHUNKS) for half in range(2)]
    loads = [
        pltpu.make_async_copy(large_in.at[piece], large.at[piece], in_sems.at[index])
        for index, piece in enumerate(pieces)
    ]
    for made in [little, arrive] + loads:
        made.start()
    little.wait()

    def row(place):
        return small[place : place + 1, :]

    for group in range(GROUPS):
        for tap in range(K * K):
            dw[tap // K, tap % K : tap % K + 1, lanes(group)] = row(group * K * K + tap)
    for index, target in enumerate((b2, scale, ln_gain, ln_bias, dwb)):
        for group in range(GROUPS):
            target[lanes(group)] = row(147 + index * GROUPS + group).reshape(LANES)
    for group in range(HID // LANES):
        b1[lanes(group)] = row(162 + group).reshape(LANES)

    arrive.wait()
    leave.start()
    stores = []
    for index, (chunk, half) in enumerate(pieces):
        loads[index].wait()
        units = slice(chunk * CHUNK, (chunk + 1) * CHUNK)
        if half == 0:
            for group in range(CHUNK // LANES):
                first = chunk * CHUNK + group * LANES
                w1[:, first : first + LANES] = large[
                    chunk, 0, group * C : (group + 1) * C, :
                ].astype(jnp.float32)
            made = pltpu.make_async_copy(w1.at[:, units], w1_out.at[:, units], out_sems.at[index])
        else:
            for group in range(GROUPS):
                w2[units, lanes(group)] = large[
                    chunk, 1, group * CHUNK : (group + 1) * CHUNK, :
                ].astype(jnp.float32)
            made = pltpu.make_async_copy(w2.at[units, :], w2_out.at[units, :], out_sems.at[index])
        made.start()
        stores.append(made)
    for made in stores + [leave]:
        made.wait()


def finish(mixed, large, small):
    def f32(*shape):
        return jax.ShapeDtypeStruct(shape, jnp.float32)

    vector = f32(C)
    spaces = [pltpu.VMEM] * 10
    spaces[0] = spaces[5] = spaces[7] = pl.ANY
    return pl.pallas_call(
        finish_kernel,
        out_shape=(
            jax.ShapeDtypeStruct(mixed.shape, mixed.dtype), f32(K, K, C), vector, vector, vector,
            f32(C, HID), f32(HID), f32(HID, C), vector, vector,
        ),
        in_specs=[pl.BlockSpec(memory_space=pl.ANY)] * 3,
        out_specs=tuple(pl.BlockSpec(memory_space=space) for space in spaces),
        scratch_shapes=[
            pltpu.VMEM(large.shape, large.dtype),
            pltpu.VMEM(small.shape, small.dtype),
            pltpu.VMEM((C, HID), jnp.float32),
            pltpu.VMEM((HID, C), jnp.float32),
            pltpu.VMEM(mixed.shape, mixed.dtype),
            pltpu.SemaphoreType.DMA((2 * CHUNKS + 2,)),
            pltpu.SemaphoreType.DMA((2 * CHUNKS + 1,)),
        ],
        compiler_params=pltpu.CompilerParams(vmem_limit_bytes=60 * 1024 * 1024),
    )(mixed, large, small)


def local(
    features,
    cotangent,
    owner_slot,
    dw_weight,
    dw_bias,
    ln_gain,
    ln_bias,
    w_in,
    b_in,
    w_out,
    b_out,
    layer_scale,
):
    mixed, large, small = run_block(
        features[0],
        cotangent[0],
        owner_slot[0],
        dw_weight,
        dw_bias,
        ln_gain,
        ln_bias,
        w_in,
        b_in,
        w_out,
        b_out,
        layer_scale,
    )
    outs = finish(mixed, large, small)
    return (outs[0][None],) + tuple(outs[1:])


def solution(mesh):
    placed = (
        P("slide", "tile", None, None),
        P("slide", "tile", None, None),
        P("slide", None, None),
        P(),
        P(),
        P(),
        P(),
        P(),
        P(),
        P(),
        P(),
        P(),
    )
    return jax.shard_map(
        local,
        mesh=mesh,
        in_specs=placed,
        out_specs=(P("slide", "tile", None, None), P(), P(), P(), P(), P(), P(), P(), P(), P()),
        check_vma=False,
    )
```

```python
import math

import jax
import jax.numpy as jnp
from jax import lax
from jax.experimental import pallas as pl
from jax.experimental.pallas import tpu as pltpu
from jax.sharding import PartitionSpec as P

C = 384
HID = 1536
K = 7
TP = 7
COLS = 14
OWN = 16
ROWS = 14
BREADTH = 98
WIDE = 104
CELLS = ROWS * WIDE
PADDED = 1536
REACH = 3
CHUNK = 512
CHUNKS = HID // CHUNK
PAIR = 2 * WIDE
BLOCKS = CELLS // PAIR
NORM_ROWS = 112
STRIP = 16
GROUPS = C // 128
LOSS_SCALE = 1.0 / math.sqrt(8 * 32 * OWN * TP * TP)

CORES = 2
SIZES = {"x": 4, "y": 4, "z": 8}
LANES = 128
MESH = pl.DeviceIdType.MESH


def coordinates():
    tile = lax.axis_index("tile")
    return {
        "z": lax.axis_index("slide"),
        "y": tile // 8,
        "x": (tile // 2) % 4,
        "core": tile % 2,
    }


def device_at(where):
    return (where["z"], where["y"] * 8 + where["x"] * 2 + where["core"])


def peer_along(where, axis, distance):
    size = SIZES[axis]
    position = (where[axis] + distance) % size
    return position, device_at({**where, axis: position})


def stack_peer(where, distance):
    place = (where["z"] * 2 + where["core"] + distance) % 16
    return place, device_at({**where, "z": place // 2, "core": place % 2})


def plane_peer(where, distance):
    place = (where["y"] * 4 + where["x"] + distance) % 16
    return place, device_at({**where, "y": place // 4, "x": place % 4})


def enter(where):
    tile = lax.axis_index("tile")
    peers = [(where["z"], (tile + step) % 32) for step in (1, 31)]
    for step in range(1, 16):
        peers += [stack_peer(where, step)[1], plane_peer(where, step)[1]]
    barrier = pltpu.get_barrier_semaphore()
    for peer in peers:
        pl.semaphore_signal(barrier, inc=1, device_id=peer, device_id_type=MESH)
    pl.semaphore_wait(barrier, len(peers))


class Sum:
    def __init__(self, rows, dtype, scatter, exchange):
        self.rows, self.dtype = rows, dtype
        self.scatter, self.exchange = scatter, exchange
        self.heights = [rows]
        for axis in scatter:
            self.heights.append(self.heights[-1] // SIZES[axis])
        self.phases = 2 * len(scatter) + len(exchange) + 3
        self.copies = 2 + 2 * sum(SIZES[a] - 1 for a in scatter) + sum(SIZES[a] - 1 for a in exchange)

    def scratch(self):
        shapes = [pltpu.VMEM((self.rows, LANES), jnp.float32)]
        for axis, before, after in zip(self.scatter, self.heights, self.heights[1:]):
            shapes.append(pltpu.VMEM((before, LANES), jnp.float32))
            shapes.append(pltpu.VMEM((before, LANES), self.dtype))
            shapes.append(pltpu.VMEM((SIZES[axis] - 1, after, LANES), self.dtype))
        for axis in self.exchange:
            shapes.append(pltpu.VMEM((SIZES[axis], self.heights[-1], LANES), self.dtype))
        shapes.append(pltpu.SemaphoreType.DMA((self.copies,)))
        shapes.append(pltpu.SemaphoreType.DMA((self.copies,)))
        return shapes

    def bind(self, where, keep, send, result, refs):
        refs = list(refs)
        self.where, self.keep, self.send, self.result = where, keep, send, result
        self.landed = refs.pop(0)
        self.levels = [tuple(refs.pop(0) for _ in range(3)) for _ in self.scatter]
        self.slots = [refs.pop(0) for _ in self.exchange]
        self.send_sems, self.recv_sems = refs
        self.used = 0
        self.flying = []
        self.done = []
        self.phase = 0
        offset = 0
        self.offsets = [offset]
        for axis, height in zip(self.scatter, self.heights[1:]):
            offset = offset + where[axis] * height
            self.offsets.append(offset)
        return self

    def copy(self, source, target, device):
        made = pltpu.make_async_remote_copy(
            src_ref=source,
            dst_ref=target,
            send_sem=self.send_sems.at[self.used],
            recv_sem=self.recv_sems.at[self.used],
            device_id=device,
            device_id_type=MESH,
        )
        self.used += 1
        made.start()
        self.flying.append(made)

    def land(self):
        for made in self.flying:
            made.wait_recv()
        self.done += self.flying
        self.flying = []

    def rows_at(self, level):
        return pl.ds(pl.multiple_of(self.offsets[level], 16), self.heights[level])

    def start_core(self):
        other = device_at({**self.where, "core": 1 - self.where["core"]})
        self.copy(self.send, self.landed, other)

    def start_scatter(self, index, total):
        axis, height = self.scatter[index], self.heights[index + 1]
        held, outgoing, incoming = self.levels[index]
        held[...] = total
        outgoing[...] = total.astype(self.dtype)
        for step in range(1, SIZES[axis]):
            position, device = peer_along(self.where, axis, step)
            self.copy(
                outgoing.at[pl.ds(pl.multiple_of(position * height, 16), height), :],
                incoming.at[step - 1],
                device,
            )

    def finish_scatter(self, index):
        axis, height = self.scatter[index], self.heights[index + 1]
        held, _, incoming = self.levels[index]
        total = held[pl.ds(pl.multiple_of(self.where[axis] * height, 16), height), :]
        for step in range(SIZES[axis] - 1):
            total = total + incoming[step].astype(jnp.float32)
        return total

    def start_exchange(self, index, total):
        axis, slots = self.exchange[index], self.slots[index]
        me = self.where[axis]
        slots[me] = total.astype(self.dtype)
        for step in range(1, SIZES[axis]):
            _, device = peer_along(self.where, axis, step)
            self.copy(slots.at[me], slots.at[me], device)

    def finish_exchange(self, index):
        axis, slots = self.exchange[index], self.slots[index]
        total = slots[0].astype(jnp.float32)
        for place in range(1, SIZES[axis]):
            total = total + slots[place].astype(jnp.float32)
        return total

    def start_gather(self, index):
        axis, core = self.scatter[index], self.where["core"]
        block = self.result.at[core, self.rows_at(index + 1), :]
        for step in range(1, SIZES[axis]):
            _, device = peer_along(self.where, axis, step)
            self.copy(block, block, device)

    def advance(self):
        phase, core = self.phase, self.where["core"]
        deep, wide = len(self.scatter), len(self.exchange)
        if phase >= self.phases:
            return False
        self.phase += 1
        self.land()
        if phase == 0:
            self.start_core()
            return True
        if phase == 1:
            total = self.keep[...] + self.landed[...]
            self.start_scatter(0, total)
            return True
        if phase <= deep + wide:
            if phase <= deep:
                total = self.finish_scatter(phase - 2)
                self.start_scatter(phase - 1, total)
                return True
            index = phase - deep - 1
            total = self.finish_scatter(deep - 1) if index == 0 else self.finish_exchange(index - 1)
            self.start_exchange(index, total)
            return True
        step = phase - deep - wide - 1
        if step == 0:
            total = self.finish_exchange(wide - 1)
            self.result[core, self.rows_at(deep), :] = total.astype(self.dtype)
        if step < deep:
            self.start_gather(deep - 1 - step)
            return True
        if step == deep:
            other = device_at({**self.where, "core": 1 - core})
            self.copy(self.result.at[core], self.result.at[core], other)
            return True
        for made in self.done:
            made.wait_send()
        return False


class Spread:
    ROWS = 16
    phases = 4

    def scratch(self):
        return [
            pltpu.VMEM((15, self.ROWS, LANES), jnp.float32),
            pltpu.VMEM((16, self.ROWS, LANES), jnp.float32),
            pltpu.SemaphoreType.DMA((45,)),
            pltpu.SemaphoreType.DMA((45,)),
        ]

    def bind(self, where, source, result, refs):
        self.where, self.source, self.result = where, source, result
        self.landed, self.slots, self.send_sems, self.recv_sems = refs
        self.used, self.phase = 0, 0
        self.flying, self.done = [], []
        return self

    copy = Sum.copy
    land = Sum.land

    def advance(self):
        phase, where, rows = self.phase, self.where, self.ROWS
        if phase >= self.phases:
            return False
        self.phase += 1
        self.land()
        place, flat = where["z"] * 2 + where["core"], where["y"] * 4 + where["x"]
        mine = pl.ds(pl.multiple_of(place * rows, rows), rows)
        if phase == 0:
            for step in range(1, 16):
                other, device = stack_peer(where, step)
                block = self.source.at[pl.ds(pl.multiple_of(other * rows, rows), rows), :]
                self.copy(block, self.landed.at[step - 1], device)
        elif phase == 1:
            total = self.source[mine, :]
            for step in range(15):
                total = total + self.landed[step]
            self.slots[flat] = total
            for step in range(1, 16):
                _, device = plane_peer(where, step)
                self.copy(self.slots.at[flat], self.slots.at[flat], device)
        elif phase == 2:
            total = self.slots[0]
            for index in range(1, 16):
                total = total + self.slots[index]
            self.result[mine, :] = total
            block = self.result.at[mine, :]
            for step in range(1, 16):
                _, device = stack_peer(where, step)
                self.copy(block, block, device)
        else:
            for made in self.done:
                made.wait_send()
            return False
        return True


def lanes(group):
    return slice(group * LANES, (group + 1) * LANES)


def line(vector, group):
    return vector[lanes(group)].reshape(1, LANES)


def by_eight(value):
    return jnp.sum(value.reshape(-1, 8, LANES), axis=0)


def gelu_parts(pre_act):
    density = jnp.exp(-0.5 * pre_act * pre_act) * 0.3989422804014327
    t = pl.reciprocal(1.0 + 0.2316419 * jnp.abs(pre_act), approx=False)
    series = 1.781477937 + t * (-1.821255978 + t * 1.330274429)
    series = t * (0.319381530 + t * (-0.356563782 + t * series))
    tail = density * series
    mass = jnp.where(pre_act >= 0.0, 1.0 - tail, tail)
    return pre_act * mass, mass + pre_act * density


def spread_tissue(table, mask):
    tile = lax.axis_index("tile")
    mask[:, 96:WIDE, :] = jnp.zeros((4, WIDE - 96, LANES), jnp.float32)
    for place in range(4):
        row = jnp.clip(2 * tile - 1 + place, 0, 63)
        inside = 1.0
        if place == 0:
            inside = jnp.where(tile > 0, 1.0, 0.0)
        if place == 3:
            inside = jnp.where(tile < 31, 1.0, 0.0)
        for column in range(COLS):
            live = jnp.where(table[column, row] >= 0, 1.0, 0.0) * inside
            mask[place, column * TP : (column + 1) * TP, :] = jnp.full((TP, LANES), live, jnp.float32)


def fill(feat, cot, mask, padded, cot_masked):
    edge = jnp.zeros((3, ROWS + 2 * REACH, 8, LANES), jnp.float32)
    padded[:, :, 0:8, :] = edge
    padded[:, :, 104:112, :] = edge
    padded[:, :, 112:120, :] = edge

    def row(i, carry):
        live = mask[1 + i // TP][:BREADTH]
        cells = feat[i].astype(jnp.float32)
        pull = cot[i].astype(jnp.float32)
        for group in range(GROUPS):
            padded[group, i + REACH, 8 : 8 + BREADTH, :] = cells[:, lanes(group)] * live
            end = pl.ds(pl.multiple_of(i * WIDE + WIDE - 8, 8), 8)
            cot_masked[group, end, :] = jnp.zeros((8, LANES), jnp.float32)
            place = pl.ds(pl.multiple_of(i * WIDE, 8), BREADTH)
            cot_masked[group, place, :] = pull[:, lanes(group)] * live
        return carry

    lax.fori_loop(0, ROWS, row, 0)


def fill_halo(halo, mask, padded):
    def row(i, carry):
        for side in range(2):
            live = mask[3 * side][:BREADTH]
            cells = halo[side, i].astype(jnp.float32)
            for group in range(GROUPS):
                padded[group, i + side * (ROWS + REACH), 8 : 8 + BREADTH, :] = (
                    cells[:, lanes(group)] * live
                )
        return carry

    lax.fori_loop(0, REACH, row, 0)


def spread_taps(weight, taps, bias, bias_rows):
    for group in range(GROUPS):
        bias_rows[group] = jnp.broadcast_to(line(bias, group), (8, LANES))
    for tap in range(K * K):
        for group in range(GROUPS):
            taps[group, tap] = jnp.broadcast_to(weight[tap // K, tap % K : tap % K + 1, lanes(group)], (8, LANES))


def conv(padded, taps, bias_rows, conv_out):
    def tile(step, carry):
        group, column = step // 13, step % 13
        total = jnp.zeros((ROWS, 8, LANES), jnp.float32) + bias_rows[group]
        for col_tap in range(K):
            window = padded[group, :, pl.ds(8 * column + 5 + col_tap, 8), :]
            for row_tap in range(K):
                total = total + window[row_tap : row_tap + ROWS] * taps[group, row_tap * K + col_tap]
        for i in range(ROWS):
            conv_out[group, pl.ds(pl.multiple_of(i * WIDE + 8 * column, 8), 8), :] = total[i]
        return carry

    lax.fori_loop(0, GROUPS * 13, tile, 0)


def conv_grad(first, last, padded, grad_conv, tap_sums):
    def tile(step, carry):
        group, column = step // 13, step % 13
        pull = jnp.stack(
            [
                grad_conv[group, pl.ds(pl.multiple_of(i * WIDE + 8 * column, 8), 8), :]
                for i in range(ROWS)
            ]
        )
        for col_tap in range(K):
            window = padded[group, :, pl.ds(8 * column + 5 + col_tap, 8), :]
            for row_tap in range(K):
                tap = row_tap * K + col_tap
                tap_sums[group, tap] += jnp.sum(window[row_tap : row_tap + ROWS] * pull, axis=0)
        return carry

    lax.fori_loop(first, last, tile, 0)


def norm(conv_out, inv_std, gain, offset, normed):
    def block(step, carry):
        place = pl.ds(pl.multiple_of(step * NORM_ROWS, 16), NORM_ROWS)
        held = [conv_out[group, place, :] for group in range(GROUPS)]
        mean = jnp.sum(held[0] + held[1] + held[2], axis=-1, keepdims=True) * (1.0 / C)
        held = [item - mean for item in held]
        squares = held[0] * held[0] + held[1] * held[1] + held[2] * held[2]
        var = jnp.sum(squares, axis=-1, keepdims=True) * (1.0 / C)
        inv = jnp.broadcast_to(lax.rsqrt(var + 1e-06), (NORM_ROWS, LANES))
        inv_std[place, :] = inv
        for group in range(GROUPS):
            centred = held[group] * inv
            conv_out[group, place, :] = centred
            normed[place, lanes(group)] = (
                centred * line(gain, group) + line(offset, group)
            ).astype(jnp.bfloat16)
        return carry

    lax.fori_loop(0, CELLS // NORM_ROWS, block, 0)


def branch_grad(cot_masked, scale, grad_branch, sums):
    def block(step, carry):
        place = pl.ds(pl.multiple_of(step * NORM_ROWS, 16), NORM_ROWS)
        for group in range(GROUPS):
            pull = cot_masked[group, place, :] * (line(scale, group) * LOSS_SCALE)
            grad_branch[place, lanes(group)] = pull.astype(jnp.bfloat16)
            sums[group] += by_eight(pull)
        return carry

    lax.fori_loop(0, CELLS // NORM_ROWS, block, 0)


def turn(rows, turned):
    def block(step, carry):
        place = pl.ds(pl.multiple_of(step * LANES, LANES), LANES)
        turned[:, place] = rows[place, :].T
        return carry

    lax.fori_loop(0, PADDED // LANES, block, 0)


def nt(left, right):
    return lax.dot_general(
        left, right, (((1,), (1,)), ((), ())), preferred_element_type=jnp.float32
    )


def rows_of(block):
    return slice(block * PAIR, (block + 1) * PAIR)


def mlp_enter(chunk, block, normed, grad_branch, w_in, w_out, pre_act, pull):
    units = slice(chunk * CHUNK, (chunk + 1) * CHUNK)
    place = rows_of(block)
    pre_act[...] = jnp.dot(normed[place, :], w_in[:, units], preferred_element_type=jnp.float32)
    pull[...] = nt(grad_branch[place, :], w_out[units, :])


def mlp_strips(chunk, block, b_in, pre_act, pull, hidden, grad_pre, in_sums):
    units = slice(chunk * CHUNK, (chunk + 1) * CHUNK)
    bias = b_in[units].reshape(1, CHUNK)
    total = in_sums[:, units]
    for first in range(0, PAIR, STRIP):
        strip = slice(first, first + STRIP)
        place = slice(block * PAIR + first, block * PAIR + first + STRIP)
        activ, slope = gelu_parts(pre_act[strip, :] + bias)
        hidden[place, :] = activ.astype(jnp.bfloat16)
        back = pull[strip, :] * slope
        total = total + back[:8] + back[8:]
        grad_pre[place, :] = back.astype(jnp.bfloat16)
    in_sums[:, units] = total


def mlp_leave(chunk, block, hidden, grad_pre, w_in, w_out, b_out, branch, grad_xn):
    units = slice(chunk * CHUNK, (chunk + 1) * CHUNK)
    place = rows_of(block)
    out = jnp.dot(hidden[place, :], w_out[units, :], preferred_element_type=jnp.float32)
    back = nt(grad_pre[place, :], w_in[:, units])
    if chunk == 0:
        branch[place, :] = out + b_out[...].reshape(1, C)
        grad_xn[place, :] = back
    else:
        branch[place, :] += out
        grad_xn[place, :] += back


def weight_grads(chunk, normed_t, grad_branch_t, hidden, grad_pre, large):
    first = jnp.dot(normed_t[...], grad_pre[...], preferred_element_type=jnp.float32)
    for group in range(CHUNK // LANES):
        large[chunk, 0, group * C : (group + 1) * C, :] = first[:, lanes(group)]
    second = jnp.dot(grad_branch_t[...], hidden[...], preferred_element_type=jnp.float32).T
    for group in range(GROUPS):
        large[chunk, 1, group * CHUNK : (group + 1) * CHUNK, :] = second[:, lanes(group)]


def after_mlp(first, last, branch, grad_xn, cot_masked, padded, centred, inv_std, mask, scale, gain, mixed, grad_conv, sums):
    def part(i, start, size):
        place = pl.ds(pl.multiple_of(i * WIDE + start, 8), size)
        live = mask[1 + i // TP, start : start + size]
        used = min(BREADTH - start, size)
        pulls, held = [], []
        for group in range(GROUPS):
            out = branch[place, lanes(group)].astype(jnp.bfloat16).astype(jnp.float32)
            sums[3 + group] += by_eight(cot_masked[group, place, :] * out)
            kept = padded[group, i + REACH, 8 + start : 8 + start + size, :]
            kept = kept + live * (line(scale, group) * out)
            mixed[i, start : start + used, lanes(group)] = kept[:used].astype(jnp.bfloat16)
        for group in range(GROUPS):
            pull = grad_xn[place, lanes(group)].astype(jnp.bfloat16).astype(jnp.float32)
            cen = centred[group, place, :]
            sums[6 + group] += by_eight(pull * cen)
            sums[9 + group] += by_eight(pull)
            pulls.append(pull * line(gain, group))
            held.append(cen)
        mean = jnp.sum(pulls[0] + pulls[1] + pulls[2], axis=-1, keepdims=True) * (1.0 / C)
        along = pulls[0] * held[0] + pulls[1] * held[1] + pulls[2] * held[2]
        along = jnp.sum(along, axis=-1, keepdims=True) * (1.0 / C)
        inv = inv_std[place, :]
        for group in range(GROUPS):
            pull = inv * (pulls[group] - mean - held[group] * along)
            grad_conv[group, place, :] = pull
            sums[12 + group] += by_eight(pull)

    def row(i, carry):
        part(i, 0, 48)
        part(i, 48, 56)
        return carry

    lax.fori_loop(first, last, row, 0)


def put(small, place, value):
    small[place : place + 1, :] = jnp.sum(value, axis=0, keepdims=True)


def collect_vectors(sums, in_sums, small):
    small[168:, :] = jnp.zeros((2 * LANES - 168, LANES), jnp.float32)
    for index in range(15):
        value = sums[index]
        put(small, 147 + index, value * LOSS_SCALE if 3 <= index < 6 else value)
    for group in range(HID // LANES):
        put(small, 162 + group, in_sums[:, lanes(group)])


def collect_taps(tap_sums, small):
    for group in range(GROUPS):
        for tap in range(K * K):
            put(small, group * K * K + tap, tap_sums[group, tap])


X_FIRST, Y_FIRST = (("x", "z"), ("y",)), (("y", "z"), ("x",))
PIECES = (
    (0, 0, 1024, X_FIRST),
    (0, 1024, 512, Y_FIRST),
    (1, 0, 1024, Y_FIRST),
    (1, 1024, 512, X_FIRST),
    (2, 0, 1024, X_FIRST),
    (2, 1024, 512, Y_FIRST),
)


def plan():
    return [Sum(rows, jnp.bfloat16, *order) for _, _, rows, order in PIECES] + [Spread()]


def work_scratch():
    def f32(*shape):
        return pltpu.VMEM(shape, jnp.float32)

    def b16(*shape):
        return pltpu.VMEM(shape, jnp.bfloat16)

    return [
        b16(2, REACH, BREADTH, C),
        pltpu.SemaphoreType.DMA((2,)),
        pltpu.SemaphoreType.DMA((2,)),
        f32(GROUPS, ROWS + 2 * REACH, 120, LANES),
        f32(GROUPS, CELLS, LANES),
        f32(GROUPS, K * K, 8, LANES),
        f32(GROUPS, CELLS, LANES),
        f32(CELLS, LANES),
        b16(PADDED, C),
        b16(PADDED, C),
        b16(C, PADDED),
        b16(C, PADDED),
        b16(2, PADDED, CHUNK),
        b16(2, PADDED, CHUNK),
        f32(CELLS, C),
        f32(CELLS, C),
        f32(8, HID),
        f32(15, 8, LANES),
        f32(GROUPS, K * K, 8, LANES),
        f32(GROUPS, CELLS, LANES),
        f32(CHUNKS, 2, 1536, LANES),
        f32(2 * LANES, LANES),
        b16(CHUNKS, 2, 1536, LANES),
        f32(2 * LANES, LANES),
        b16(ROWS, BREADTH, C),
        pltpu.SemaphoreType.DMA((len(PIECES) + 2,)),
        f32(4, WIDE, LANES),
        f32(GROUPS, 8, LANES),
        b16(ROWS, BREADTH, C),
        b16(C, HID),
        b16(HID, C),
        pltpu.SemaphoreType.DMA((3,)),
        f32(2, PAIR, CHUNK),
        f32(2, PAIR, CHUNK),
    ]


def block_kernel(
    feat, cot_in, table, dw_weight, dw_bias, gain, offset, w_in_in, b_in, w_out_in, b_out, scale,
    mixed_out, large_out, small_out, *refs
):
    refs = list(refs)
    own = len(work_scratch())
    (
        halo, halo_send, halo_recv, padded, cot_masked, taps, centred, inv_std, normed, grad_branch,
        normed_t, grad_branch_t, hidden, grad_pre, branch, grad_xn, in_sums, sums, tap_sums,
        grad_conv, large, small, large_held, small_held, mixed, out_sems,
        mask, bias_rows, cot, w_in, w_out, in_sems, pre_act, pull,
    ) = refs[:own]
    refs = refs[own:]
    where = coordinates()
    core, tile = where["core"], lax.axis_index("tile")
    loads = [
        pltpu.make_async_copy(source, target, in_sems.at[index])
        for index, (source, target) in enumerate(((cot_in, cot), (w_in_in, w_in), (w_out_in, w_out)))
    ]
    for made in loads:
        made.start()
    enter(where)
    halves = []
    for side, step, first in ((0, 1, ROWS - REACH), (1, 31, 0)):
        made = pltpu.make_async_remote_copy(
            src_ref=feat.at[pl.ds(first, REACH)],
            dst_ref=halo.at[side],
            send_sem=halo_send.at[side],
            recv_sem=halo_recv.at[side],
            device_id=(where["z"], (tile + step) % 32),
            device_id_type=MESH,
        )
        made.start()
        halves.append(made)
    running = []
    for index, item in enumerate(plan()):
        count = len(item.scratch())
        mine, refs = refs[:count], refs[count:]
        if index < len(PIECES):
            chunk, start, rows, _ = PIECES[index]
            span = pl.ds(start, rows)
            keep, send = large.at[chunk, core, span, :], large.at[chunk, 1 - core, span, :]
            item.bind(where, keep, send, large_held.at[chunk, :, span, :], mine)
        else:
            item.bind(where, small, small_held, mine)
        running.append(item)

    copies = []

    def store(source, target):
        made = pltpu.make_async_copy(source, target, out_sems.at[len(copies)])
        made.start()
        copies.append(made)

    def advance(*which):
        for index, item in enumerate(running):
            chunk = PIECES[index][0] if index < len(PIECES) else CHUNKS
            before = item.phase
            if chunk in which and not item.advance() and item.phase > before:
                if chunk < CHUNKS:
                    _, start, rows, _ = PIECES[index]
                    span = pl.ds(start, rows)
                    store(large_held.at[chunk, :, span, :], large_out.at[chunk, :, span, :])
                else:
                    store(small_held, small_out)

    spread_tissue(table, mask)
    spread_taps(dw_weight, taps, dw_bias, bias_rows)
    sums[...] = jnp.zeros(sums.shape, jnp.float32)
    tap_sums[...] = jnp.zeros(tap_sums.shape, jnp.float32)
    in_sums[...] = jnp.zeros(in_sums.shape, jnp.float32)
    for rows in (normed, grad_branch, hidden.at[0], hidden.at[1], grad_pre.at[0], grad_pre.at[1]):
        rows[CELLS:, :] = jnp.zeros((PADDED - CELLS, rows.shape[1]), jnp.bfloat16)
    loads[0].wait()
    fill(feat, cot, mask, padded, cot_masked)
    branch_grad(cot_masked, scale, grad_branch, sums)
    turn(grad_branch, grad_branch_t)
    for made in halves:
        made.wait_recv()
    fill_halo(halo, mask, padded)
    conv(padded, taps, bias_rows, centred)
    norm(centred, inv_std, gain, offset, normed)
    turn(normed, normed_t)
    loads[1].wait()
    loads[2].wait()

    steps = [(chunk, block) for chunk in range(CHUNKS) for block in range(BLOCKS)]

    def enter_step(place):
        if place < len(steps):
            chunk, block = steps[place]
            side = place % 2
            mlp_enter(
                chunk, block, normed, grad_branch, w_in, w_out, pre_act.at[side], pull.at[side]
            )

    def leave_step(place):
        chunk, block = steps[place]
        half = chunk % 2
        mlp_leave(
            chunk, block, hidden.at[half], grad_pre.at[half], w_in, w_out, b_out, branch, grad_xn
        )

    def finish_chunk(chunk):
        half = chunk % 2
        weight_grads(chunk, normed_t, grad_branch_t, hidden.at[half], grad_pre.at[half], large)

    after_block = {
        (1, 1): (0,), (1, 4): (0,), (2, 0): (0,), (2, 1): (1,), (2, 4): (1, 0), (2, 6): (0,)
    }
    enter_step(0)
    for place, (chunk, block) in enumerate(steps):
        half, side = chunk % 2, place % 2
        enter_step(place + 1)
        mlp_strips(
            chunk, block, b_in, pre_act.at[side], pull.at[side], hidden.at[half], grad_pre.at[half],
            in_sums,
        )
        if place > 0:
            leave_step(place - 1)
        if block == 0 and chunk > 0:
            finish_chunk(chunk - 1)
        advance(*after_block.get((chunk, block), ()))
    leave_step(len(steps) - 1)
    finish_chunk(CHUNKS - 1)
    advance(2)
    advance(1)
    first = 0
    for last, which in ((5, (2,)), (10, (0,)), (14, (1,))):
        after_mlp(
            first, last, branch, grad_xn, cot_masked, padded, centred, inv_std, mask, scale, gain, mixed,
            grad_conv, sums,
        )
        advance(*which)
        first = last
    store(mixed, mixed_out)
    collect_vectors(sums, in_sums, small)
    first = 0
    for last, which in (
        (5, (2,)), (10, (0, 1)), (16, (2,)), (22, (0, 1)), (27, (2,)), (33, (1,)), (39, ())
    ):
        conv_grad(first, last, padded, grad_conv, tap_sums)
        advance(*which)
        first = last
    collect_taps(tap_sums, small)
    advance(3)
    for which in (2, 1, 3, 2, 3, 2, 3):
        advance(which)
    while any(item.phase < item.phases for item in running):
        advance(2)
        advance(3)
        advance(1)
        advance(0)
    for made in copies:
        made.wait()
    for made in halves:
        made.wait_send()


def run_block(*operands):
    scratch = work_scratch()
    spaces = [pltpu.VMEM] * len(operands)
    spaces[1] = spaces[7] = spaces[9] = pl.ANY
    spaces[2] = pltpu.SMEM
    for item in plan():
        scratch += item.scratch()
    return pl.pallas_call(
        block_kernel,
        out_shape=(
            jax.ShapeDtypeStruct((ROWS, BREADTH, C), jnp.bfloat16),
            jax.ShapeDtypeStruct((CHUNKS, 2, 1536, LANES), jnp.bfloat16),
            jax.ShapeDtypeStruct((2 * LANES, LANES), jnp.float32),
        ),
        in_specs=[pl.BlockSpec(memory_space=space) for space in spaces],
        out_specs=(pl.BlockSpec(memory_space=pl.ANY),) * 3,
        scratch_shapes=scratch,
        compiler_params=pltpu.CompilerParams(
            collective_id=0, has_side_effects=True, vmem_limit_bytes=60 * 1024 * 1024
        ),
    )(*operands)


def finish_kernel(
    mixed_in, large_in, small_in, mixed, dw, dwb, ln_gain, ln_bias, w1_out, b1, w2_out, b2, scale,
    large, small, w1, w2, held, in_sems, out_sems
):
    arrive = pltpu.make_async_copy(mixed_in, held, in_sems.at[2 * CHUNKS + 1])
    leave = pltpu.make_async_copy(held, mixed, out_sems.at[2 * CHUNKS])
    little = pltpu.make_async_copy(small_in, small, in_sems.at[2 * CHUNKS])
    pieces = [(chunk, half) for chunk in range(CHUNKS) for half in range(2)]
    loads = [
        pltpu.make_async_copy(large_in.at[piece], large.at[piece], in_sems.at[index])
        for index, piece in enumerate(pieces)
    ]
    for made in [little, arrive] + loads:
        made.start()
    little.wait()

    def row(place):
        return small[place : place + 1, :]

    for group in range(GROUPS):
        for tap in range(K * K):
            dw[tap // K, tap % K : tap % K + 1, lanes(group)] = row(group * K * K + tap)
    for index, target in enumerate((b2, scale, ln_gain, ln_bias, dwb)):
        for group in range(GROUPS):
            target[lanes(group)] = row(147 + index * GROUPS + group).reshape(LANES)
    for group in range(HID // LANES):
        b1[lanes(group)] = row(162 + group).reshape(LANES)

    arrive.wait()
    leave.start()
    stores = []
    for index, (chunk, half) in enumerate(pieces):
        loads[index].wait()
        units = slice(chunk * CHUNK, (chunk + 1) * CHUNK)
        if half == 0:
            for group in range(CHUNK // LANES):
                first = chunk * CHUNK + group * LANES
                w1[:, first : first + LANES] = large[
                    chunk, 0, group * C : (group + 1) * C, :
                ].astype(jnp.float32)
            made = pltpu.make_async_copy(w1.at[:, units], w1_out.at[:, units], out_sems.at[index])
        else:
            for group in range(GROUPS):
                w2[units, lanes(group)] = large[
                    chunk, 1, group * CHUNK : (group + 1) * CHUNK, :
                ].astype(jnp.float32)
            made = pltpu.make_async_copy(w2.at[units, :], w2_out.at[units, :], out_sems.at[index])
        made.start()
        stores.append(made)
    for made in stores + [leave]:
        made.wait()


def finish(mixed, large, small):
    def f32(*shape):
        return jax.ShapeDtypeStruct(shape, jnp.float32)

    vector = f32(C)
    spaces = [pltpu.VMEM] * 10
    spaces[0] = spaces[5] = spaces[7] = pl.ANY
    return pl.pallas_call(
        finish_kernel,
        out_shape=(
            jax.ShapeDtypeStruct(mixed.shape, mixed.dtype), f32(K, K, C), vector, vector, vector,
            f32(C, HID), f32(HID), f32(HID, C), vector, vector,
        ),
        in_specs=[pl.BlockSpec(memory_space=pl.ANY)] * 3,
        out_specs=tuple(pl.BlockSpec(memory_space=space) for space in spaces),
        scratch_shapes=[
            pltpu.VMEM(large.shape, large.dtype),
            pltpu.VMEM(small.shape, small.dtype),
            pltpu.VMEM((C, HID), jnp.float32),
            pltpu.VMEM((HID, C), jnp.float32),
            pltpu.VMEM(mixed.shape, mixed.dtype),
            pltpu.SemaphoreType.DMA((2 * CHUNKS + 2,)),
            pltpu.SemaphoreType.DMA((2 * CHUNKS + 1,)),
        ],
        compiler_params=pltpu.CompilerParams(vmem_limit_bytes=60 * 1024 * 1024),
    )(mixed, large, small)


def local(
    features,
    cotangent,
    owner_slot,
    dw_weight,
    dw_bias,
    ln_gain,
    ln_bias,
    w_in,
    b_in,
    w_out,
    b_out,
    layer_scale,
):
    mixed, large, small = run_block(
        features[0],
        cotangent[0],
        owner_slot[0].T,
        dw_weight,
        dw_bias,
        ln_gain,
        ln_bias,
        w_in,
        b_in,
        w_out,
        b_out,
        layer_scale,
    )
    outs = finish(mixed, large, small)
    return (outs[0][None],) + tuple(outs[1:])


def solution(mesh):
    placed = (
        P("slide", "tile", None, None),
        P("slide", "tile", None, None),
        P("slide", None, None),
        P(),
        P(),
        P(),
        P(),
        P(),
        P(),
        P(),
        P(),
        P(),
    )
    return jax.shard_map(
        local,
        mesh=mesh,
        in_specs=placed,
        out_specs=(P("slide", "tile", None, None), P(), P(), P(), P(), P(), P(), P(), P(), P()),
        check_vma=False,
    )
```

```python
import math

import jax
import jax.numpy as jnp
from jax import lax
from jax.experimental import pallas as pl
from jax.experimental.pallas import tpu as pltpu
from jax.sharding import PartitionSpec as P

C = 384
HID = 1536
K = 7
TP = 7
COLS = 14
OWN = 16
ROWS = 14
BREADTH = 98
WIDE = 104
CELLS = ROWS * WIDE
PADDED = 1536
REACH = 3
CHUNK = 512
CHUNKS = HID // CHUNK
PAIR = 2 * WIDE
BLOCKS = CELLS // PAIR
NORM_ROWS = 112
STRIP = 16
GROUPS = C // 128
LOSS_SCALE = 1.0 / math.sqrt(8 * 32 * OWN * TP * TP)

CORES = 2
SIZES = {"x": 4, "y": 4, "z": 8}
LANES = 128
MESH = pl.DeviceIdType.MESH


def coordinates():
    tile = lax.axis_index("tile")
    return {
        "z": lax.axis_index("slide"),
        "y": tile // 8,
        "x": (tile // 2) % 4,
        "core": tile % 2,
    }


def device_at(where):
    return (where["z"], where["y"] * 8 + where["x"] * 2 + where["core"])


def peer_along(where, axis, distance):
    size = SIZES[axis]
    position = (where[axis] + distance) % size
    return position, device_at({**where, axis: position})


def stack_peer(where, distance):
    place = (where["z"] * 2 + where["core"] + distance) % 16
    return place, device_at({**where, "z": place // 2, "core": place % 2})


def plane_peer(where, distance):
    place = (where["y"] * 4 + where["x"] + distance) % 16
    return place, device_at({**where, "y": place // 4, "x": place % 4})


def enter(where):
    tile = lax.axis_index("tile")
    peers = [(where["z"], (tile + step) % 32) for step in (1, 31)]
    for step in range(1, 16):
        peers += [stack_peer(where, step)[1], plane_peer(where, step)[1]]
    barrier = pltpu.get_barrier_semaphore()
    for peer in peers:
        pl.semaphore_signal(barrier, inc=1, device_id=peer, device_id_type=MESH)
    return barrier, len(peers)


class Sum:
    def __init__(self, rows, dtype, scatter, exchange):
        self.rows, self.dtype = rows, dtype
        self.scatter, self.exchange = scatter, exchange
        self.heights = [rows]
        for axis in scatter:
            self.heights.append(self.heights[-1] // SIZES[axis])
        self.phases = 2 * len(scatter) + len(exchange) + 3

    def scratch(self):
        shapes = [pltpu.VMEM((self.rows, LANES), jnp.float32)]
        for axis, before, after in zip(self.scatter, self.heights, self.heights[1:]):
            shapes.append(pltpu.VMEM((before, LANES), jnp.float32))
            shapes.append(pltpu.VMEM((before, LANES), self.dtype))
            shapes.append(pltpu.VMEM((SIZES[axis] - 1, after, LANES), self.dtype))
        for axis in self.exchange:
            shapes.append(pltpu.VMEM((SIZES[axis], self.heights[-1], LANES), self.dtype))
        shapes.append(pltpu.SemaphoreType.DMA((self.phases,)))
        shapes.append(pltpu.SemaphoreType.DMA((self.phases,)))
        return shapes

    def bind(self, where, keep, send, result, refs):
        refs = list(refs)
        self.where, self.keep, self.send, self.result = where, keep, send, result
        self.landed = refs.pop(0)
        self.levels = [tuple(refs.pop(0) for _ in range(3)) for _ in self.scatter]
        self.slots = [refs.pop(0) for _ in self.exchange]
        self.send_sems, self.recv_sems = refs
        self.flying = []
        self.done = []
        self.phase = 0
        offset = 0
        self.offsets = [offset]
        for axis, height in zip(self.scatter, self.heights[1:]):
            offset = offset + where[axis] * height
            self.offsets.append(offset)
        return self

    def copy(self, source, target, device, start=True):
        made = pltpu.make_async_remote_copy(
            src_ref=source,
            dst_ref=target,
            send_sem=self.send_sems.at[self.phase],
            recv_sem=self.recv_sems.at[self.phase],
            device_id=device,
            device_id_type=MESH,
        )
        if start:
            made.start()
        return made

    def fly(self, everything, device):
        self.flying.append(self.copy(everything, everything, device, start=False))

    def land(self):
        for made in self.flying:
            made.wait_recv()
        self.done += self.flying
        self.flying = []

    def rows_at(self, level):
        return pl.ds(pl.multiple_of(self.offsets[level], 16), self.heights[level])

    def start_core(self):
        other = device_at({**self.where, "core": 1 - self.where["core"]})
        self.copy(self.send, self.landed, other)
        self.fly(self.landed, other)

    def start_scatter(self, index, total):
        axis, height = self.scatter[index], self.heights[index + 1]
        held, outgoing, incoming = self.levels[index]
        held[...] = total
        outgoing[...] = total.astype(self.dtype)
        for step in range(1, SIZES[axis]):
            position, device = peer_along(self.where, axis, step)
            self.copy(
                outgoing.at[pl.ds(pl.multiple_of(position * height, 16), height), :],
                incoming.at[step - 1],
                device,
            )
        self.fly(incoming, device)

    def finish_scatter(self, index):
        axis, height = self.scatter[index], self.heights[index + 1]
        held, _, incoming = self.levels[index]
        total = held[pl.ds(pl.multiple_of(self.where[axis] * height, 16), height), :]
        for step in range(SIZES[axis] - 1):
            total = total + incoming[step].astype(jnp.float32)
        return total

    def start_exchange(self, index, total):
        axis, slots = self.exchange[index], self.slots[index]
        me = self.where[axis]
        slots[me] = total.astype(self.dtype)
        for step in range(1, SIZES[axis]):
            _, device = peer_along(self.where, axis, step)
            self.copy(slots.at[me], slots.at[me], device)
        self.fly(slots.at[pl.ds(0, SIZES[axis] - 1)], device)

    def finish_exchange(self, index):
        axis, slots = self.exchange[index], self.slots[index]
        total = slots[0].astype(jnp.float32)
        for place in range(1, SIZES[axis]):
            total = total + slots[place].astype(jnp.float32)
        return total

    def start_gather(self, index):
        axis, core = self.scatter[index], self.where["core"]
        block = self.result.at[core, self.rows_at(index + 1), :]
        for step in range(1, SIZES[axis]):
            _, device = peer_along(self.where, axis, step)
            self.copy(block, block, device)
        count = (SIZES[axis] - 1) * self.heights[index + 1]
        self.fly(self.result.at[core, pl.ds(0, count), :], device)

    def advance(self):
        phase, core = self.phase, self.where["core"]
        deep, wide = len(self.scatter), len(self.exchange)
        if phase >= self.phases:
            return False
        self.land()
        more = self.step(phase, deep, wide, core)
        self.phase += 1
        return more

    def step(self, phase, deep, wide, core):
        if phase == 0:
            self.start_core()
            return True
        if phase == 1:
            total = self.keep[...] + self.landed[...]
            self.start_scatter(0, total)
            return True
        if phase <= deep + wide:
            if phase <= deep:
                total = self.finish_scatter(phase - 2)
                self.start_scatter(phase - 1, total)
                return True
            index = phase - deep - 1
            total = self.finish_scatter(deep - 1) if index == 0 else self.finish_exchange(index - 1)
            self.start_exchange(index, total)
            return True
        step = phase - deep - wide - 1
        if step == 0:
            total = self.finish_exchange(wide - 1)
            self.result[core, self.rows_at(deep), :] = total.astype(self.dtype)
        if step < deep:
            self.start_gather(deep - 1 - step)
            return True
        if step == deep:
            other = device_at({**self.where, "core": 1 - core})
            self.copy(self.result.at[core], self.result.at[core], other)
            self.fly(self.result.at[core], other)
            return True
        for made in self.done:
            made.wait_send()
        return False


class Spread:
    ROWS = 16
    phases = 4

    def scratch(self):
        return [
            pltpu.VMEM((15, self.ROWS, LANES), jnp.float32),
            pltpu.VMEM((16, self.ROWS, LANES), jnp.float32),
            pltpu.SemaphoreType.DMA((3,)),
            pltpu.SemaphoreType.DMA((3,)),
        ]

    def bind(self, where, source, result, refs):
        self.where, self.source, self.result = where, source, result
        self.landed, self.slots, self.send_sems, self.recv_sems = refs
        self.phase = 0
        self.flying, self.done = [], []
        return self

    copy = Sum.copy
    fly = Sum.fly
    land = Sum.land

    def advance(self):
        phase, where, rows = self.phase, self.where, self.ROWS
        if phase >= self.phases:
            return False
        self.land()
        more = self.step(phase, where, rows)
        self.phase += 1
        return more

    def step(self, phase, where, rows):
        place, flat = where["z"] * 2 + where["core"], where["y"] * 4 + where["x"]
        mine = pl.ds(pl.multiple_of(place * rows, rows), rows)
        if phase == 0:
            for step in range(1, 16):
                other, device = stack_peer(where, step)
                block = self.source.at[pl.ds(pl.multiple_of(other * rows, rows), rows), :]
                self.copy(block, self.landed.at[step - 1], device)
            self.fly(self.landed, device)
        elif phase == 1:
            total = self.source[mine, :]
            for step in range(15):
                total = total + self.landed[step]
            self.slots[flat] = total
            for step in range(1, 16):
                _, device = plane_peer(where, step)
                self.copy(self.slots.at[flat], self.slots.at[flat], device)
            self.fly(self.slots.at[pl.ds(0, 15)], device)
        elif phase == 2:
            total = self.slots[0]
            for index in range(1, 16):
                total = total + self.slots[index]
            self.result[mine, :] = total
            block = self.result.at[mine, :]
            for step in range(1, 16):
                _, device = stack_peer(where, step)
                self.copy(block, block, device)
            self.fly(self.result.at[pl.ds(0, 15 * rows), :], device)
        else:
            for made in self.done:
                made.wait_send()
            return False
        return True


def lanes(group):
    return slice(group * LANES, (group + 1) * LANES)


def line(vector, group):
    return vector[lanes(group)].reshape(1, LANES)


def by_eight(value):
    return jnp.sum(value.reshape(-1, 8, LANES), axis=0)


def gelu_parts(pre_act):
    density = jnp.exp(-0.5 * pre_act * pre_act) * 0.3989422804014327
    t = pl.reciprocal(1.0 + 0.2316419 * jnp.abs(pre_act), approx=False)
    series = 1.781477937 + t * (-1.821255978 + t * 1.330274429)
    series = t * (0.319381530 + t * (-0.356563782 + t * series))
    tail = density * series
    mass = jnp.where(pre_act >= 0.0, 1.0 - tail, tail)
    return pre_act * mass, mass + pre_act * density


def spread_tissue(table, mask):
    tile = lax.axis_index("tile")
    mask[:, 96:WIDE, :] = jnp.zeros((4, WIDE - 96, LANES), jnp.float32)
    for place in range(4):
        row = jnp.clip(2 * tile - 1 + place, 0, 63)
        inside = 1.0
        if place == 0:
            inside = jnp.where(tile > 0, 1.0, 0.0)
        if place == 3:
            inside = jnp.where(tile < 31, 1.0, 0.0)
        for column in range(COLS):
            live = jnp.where(table[column, 0, row] >= 0, 1.0, 0.0) * inside
            mask[place, column * TP : (column + 1) * TP, :] = jnp.full((TP, LANES), live, jnp.float32)


def fill(feat, cot, mask, padded, cot_masked):
    edge = jnp.zeros((3, ROWS + 2 * REACH, 8, LANES), jnp.float32)
    padded[:, :, 0:8, :] = edge
    padded[:, :, 104:112, :] = edge
    padded[:, :, 112:120, :] = edge

    def row(i, carry):
        live = mask[1 + i // TP][:BREADTH]
        cells = feat[i].astype(jnp.float32)
        pull = cot[i].astype(jnp.float32)
        for group in range(GROUPS):
            padded[group, i + REACH, 8 : 8 + BREADTH, :] = cells[:, lanes(group)] * live
            end = pl.ds(pl.multiple_of(i * WIDE + WIDE - 8, 8), 8)
            cot_masked[group, end, :] = jnp.zeros((8, LANES), jnp.float32)
            place = pl.ds(pl.multiple_of(i * WIDE, 8), BREADTH)
            cot_masked[group, place, :] = pull[:, lanes(group)] * live
        return carry

    lax.fori_loop(0, ROWS, row, 0)


def fill_halo(halo, mask, padded):
    def row(i, carry):
        for side in range(2):
            live = mask[3 * side][:BREADTH]
            cells = halo[side, i].astype(jnp.float32)
            for group in range(GROUPS):
                padded[group, i + side * (ROWS + REACH), 8 : 8 + BREADTH, :] = (
                    cells[:, lanes(group)] * live
                )
        return carry

    lax.fori_loop(0, REACH, row, 0)


def spread_taps(weight, taps, bias, bias_rows):
    for group in range(GROUPS):
        bias_rows[group] = jnp.broadcast_to(line(bias, group), (8, LANES))
    for tap in range(K * K):
        for group in range(GROUPS):
            taps[group, tap] = jnp.broadcast_to(weight[tap // K, tap % K : tap % K + 1, lanes(group)], (8, LANES))


def conv(padded, taps, bias_rows, conv_out):
    def tile(step, carry):
        group, column = step // 13, step % 13
        total = jnp.zeros((ROWS, 8, LANES), jnp.float32) + bias_rows[group]
        for col_tap in range(K):
            window = padded[group, :, pl.ds(8 * column + 5 + col_tap, 8), :]
            for row_tap in range(K):
                total = total + window[row_tap : row_tap + ROWS] * taps[group, row_tap * K + col_tap]
        for i in range(ROWS):
            conv_out[group, pl.ds(pl.multiple_of(i * WIDE + 8 * column, 8), 8), :] = total[i]
        return carry

    lax.fori_loop(0, GROUPS * 13, tile, 0)


def conv_grad(first, last, padded, grad_conv, tap_sums):
    def tile(step, carry):
        group, column = step // 13, step % 13
        pull = jnp.stack(
            [
                grad_conv[group, pl.ds(pl.multiple_of(i * WIDE + 8 * column, 8), 8), :]
                for i in range(ROWS)
            ]
        )
        for col_tap in range(K):
            window = padded[group, :, pl.ds(8 * column + 5 + col_tap, 8), :]
            for row_tap in range(K):
                tap = row_tap * K + col_tap
                tap_sums[group, tap] += jnp.sum(window[row_tap : row_tap + ROWS] * pull, axis=0)
        return carry

    lax.fori_loop(first, last, tile, 0)


def norm(conv_out, inv_std, gain, offset, normed):
    def block(step, carry):
        place = pl.ds(pl.multiple_of(step * NORM_ROWS, 16), NORM_ROWS)
        held = [conv_out[group, place, :] for group in range(GROUPS)]
        mean = jnp.sum(held[0] + held[1] + held[2], axis=-1, keepdims=True) * (1.0 / C)
        held = [item - mean for item in held]
        squares = held[0] * held[0] + held[1] * held[1] + held[2] * held[2]
        var = jnp.sum(squares, axis=-1, keepdims=True) * (1.0 / C)
        inv = jnp.broadcast_to(lax.rsqrt(var + 1e-06), (NORM_ROWS, LANES))
        inv_std[place, :] = inv
        for group in range(GROUPS):
            centred = held[group] * inv
            conv_out[group, place, :] = centred
            normed[place, lanes(group)] = (
                centred * line(gain, group) + line(offset, group)
            ).astype(jnp.bfloat16)
        return carry

    lax.fori_loop(0, CELLS // NORM_ROWS, block, 0)


def branch_grad(cot_masked, scale, grad_branch, sums):
    def block(step, carry):
        place = pl.ds(pl.multiple_of(step * NORM_ROWS, 16), NORM_ROWS)
        for group in range(GROUPS):
            pull = cot_masked[group, place, :] * (line(scale, group) * LOSS_SCALE)
            grad_branch[place, lanes(group)] = pull.astype(jnp.bfloat16)
            sums[group] += by_eight(pull)
        return carry

    lax.fori_loop(0, CELLS // NORM_ROWS, block, 0)


def turn(rows, turned):
    def block(step, carry):
        place = pl.ds(pl.multiple_of(step * LANES, LANES), LANES)
        turned[:, place] = rows[place, :].T
        return carry

    lax.fori_loop(0, PADDED // LANES, block, 0)


def nt(left, right):
    return lax.dot_general(
        left, right, (((1,), (1,)), ((), ())), preferred_element_type=jnp.float32
    )


def rows_of(block):
    return slice(block * PAIR, (block + 1) * PAIR)


def mlp_enter(chunk, block, normed, grad_branch, w_in, w_out, pre_act, pull):
    units = slice(chunk * CHUNK, (chunk + 1) * CHUNK)
    place = rows_of(block)
    pre_act[...] = jnp.dot(normed[place, :], w_in[:, units], preferred_element_type=jnp.float32)
    pull[...] = nt(grad_branch[place, :], w_out[units, :])


def mlp_strips(chunk, block, b_in, pre_act, pull, hidden, grad_pre, in_sums):
    units = slice(chunk * CHUNK, (chunk + 1) * CHUNK)
    bias = b_in[units].reshape(1, CHUNK)
    total = in_sums[:, units]
    for first in range(0, PAIR, STRIP):
        strip = slice(first, first + STRIP)
        place = slice(block * PAIR + first, block * PAIR + first + STRIP)
        activ, slope = gelu_parts(pre_act[strip, :] + bias)
        hidden[place, :] = activ.astype(jnp.bfloat16)
        back = pull[strip, :] * slope
        total = total + back[:8] + back[8:]
        grad_pre[place, :] = back.astype(jnp.bfloat16)
    in_sums[:, units] = total


def mlp_leave(chunk, block, hidden, grad_pre, w_in, w_out, b_out, branch, grad_xn):
    units = slice(chunk * CHUNK, (chunk + 1) * CHUNK)
    place = rows_of(block)
    out = jnp.dot(hidden[place, :], w_out[units, :], preferred_element_type=jnp.float32)
    back = nt(grad_pre[place, :], w_in[:, units])
    if chunk == 0:
        branch[place, :] = out + b_out[...].reshape(1, C)
        grad_xn[place, :] = back
    else:
        branch[place, :] += out
        grad_xn[place, :] += back


def weight_grads(chunk, normed_t, grad_branch_t, hidden, grad_pre, large):
    first = jnp.dot(normed_t[...], grad_pre[...], preferred_element_type=jnp.float32)
    for group in range(CHUNK // LANES):
        large[chunk, 0, group * C : (group + 1) * C, :] = first[:, lanes(group)]
    second = jnp.dot(grad_branch_t[...], hidden[...], preferred_element_type=jnp.float32).T
    for group in range(GROUPS):
        large[chunk, 1, group * CHUNK : (group + 1) * CHUNK, :] = second[:, lanes(group)]


def after_mlp(first, last, branch, grad_xn, cot_masked, padded, centred, inv_std, mask, scale, gain, mixed, grad_conv, sums):
    def part(i, start, size):
        place = pl.ds(pl.multiple_of(i * WIDE + start, 8), size)
        live = mask[1 + i // TP, start : start + size]
        used = min(BREADTH - start, size)
        pulls, held = [], []
        for group in range(GROUPS):
            out = branch[place, lanes(group)].astype(jnp.bfloat16).astype(jnp.float32)
            sums[3 + group] += by_eight(cot_masked[group, place, :] * out)
            kept = padded[group, i + REACH, 8 + start : 8 + start + size, :]
            kept = kept + live * (line(scale, group) * out)
            mixed[i, start : start + used, lanes(group)] = kept[:used].astype(jnp.bfloat16)
        for group in range(GROUPS):
            pull = grad_xn[place, lanes(group)].astype(jnp.bfloat16).astype(jnp.float32)
            cen = centred[group, place, :]
            sums[6 + group] += by_eight(pull * cen)
            sums[9 + group] += by_eight(pull)
            pulls.append(pull * line(gain, group))
            held.append(cen)
        mean = jnp.sum(pulls[0] + pulls[1] + pulls[2], axis=-1, keepdims=True) * (1.0 / C)
        along = pulls[0] * held[0] + pulls[1] * held[1] + pulls[2] * held[2]
        along = jnp.sum(along, axis=-1, keepdims=True) * (1.0 / C)
        inv = inv_std[place, :]
        for group in range(GROUPS):
            pull = inv * (pulls[group] - mean - held[group] * along)
            grad_conv[group, place, :] = pull
            sums[12 + group] += by_eight(pull)

    def row(i, carry):
        part(i, 0, 48)
        part(i, 48, 56)
        return carry

    lax.fori_loop(first, last, row, 0)


def put(small, place, value):
    small[place : place + 1, :] = jnp.sum(value, axis=0, keepdims=True)


def collect_vectors(sums, in_sums, small):
    small[168:, :] = jnp.zeros((2 * LANES - 168, LANES), jnp.float32)
    for index in range(15):
        value = sums[index]
        put(small, 147 + index, value * LOSS_SCALE if 3 <= index < 6 else value)
    for group in range(HID // LANES):
        put(small, 162 + group, in_sums[:, lanes(group)])


def collect_taps(tap_sums, small):
    for group in range(GROUPS):
        for tap in range(K * K):
            put(small, group * K * K + tap, tap_sums[group, tap])


X_FIRST, Y_FIRST = (("x", "z"), ("y",)), (("y", "z"), ("x",))
PIECES = ((0, 0, 1536, X_FIRST), (1, 0, 1536, Y_FIRST), (2, 0, 1536, X_FIRST))


def plan():
    return [Sum(rows, jnp.bfloat16, *order) for _, _, rows, order in PIECES] + [Spread()]


def work_scratch():
    def f32(*shape):
        return pltpu.VMEM(shape, jnp.float32)

    def b16(*shape):
        return pltpu.VMEM(shape, jnp.bfloat16)

    return [
        b16(2, REACH, BREADTH, C),
        pltpu.SemaphoreType.DMA((2,)),
        pltpu.SemaphoreType.DMA((2,)),
        f32(GROUPS, ROWS + 2 * REACH, 120, LANES),
        f32(GROUPS, CELLS, LANES),
        f32(GROUPS, K * K, 8, LANES),
        f32(GROUPS, CELLS, LANES),
        f32(CELLS, LANES),
        b16(PADDED, C),
        b16(PADDED, C),
        b16(C, PADDED),
        b16(C, PADDED),
        b16(2, PADDED, CHUNK),
        b16(2, PADDED, CHUNK),
        f32(CELLS, C),
        f32(CELLS, C),
        f32(8, HID),
        f32(15, 8, LANES),
        f32(GROUPS, K * K, 8, LANES),
        f32(GROUPS, CELLS, LANES),
        f32(CHUNKS, 2, 1536, LANES),
        f32(2 * LANES, LANES),
        b16(CHUNKS, 2, 1536, LANES),
        f32(2 * LANES, LANES),
        b16(ROWS, BREADTH, C),
        pltpu.SemaphoreType.DMA((len(PIECES) + 2,)),
        f32(4, WIDE, LANES),
        f32(GROUPS, 8, LANES),
        b16(ROWS, BREADTH, C),
        b16(C, HID),
        b16(HID, C),
        pltpu.SemaphoreType.DMA((3,)),
        f32(2, PAIR, CHUNK),
        f32(2, PAIR, CHUNK),
    ]


def block_kernel(
    feat, cot_in, table, dw_weight, dw_bias, gain, offset, w_in_in, b_in, w_out_in, b_out, scale,
    mixed_out, large_out, small_out, *refs
):
    refs = list(refs)
    own = len(work_scratch())
    (
        halo, halo_send, halo_recv, padded, cot_masked, taps, centred, inv_std, normed, grad_branch,
        normed_t, grad_branch_t, hidden, grad_pre, branch, grad_xn, in_sums, sums, tap_sums,
        grad_conv, large, small, large_held, small_held, mixed, out_sems,
        mask, bias_rows, cot, w_in, w_out, in_sems, pre_act, pull,
    ) = refs[:own]
    refs = refs[own:]
    where = coordinates()
    core, tile = where["core"], lax.axis_index("tile")
    loads = [
        pltpu.make_async_copy(source, target, in_sems.at[index])
        for index, (source, target) in enumerate(((cot_in, cot), (w_in_in, w_in), (w_out_in, w_out)))
    ]
    for made in loads:
        made.start()
    greeting = enter(where)
    spread_tissue(table, mask)
    spread_taps(dw_weight, taps, dw_bias, bias_rows)
    pl.semaphore_wait(*greeting)
    halves = []
    for side, step, first in ((0, 1, ROWS - REACH), (1, 31, 0)):
        made = pltpu.make_async_remote_copy(
            src_ref=feat.at[pl.ds(first, REACH)],
            dst_ref=halo.at[side],
            send_sem=halo_send.at[side],
            recv_sem=halo_recv.at[side],
            device_id=(where["z"], (tile + step) % 32),
            device_id_type=MESH,
        )
        made.start()
        halves.append(made)
    running = []
    for index, item in enumerate(plan()):
        count = len(item.scratch())
        mine, refs = refs[:count], refs[count:]
        if index < len(PIECES):
            chunk, start, rows, _ = PIECES[index]
            span = pl.ds(start, rows)
            keep, send = large.at[chunk, core, span, :], large.at[chunk, 1 - core, span, :]
            item.bind(where, keep, send, large_held.at[chunk, :, span, :], mine)
        else:
            item.bind(where, small, small_held, mine)
        running.append(item)

    copies = []

    def store(source, target):
        made = pltpu.make_async_copy(source, target, out_sems.at[len(copies)])
        made.start()
        copies.append(made)

    def advance(*which):
        for index, item in enumerate(running):
            chunk = PIECES[index][0] if index < len(PIECES) else CHUNKS
            before = item.phase
            if chunk in which and not item.advance() and item.phase > before:
                if chunk < CHUNKS:
                    _, start, rows, _ = PIECES[index]
                    span = pl.ds(start, rows)
                    store(large_held.at[chunk, :, span, :], large_out.at[chunk, :, span, :])
                else:
                    store(small_held, small_out)

    sums[...] = jnp.zeros(sums.shape, jnp.float32)
    tap_sums[...] = jnp.zeros(tap_sums.shape, jnp.float32)
    in_sums[...] = jnp.zeros(in_sums.shape, jnp.float32)
    for rows in (normed, grad_branch, hidden.at[0], hidden.at[1], grad_pre.at[0], grad_pre.at[1]):
        rows[CELLS:, :] = jnp.zeros((PADDED - CELLS, rows.shape[1]), jnp.bfloat16)
    loads[0].wait()
    fill(feat, cot, mask, padded, cot_masked)
    branch_grad(cot_masked, scale, grad_branch, sums)
    turn(grad_branch, grad_branch_t)
    for made in halves:
        made.wait_recv()
    fill_halo(halo, mask, padded)
    conv(padded, taps, bias_rows, centred)
    norm(centred, inv_std, gain, offset, normed)
    turn(normed, normed_t)
    loads[1].wait()
    loads[2].wait()

    steps = [(chunk, block) for chunk in range(CHUNKS) for block in range(BLOCKS)]

    def enter_step(place):
        if place < len(steps):
            chunk, block = steps[place]
            side = place % 2
            mlp_enter(
                chunk, block, normed, grad_branch, w_in, w_out, pre_act.at[side], pull.at[side]
            )

    def leave_step(place):
        chunk, block = steps[place]
        half = chunk % 2
        mlp_leave(
            chunk, block, hidden.at[half], grad_pre.at[half], w_in, w_out, b_out, branch, grad_xn
        )

    def finish_chunk(chunk):
        half = chunk % 2
        weight_grads(chunk, normed_t, grad_branch_t, hidden.at[half], grad_pre.at[half], large)

    after_block = {
        (1, 1): (0,), (1, 4): (0,), (2, 0): (0,), (2, 1): (1,), (2, 4): (1, 0), (2, 6): (0,)
    }
    enter_step(0)
    for place, (chunk, block) in enumerate(steps):
        half, side = chunk % 2, place % 2
        enter_step(place + 1)
        mlp_strips(
            chunk, block, b_in, pre_act.at[side], pull.at[side], hidden.at[half], grad_pre.at[half],
            in_sums,
        )
        if place > 0:
            leave_step(place - 1)
        if block == 0 and chunk > 0:
            finish_chunk(chunk - 1)
        advance(*after_block.get((chunk, block), ()))
    leave_step(len(steps) - 1)
    finish_chunk(CHUNKS - 1)
    advance(2)
    advance(1)
    first = 0
    for last, which in ((5, (2,)), (10, (0,)), (14, (1,))):
        after_mlp(
            first, last, branch, grad_xn, cot_masked, padded, centred, inv_std, mask, scale, gain, mixed,
            grad_conv, sums,
        )
        advance(*which)
        first = last
    store(mixed, mixed_out)
    collect_vectors(sums, in_sums, small)
    first = 0
    for last, which in (
        (5, (2,)), (10, (0, 1)), (16, (2,)), (22, (0, 1)), (27, (2,)), (33, (1,)), (39, ())
    ):
        conv_grad(first, last, padded, grad_conv, tap_sums)
        advance(*which)
        first = last
    collect_taps(tap_sums, small)
    advance(3)
    for which in (2, 1, 3, 2, 3, 2, 3):
        advance(which)
    while any(item.phase < item.phases for item in running):
        advance(2)
        advance(3)
        advance(1)
        advance(0)
    for made in copies:
        made.wait()
    for made in halves:
        made.wait_send()


def run_block(*operands):
    scratch = work_scratch()
    spaces = [pltpu.VMEM] * len(operands)
    spaces[1] = spaces[7] = spaces[9] = pl.ANY
    spaces[2] = pltpu.SMEM
    for item in plan():
        scratch += item.scratch()
    return pl.pallas_call(
        block_kernel,
        out_shape=(
            jax.ShapeDtypeStruct((ROWS, BREADTH, C), jnp.bfloat16),
            jax.ShapeDtypeStruct((CHUNKS, 2, 1536, LANES), jnp.bfloat16),
            jax.ShapeDtypeStruct((2 * LANES, LANES), jnp.float32),
        ),
        in_specs=[pl.BlockSpec(memory_space=space) for space in spaces],
        out_specs=(pl.BlockSpec(memory_space=pl.ANY),) * 3,
        scratch_shapes=scratch,
        compiler_params=pltpu.CompilerParams(
            collective_id=0, has_side_effects=True, vmem_limit_bytes=60 * 1024 * 1024
        ),
    )(*operands)


def finish_kernel(
    mixed_in, large_in, small_in, mixed, dw, dwb, ln_gain, ln_bias, w1_out, b1, w2_out, b2, scale,
    large, small, w1, w2, held, in_sems, out_sems
):
    arrive = pltpu.make_async_copy(mixed_in, held, in_sems.at[2 * CHUNKS + 1])
    leave = pltpu.make_async_copy(held, mixed, out_sems.at[2 * CHUNKS])
    little = pltpu.make_async_copy(small_in, small, in_sems.at[2 * CHUNKS])
    pieces = [(chunk, half) for chunk in range(CHUNKS) for half in range(2)]
    loads = [
        pltpu.make_async_copy(large_in.at[piece], large.at[piece], in_sems.at[index])
        for index, piece in enumerate(pieces)
    ]
    for made in [little, arrive] + loads:
        made.start()
    little.wait()

    def row(place):
        return small[place : place + 1, :]

    for group in range(GROUPS):
        for tap in range(K * K):
            dw[tap // K, tap % K : tap % K + 1, lanes(group)] = row(group * K * K + tap)
    for index, target in enumerate((b2, scale, ln_gain, ln_bias, dwb)):
        for group in range(GROUPS):
            target[lanes(group)] = row(147 + index * GROUPS + group).reshape(LANES)
    for group in range(HID // LANES):
        b1[lanes(group)] = row(162 + group).reshape(LANES)

    arrive.wait()
    leave.start()
    stores = []
    for index, (chunk, half) in enumerate(pieces):
        loads[index].wait()
        units = slice(chunk * CHUNK, (chunk + 1) * CHUNK)
        if half == 0:
            for group in range(CHUNK // LANES):
                first = chunk * CHUNK + group * LANES
                w1[:, first : first + LANES] = large[
                    chunk, 0, group * C : (group + 1) * C, :
                ].astype(jnp.float32)
            made = pltpu.make_async_copy(w1.at[:, units], w1_out.at[:, units], out_sems.at[index])
        else:
            for group in range(GROUPS):
                w2[units, lanes(group)] = large[
                    chunk, 1, group * CHUNK : (group + 1) * CHUNK, :
                ].astype(jnp.float32)
            made = pltpu.make_async_copy(w2.at[units, :], w2_out.at[units, :], out_sems.at[index])
        made.start()
        stores.append(made)
    for made in stores + [leave]:
        made.wait()


def finish(mixed, large, small):
    def f32(*shape):
        return jax.ShapeDtypeStruct(shape, jnp.float32)

    vector = f32(C)
    spaces = [pltpu.VMEM] * 10
    spaces[0] = spaces[5] = spaces[7] = pl.ANY
    return pl.pallas_call(
        finish_kernel,
        out_shape=(
            jax.ShapeDtypeStruct(mixed.shape, mixed.dtype), f32(K, K, C), vector, vector, vector,
            f32(C, HID), f32(HID), f32(HID, C), vector, vector,
        ),
        in_specs=[pl.BlockSpec(memory_space=pl.ANY)] * 3,
        out_specs=tuple(pl.BlockSpec(memory_space=space) for space in spaces),
        scratch_shapes=[
            pltpu.VMEM(large.shape, large.dtype),
            pltpu.VMEM(small.shape, small.dtype),
            pltpu.VMEM((C, HID), jnp.float32),
            pltpu.VMEM((HID, C), jnp.float32),
            pltpu.VMEM(mixed.shape, mixed.dtype),
            pltpu.SemaphoreType.DMA((2 * CHUNKS + 2,)),
            pltpu.SemaphoreType.DMA((2 * CHUNKS + 1,)),
        ],
        compiler_params=pltpu.CompilerParams(vmem_limit_bytes=60 * 1024 * 1024),
    )(mixed, large, small)


def local(
    features,
    cotangent,
    owner_slot,
    dw_weight,
    dw_bias,
    ln_gain,
    ln_bias,
    w_in,
    b_in,
    w_out,
    b_out,
    layer_scale,
):
    mixed, large, small = run_block(
        features[0],
        cotangent[0],
        owner_slot.transpose(2, 0, 1),
        dw_weight,
        dw_bias,
        ln_gain,
        ln_bias,
        w_in,
        b_in,
        w_out,
        b_out,
        layer_scale,
    )
    outs = finish(mixed, large, small)
    return (outs[0][None],) + tuple(outs[1:])


def solution(mesh):
    placed = (
        P("slide", "tile", None, None),
        P("slide", "tile", None, None),
        P("slide", None, None),
        P(),
        P(),
        P(),
        P(),
        P(),
        P(),
        P(),
        P(),
        P(),
    )
    return jax.shard_map(
        local,
        mesh=mesh,
        in_specs=placed,
        out_specs=(P("slide", "tile", None, None), P(), P(), P(), P(), P(), P(), P(), P(), P()),
        check_vma=False,
    )
```

```python
import math

import jax
import jax.numpy as jnp
from jax import lax
from jax.experimental import pallas as pl
from jax.experimental.pallas import tpu as pltpu
from jax.sharding import PartitionSpec as P

C = 384
HID = 1536
K = 7
TP = 7
COLS = 14
OWN = 16
ROWS = 14
BREADTH = 98
WIDE = 104
CELLS = ROWS * WIDE
PADDED = 1536
REACH = 3
CHUNK = 512
CHUNKS = HID // CHUNK
PAIR = 2 * WIDE
BLOCKS = CELLS // PAIR
NORM_ROWS = 112
STRIP = 16
GROUPS = C // 128
LOSS_SCALE = 1.0 / math.sqrt(8 * 32 * OWN * TP * TP)

CORES = 2
SIZES = {"x": 4, "y": 4, "z": 8}
LANES = 128
MESH = pl.DeviceIdType.MESH


def coordinates():
    tile = lax.axis_index("tile")
    return {
        "z": lax.axis_index("slide"),
        "y": tile // 8,
        "x": (tile // 2) % 4,
        "core": tile % 2,
    }


def device_at(where):
    return (where["z"], where["y"] * 8 + where["x"] * 2 + where["core"])


def peer_along(where, axis, distance):
    size = SIZES[axis]
    position = (where[axis] + distance) % size
    return position, device_at({**where, axis: position})


def stack_peer(where, distance):
    place = (where["z"] * 2 + where["core"] + distance) % 16
    return place, device_at({**where, "z": place // 2, "core": place % 2})


def plane_peer(where, distance):
    place = (where["y"] * 4 + where["x"] + distance) % 16
    return place, device_at({**where, "y": place // 4, "x": place % 4})


def enter(where):
    tile = lax.axis_index("tile")
    peers = [(where["z"], (tile + step) % 32) for step in (1, 31)]
    for step in range(1, 16):
        peers += [stack_peer(where, step)[1], plane_peer(where, step)[1]]
    barrier = pltpu.get_barrier_semaphore()
    for peer in peers:
        pl.semaphore_signal(barrier, inc=1, device_id=peer, device_id_type=MESH)
    return barrier, len(peers)


class Sum:
    def __init__(self, rows, dtype, scatter, exchange):
        self.rows, self.dtype = rows, dtype
        self.scatter, self.exchange = scatter, exchange
        self.heights = [rows]
        for axis in scatter:
            self.heights.append(self.heights[-1] // SIZES[axis])
        self.phases = 2 * len(scatter) + len(exchange) + 3

    def scratch(self):
        shapes = [pltpu.VMEM((self.rows, LANES), jnp.float32)]
        for axis, before, after in zip(self.scatter, self.heights, self.heights[1:]):
            shapes.append(pltpu.VMEM((before, LANES), jnp.float32))
            shapes.append(pltpu.VMEM((before, LANES), self.dtype))
            shapes.append(pltpu.VMEM((SIZES[axis] - 1, after, LANES), self.dtype))
        for axis in self.exchange:
            shapes.append(pltpu.VMEM((SIZES[axis], self.heights[-1], LANES), self.dtype))
        shapes.append(pltpu.SemaphoreType.DMA((self.phases,)))
        shapes.append(pltpu.SemaphoreType.DMA((self.phases,)))
        return shapes

    def bind(self, where, keep, send, result, refs):
        refs = list(refs)
        self.where, self.keep, self.send, self.result = where, keep, send, result
        self.landed = refs.pop(0)
        self.levels = [tuple(refs.pop(0) for _ in range(3)) for _ in self.scatter]
        self.slots = [refs.pop(0) for _ in self.exchange]
        self.send_sems, self.recv_sems = refs
        self.flying = []
        self.done = []
        self.phase = 0
        offset = 0
        self.offsets = [offset]
        for axis, height in zip(self.scatter, self.heights[1:]):
            offset = offset + where[axis] * height
            self.offsets.append(offset)
        return self

    def copy(self, source, target, device, start=True):
        made = pltpu.make_async_remote_copy(
            src_ref=source,
            dst_ref=target,
            send_sem=self.send_sems.at[self.phase],
            recv_sem=self.recv_sems.at[self.phase],
            device_id=device,
            device_id_type=MESH,
        )
        if start:
            made.start()
        return made

    def fly(self, everything, device):
        self.flying.append(self.copy(everything, everything, device, start=False))

    def land(self):
        for made in self.flying:
            made.wait_recv()
        self.done += self.flying
        self.flying = []

    def rows_at(self, level):
        return pl.ds(pl.multiple_of(self.offsets[level], 16), self.heights[level])

    def start_core(self):
        other = device_at({**self.where, "core": 1 - self.where["core"]})
        self.copy(self.send, self.landed, other)
        self.fly(self.landed, other)

    def start_scatter(self, index, total):
        axis, height = self.scatter[index], self.heights[index + 1]
        held, outgoing, incoming = self.levels[index]
        held[...] = total
        outgoing[...] = total.astype(self.dtype)
        for step in range(1, SIZES[axis]):
            position, device = peer_along(self.where, axis, step)
            self.copy(
                outgoing.at[pl.ds(pl.multiple_of(position * height, 16), height), :],
                incoming.at[step - 1],
                device,
            )
        self.fly(incoming, device)

    def finish_scatter(self, index):
        axis, height = self.scatter[index], self.heights[index + 1]
        held, _, incoming = self.levels[index]
        total = held[pl.ds(pl.multiple_of(self.where[axis] * height, 16), height), :]
        for step in range(SIZES[axis] - 1):
            total = total + incoming[step].astype(jnp.float32)
        return total

    def start_exchange(self, index, total):
        axis, slots = self.exchange[index], self.slots[index]
        me = self.where[axis]
        slots[me] = total.astype(self.dtype)
        for step in range(1, SIZES[axis]):
            _, device = peer_along(self.where, axis, step)
            self.copy(slots.at[me], slots.at[me], device)
        self.fly(slots.at[pl.ds(0, SIZES[axis] - 1)], device)

    def finish_exchange(self, index):
        axis, slots = self.exchange[index], self.slots[index]
        total = slots[0].astype(jnp.float32)
        for place in range(1, SIZES[axis]):
            total = total + slots[place].astype(jnp.float32)
        return total

    def start_gather(self, index):
        axis, core = self.scatter[index], self.where["core"]
        block = self.result.at[core, self.rows_at(index + 1), :]
        for step in range(1, SIZES[axis]):
            _, device = peer_along(self.where, axis, step)
            self.copy(block, block, device)
        count = (SIZES[axis] - 1) * self.heights[index + 1]
        self.fly(self.result.at[core, pl.ds(0, count), :], device)

    def advance(self):
        phase, core = self.phase, self.where["core"]
        deep, wide = len(self.scatter), len(self.exchange)
        if phase >= self.phases:
            return False
        self.land()
        more = self.step(phase, deep, wide, core)
        self.phase += 1
        return more

    def step(self, phase, deep, wide, core):
        if phase == 0:
            self.start_core()
            return True
        if phase == 1:
            total = self.keep[...] + self.landed[...]
            self.start_scatter(0, total)
            return True
        if phase <= deep + wide:
            if phase <= deep:
                total = self.finish_scatter(phase - 2)
                self.start_scatter(phase - 1, total)
                return True
            index = phase - deep - 1
            total = self.finish_scatter(deep - 1) if index == 0 else self.finish_exchange(index - 1)
            self.start_exchange(index, total)
            return True
        step = phase - deep - wide - 1
        if step == 0:
            total = self.finish_exchange(wide - 1)
            self.result[core, self.rows_at(deep), :] = total.astype(self.dtype)
        if step < deep:
            self.start_gather(deep - 1 - step)
            return True
        if step == deep:
            other = device_at({**self.where, "core": 1 - core})
            self.copy(self.result.at[core], self.result.at[core], other)
            self.fly(self.result.at[core], other)
            return True
        for made in self.done:
            made.wait_send()
        return False


class Spread:
    ROWS = 16
    phases = 4

    def scratch(self):
        return [
            pltpu.VMEM((15, self.ROWS, LANES), jnp.float32),
            pltpu.VMEM((16, self.ROWS, LANES), jnp.float32),
            pltpu.SemaphoreType.DMA((3,)),
            pltpu.SemaphoreType.DMA((3,)),
        ]

    def bind(self, where, source, result, refs):
        self.where, self.source, self.result = where, source, result
        self.landed, self.slots, self.send_sems, self.recv_sems = refs
        self.phase = 0
        self.flying, self.done = [], []
        return self

    copy = Sum.copy
    fly = Sum.fly
    land = Sum.land

    def advance(self):
        phase, where, rows = self.phase, self.where, self.ROWS
        if phase >= self.phases:
            return False
        self.land()
        more = self.step(phase, where, rows)
        self.phase += 1
        return more

    def step(self, phase, where, rows):
        place, flat = where["z"] * 2 + where["core"], where["y"] * 4 + where["x"]
        mine = pl.ds(pl.multiple_of(place * rows, rows), rows)
        if phase == 0:
            for step in range(1, 16):
                other, device = stack_peer(where, step)
                block = self.source.at[pl.ds(pl.multiple_of(other * rows, rows), rows), :]
                self.copy(block, self.landed.at[step - 1], device)
            self.fly(self.landed, device)
        elif phase == 1:
            total = self.source[mine, :]
            for step in range(15):
                total = total + self.landed[step]
            self.slots[flat] = total
            for step in range(1, 16):
                _, device = plane_peer(where, step)
                self.copy(self.slots.at[flat], self.slots.at[flat], device)
            self.fly(self.slots.at[pl.ds(0, 15)], device)
        elif phase == 2:
            total = self.slots[0]
            for index in range(1, 16):
                total = total + self.slots[index]
            self.result[mine, :] = total
            block = self.result.at[mine, :]
            for step in range(1, 16):
                _, device = stack_peer(where, step)
                self.copy(block, block, device)
            self.fly(self.result.at[pl.ds(0, 15 * rows), :], device)
        else:
            for made in self.done:
                made.wait_send()
            return False
        return True


def lanes(group):
    return slice(group * LANES, (group + 1) * LANES)


def line(vector, group):
    return vector[lanes(group)].reshape(1, LANES)


def by_eight(value):
    return jnp.sum(value.reshape(-1, 8, LANES), axis=0)


def gelu_parts(pre_act):
    density = jnp.exp(-0.5 * pre_act * pre_act) * 0.3989422804014327
    t = pl.reciprocal(1.0 + 0.2316419 * jnp.abs(pre_act), approx=False)
    series = 1.781477937 + t * (-1.821255978 + t * 1.330274429)
    series = t * (0.319381530 + t * (-0.356563782 + t * series))
    tail = density * series
    mass = jnp.where(pre_act >= 0.0, 1.0 - tail, tail)
    return pre_act * mass, mass + pre_act * density


def spread_tissue(table, mask):
    tile = lax.axis_index("tile")
    mask[:, 96:WIDE, :] = jnp.zeros((4, WIDE - 96, LANES), jnp.float32)
    for place in range(4):
        row = jnp.clip(2 * tile - 1 + place, 0, 63)
        inside = 1.0
        if place == 0:
            inside = jnp.where(tile > 0, 1.0, 0.0)
        if place == 3:
            inside = jnp.where(tile < 31, 1.0, 0.0)
        for column in range(COLS):
            live = jnp.where(table[column, 0, row] >= 0, 1.0, 0.0) * inside
            mask[place, column * TP : (column + 1) * TP, :] = jnp.full((TP, LANES), live, jnp.float32)


def fill(feat, cot, mask, padded, cot_masked):
    edge = jnp.zeros((3, ROWS + 2 * REACH, 8, LANES), jnp.float32)
    padded[:, :, 0:8, :] = edge
    padded[:, :, 104:112, :] = edge
    padded[:, :, 112:120, :] = edge

    def row(i, carry):
        live = mask[1 + i // TP][:BREADTH]
        cells = feat[i].astype(jnp.float32)
        pull = cot[i].astype(jnp.float32)
        for group in range(GROUPS):
            padded[group, i + REACH, 8 : 8 + BREADTH, :] = cells[:, lanes(group)] * live
            end = pl.ds(pl.multiple_of(i * WIDE + WIDE - 8, 8), 8)
            cot_masked[group, end, :] = jnp.zeros((8, LANES), jnp.float32)
            place = pl.ds(pl.multiple_of(i * WIDE, 8), BREADTH)
            cot_masked[group, place, :] = pull[:, lanes(group)] * live
        return carry

    lax.fori_loop(0, ROWS, row, 0)


def fill_halo(halo, mask, padded):
    def row(i, carry):
        for side in range(2):
            live = mask[3 * side][:BREADTH]
            cells = halo[side, i].astype(jnp.float32)
            for group in range(GROUPS):
                padded[group, i + side * (ROWS + REACH), 8 : 8 + BREADTH, :] = (
                    cells[:, lanes(group)] * live
                )
        return carry

    lax.fori_loop(0, REACH, row, 0)


def spread_taps(weight, taps, bias, bias_rows):
    for group in range(GROUPS):
        bias_rows[group] = jnp.broadcast_to(line(bias, group), (8, LANES))
    for tap in range(K * K):
        for group in range(GROUPS):
            taps[group, tap] = jnp.broadcast_to(weight[tap // K, tap % K : tap % K + 1, lanes(group)], (8, LANES))


def conv(padded, taps, bias_rows, conv_out):
    def tile(step, carry):
        group, column = step // 13, step % 13
        total = jnp.zeros((ROWS, 8, LANES), jnp.float32) + bias_rows[group]
        for col_tap in range(K):
            window = padded[group, :, pl.ds(8 * column + 5 + col_tap, 8), :]
            for row_tap in range(K):
                total = total + window[row_tap : row_tap + ROWS] * taps[group, row_tap * K + col_tap]
        for i in range(ROWS):
            conv_out[group, pl.ds(pl.multiple_of(i * WIDE + 8 * column, 8), 8), :] = total[i]
        return carry

    lax.fori_loop(0, GROUPS * 13, tile, 0)


def conv_grad(first, last, padded, grad_conv, tap_sums):
    def unit(step, carry):
        group, col_tap = step // K, step % K
        totals = [jnp.zeros((8, LANES), jnp.float32)] * K
        for column in range(13):
            pull = jnp.stack(
                [
                    grad_conv[group, i * WIDE + 8 * column : i * WIDE + 8 * column + 8, :]
                    for i in range(ROWS)
                ]
            )
            window = padded[group, :, pl.ds(8 * column + 5 + col_tap, 8), :]
            for row_tap in range(K):
                totals[row_tap] = totals[row_tap] + jnp.sum(
                    window[row_tap : row_tap + ROWS] * pull, axis=0
                )
        for row_tap in range(K):
            tap_sums[group, row_tap * K + col_tap] = totals[row_tap]
        return carry

    lax.fori_loop(first, last, unit, 0)


def norm(conv_out, inv_std, gain, offset, normed):
    def block(step, carry):
        place = pl.ds(pl.multiple_of(step * NORM_ROWS, 16), NORM_ROWS)
        held = [conv_out[group, place, :] for group in range(GROUPS)]
        mean = jnp.sum(held[0] + held[1] + held[2], axis=-1, keepdims=True) * (1.0 / C)
        held = [item - mean for item in held]
        squares = held[0] * held[0] + held[1] * held[1] + held[2] * held[2]
        var = jnp.sum(squares, axis=-1, keepdims=True) * (1.0 / C)
        inv = jnp.broadcast_to(lax.rsqrt(var + 1e-06), (NORM_ROWS, LANES))
        inv_std[place, :] = inv
        for group in range(GROUPS):
            centred = held[group] * inv
            conv_out[group, place, :] = centred
            normed[place, lanes(group)] = (
                centred * line(gain, group) + line(offset, group)
            ).astype(jnp.bfloat16)
        return carry

    lax.fori_loop(0, CELLS // NORM_ROWS, block, 0)


def branch_grad(cot_masked, scale, grad_branch, sums):
    def block(step, carry):
        place = pl.ds(pl.multiple_of(step * NORM_ROWS, 16), NORM_ROWS)
        for group in range(GROUPS):
            pull = cot_masked[group, place, :] * (line(scale, group) * LOSS_SCALE)
            grad_branch[place, lanes(group)] = pull.astype(jnp.bfloat16)
            sums[group] += by_eight(pull)
        return carry

    lax.fori_loop(0, CELLS // NORM_ROWS, block, 0)


def turn(rows, turned):
    def block(step, carry):
        place = pl.ds(pl.multiple_of(step * LANES, LANES), LANES)
        turned[:, place] = rows[place, :].T
        return carry

    lax.fori_loop(0, PADDED // LANES, block, 0)


def nt(left, right):
    return lax.dot_general(
        left, right, (((1,), (1,)), ((), ())), preferred_element_type=jnp.float32
    )


def rows_of(block):
    return slice(block * PAIR, (block + 1) * PAIR)


def mlp_enter(chunk, block, normed, grad_branch, w_in, w_out, pre_act, pull):
    units = slice(chunk * CHUNK, (chunk + 1) * CHUNK)
    place = rows_of(block)
    pre_act[...] = jnp.dot(normed[place, :], w_in[:, units], preferred_element_type=jnp.float32)
    pull[...] = nt(grad_branch[place, :], w_out[units, :])


def mlp_strips(chunk, block, b_in, pre_act, pull, hidden, grad_pre, in_sums):
    units = slice(chunk * CHUNK, (chunk + 1) * CHUNK)
    bias = b_in[units].reshape(1, CHUNK)
    total = in_sums[:, units]
    for first in range(0, PAIR, STRIP):
        strip = slice(first, first + STRIP)
        place = slice(block * PAIR + first, block * PAIR + first + STRIP)
        activ, slope = gelu_parts(pre_act[strip, :] + bias)
        hidden[place, :] = activ.astype(jnp.bfloat16)
        back = pull[strip, :] * slope
        total = total + back[:8] + back[8:]
        grad_pre[place, :] = back.astype(jnp.bfloat16)
    in_sums[:, units] = total


def mlp_leave(chunk, block, hidden, grad_pre, w_in, w_out, b_out, branch, grad_xn):
    units = slice(chunk * CHUNK, (chunk + 1) * CHUNK)
    place = rows_of(block)
    out = jnp.dot(hidden[place, :], w_out[units, :], preferred_element_type=jnp.float32)
    back = nt(grad_pre[place, :], w_in[:, units])
    if chunk == 0:
        branch[place, :] = out + b_out[...].reshape(1, C)
        grad_xn[place, :] = back
    else:
        branch[place, :] += out
        grad_xn[place, :] += back


def weight_grads(chunk, normed_t, grad_branch_t, hidden, grad_pre, large):
    first = jnp.dot(normed_t[...], grad_pre[...], preferred_element_type=jnp.float32)
    for group in range(CHUNK // LANES):
        large[chunk, 0, group * C : (group + 1) * C, :] = first[:, lanes(group)]
    second = jnp.dot(grad_branch_t[...], hidden[...], preferred_element_type=jnp.float32).T
    for group in range(GROUPS):
        large[chunk, 1, group * CHUNK : (group + 1) * CHUNK, :] = second[:, lanes(group)]


def after_mlp(first, last, branch, grad_xn, cot_masked, padded, centred, inv_std, mask, scale, gain, mixed, grad_conv, sums):
    def part(i, start, size, totals):
        totals = list(totals)
        place = pl.ds(pl.multiple_of(i * WIDE + start, 8), size)
        live = mask[1 + i // TP, start : start + size]
        used = min(BREADTH - start, size)
        kept = []
        for group in range(GROUPS):
            out = branch[place, lanes(group)].astype(jnp.bfloat16).astype(jnp.float32)
            totals[group] = totals[group] + by_eight(cot_masked[group, place, :] * out)
            cells = padded[group, i + REACH, 8 + start : 8 + start + size, :]
            cells = cells + live * (line(scale, group) * out)
            kept.append(cells[:used].astype(jnp.bfloat16))
        pulls, held = [], []
        for group in range(GROUPS):
            pull = grad_xn[place, lanes(group)].astype(jnp.bfloat16).astype(jnp.float32)
            cen = centred[group, place, :]
            totals[3 + group] = totals[3 + group] + by_eight(pull * cen)
            totals[6 + group] = totals[6 + group] + by_eight(pull)
            pulls.append(pull * line(gain, group))
            held.append(cen)
        mean = jnp.sum(pulls[0] + pulls[1] + pulls[2], axis=-1, keepdims=True) * (1.0 / C)
        along = pulls[0] * held[0] + pulls[1] * held[1] + pulls[2] * held[2]
        along = jnp.sum(along, axis=-1, keepdims=True) * (1.0 / C)
        inv = inv_std[place, :]
        for group in range(GROUPS):
            pulls[group] = inv * (pulls[group] - mean - held[group] * along)
            totals[9 + group] = totals[9 + group] + by_eight(pulls[group])
        for group in range(GROUPS):
            mixed[i, start : start + used, lanes(group)] = kept[group]
            grad_conv[group, place, :] = pulls[group]
        return tuple(totals)

    def row(i, totals):
        return part(i, 48, 56, part(i, 0, 48, totals))

    totals = lax.fori_loop(first, last, row, tuple(sums[3 + index] for index in range(12)))
    for index in range(12):
        sums[3 + index] = totals[index]


def put(small, place, value):
    small[place : place + 1, :] = jnp.sum(value, axis=0, keepdims=True)


def collect_vectors(sums, in_sums, small):
    small[168:, :] = jnp.zeros((2 * LANES - 168, LANES), jnp.float32)
    for index in range(15):
        value = sums[index]
        put(small, 147 + index, value * LOSS_SCALE if 3 <= index < 6 else value)
    for group in range(HID // LANES):
        put(small, 162 + group, in_sums[:, lanes(group)])


def collect_taps(tap_sums, small):
    for group in range(GROUPS):
        for tap in range(K * K):
            put(small, group * K * K + tap, tap_sums[group, tap])


X_FIRST, Y_FIRST = (("x", "z"), ("y",)), (("y", "z"), ("x",))
PIECES = (
    (0, 0, 1024, X_FIRST),
    (0, 1024, 512, Y_FIRST),
    (1, 0, 1024, Y_FIRST),
    (1, 1024, 512, X_FIRST),
    (2, 0, 1024, X_FIRST),
    (2, 1024, 512, Y_FIRST),
)


def plan():
    return [Sum(rows, jnp.bfloat16, *order) for _, _, rows, order in PIECES] + [Spread()]


def work_scratch():
    def f32(*shape):
        return pltpu.VMEM(shape, jnp.float32)

    def b16(*shape):
        return pltpu.VMEM(shape, jnp.bfloat16)

    return [
        b16(2, REACH, BREADTH, C),
        pltpu.SemaphoreType.DMA((2,)),
        pltpu.SemaphoreType.DMA((2,)),
        f32(GROUPS, ROWS + 2 * REACH, 120, LANES),
        f32(GROUPS, CELLS, LANES),
        f32(GROUPS, K * K, 8, LANES),
        f32(GROUPS, CELLS, LANES),
        f32(CELLS, LANES),
        b16(PADDED, C),
        b16(PADDED, C),
        b16(C, PADDED),
        b16(C, PADDED),
        b16(2, PADDED, CHUNK),
        b16(2, PADDED, CHUNK),
        f32(CELLS, C),
        f32(CELLS, C),
        f32(8, HID),
        f32(15, 8, LANES),
        f32(GROUPS, K * K, 8, LANES),
        f32(GROUPS, CELLS, LANES),
        f32(CHUNKS, 2, 1536, LANES),
        f32(2 * LANES, LANES),
        b16(CHUNKS, 2, 1536, LANES),
        f32(2 * LANES, LANES),
        b16(ROWS, BREADTH, C),
        pltpu.SemaphoreType.DMA((len(PIECES) + 2,)),
        f32(4, WIDE, LANES),
        f32(GROUPS, 8, LANES),
        b16(ROWS, BREADTH, C),
        b16(C, HID),
        b16(HID, C),
        pltpu.SemaphoreType.DMA((3,)),
        f32(2, PAIR, CHUNK),
        f32(2, PAIR, CHUNK),
    ]


def block_kernel(
    feat, cot_in, table, dw_weight, dw_bias, gain, offset, w_in_in, b_in, w_out_in, b_out, scale,
    mixed_out, large_out, small_out, *refs
):
    refs = list(refs)
    own = len(work_scratch())
    (
        halo, halo_send, halo_recv, padded, cot_masked, taps, centred, inv_std, normed, grad_branch,
        normed_t, grad_branch_t, hidden, grad_pre, branch, grad_xn, in_sums, sums, tap_sums,
        grad_conv, large, small, large_held, small_held, mixed, out_sems,
        mask, bias_rows, cot, w_in, w_out, in_sems, pre_act, pull,
    ) = refs[:own]
    refs = refs[own:]
    where = coordinates()
    core, tile = where["core"], lax.axis_index("tile")
    loads = [
        pltpu.make_async_copy(source, target, in_sems.at[index])
        for index, (source, target) in enumerate(((cot_in, cot), (w_in_in, w_in), (w_out_in, w_out)))
    ]
    for made in loads:
        made.start()
    greeting = enter(where)
    spread_tissue(table, mask)
    spread_taps(dw_weight, taps, dw_bias, bias_rows)
    pl.semaphore_wait(*greeting)
    halves = []
    for side, step, first in ((0, 1, ROWS - REACH), (1, 31, 0)):
        made = pltpu.make_async_remote_copy(
            src_ref=feat.at[pl.ds(first, REACH)],
            dst_ref=halo.at[side],
            send_sem=halo_send.at[side],
            recv_sem=halo_recv.at[side],
            device_id=(where["z"], (tile + step) % 32),
            device_id_type=MESH,
        )
        made.start()
        halves.append(made)
    running = []
    for index, item in enumerate(plan()):
        count = len(item.scratch())
        mine, refs = refs[:count], refs[count:]
        if index < len(PIECES):
            chunk, start, rows, _ = PIECES[index]
            span = pl.ds(start, rows)
            keep, send = large.at[chunk, core, span, :], large.at[chunk, 1 - core, span, :]
            item.bind(where, keep, send, large_held.at[chunk, :, span, :], mine)
        else:
            item.bind(where, small, small_held, mine)
        running.append(item)

    copies = []

    def store(source, target):
        made = pltpu.make_async_copy(source, target, out_sems.at[len(copies)])
        made.start()
        copies.append(made)

    def advance(*which):
        for index, item in enumerate(running):
            chunk = PIECES[index][0] if index < len(PIECES) else CHUNKS
            before = item.phase
            if chunk in which and not item.advance() and item.phase > before:
                if chunk < CHUNKS:
                    _, start, rows, _ = PIECES[index]
                    span = pl.ds(start, rows)
                    store(large_held.at[chunk, :, span, :], large_out.at[chunk, :, span, :])
                else:
                    store(small_held, small_out)

    sums[...] = jnp.zeros(sums.shape, jnp.float32)
    in_sums[...] = jnp.zeros(in_sums.shape, jnp.float32)
    for rows in (normed, grad_branch, hidden.at[0], hidden.at[1], grad_pre.at[0], grad_pre.at[1]):
        rows[CELLS:, :] = jnp.zeros((PADDED - CELLS, rows.shape[1]), jnp.bfloat16)
    loads[0].wait()
    fill(feat, cot, mask, padded, cot_masked)
    branch_grad(cot_masked, scale, grad_branch, sums)
    turn(grad_branch, grad_branch_t)
    for made in halves:
        made.wait_recv()
    fill_halo(halo, mask, padded)
    conv(padded, taps, bias_rows, centred)
    norm(centred, inv_std, gain, offset, normed)
    turn(normed, normed_t)
    loads[1].wait()
    loads[2].wait()

    steps = [(chunk, block) for chunk in range(CHUNKS) for block in range(BLOCKS)]

    def enter_step(place):
        if place < len(steps):
            chunk, block = steps[place]
            side = place % 2
            mlp_enter(
                chunk, block, normed, grad_branch, w_in, w_out, pre_act.at[side], pull.at[side]
            )

    def leave_step(place):
        chunk, block = steps[place]
        half = chunk % 2
        mlp_leave(
            chunk, block, hidden.at[half], grad_pre.at[half], w_in, w_out, b_out, branch, grad_xn
        )

    def finish_chunk(chunk):
        half = chunk % 2
        weight_grads(chunk, normed_t, grad_branch_t, hidden.at[half], grad_pre.at[half], large)

    after_block = {(1, 0): (0,), (1, 4): (0,), (2, 0): (1,), (2, 3): (0,), (2, 4): (1,)}
    enter_step(0)
    for place, (chunk, block) in enumerate(steps):
        half, side = chunk % 2, place % 2
        enter_step(place + 1)
        mlp_strips(
            chunk, block, b_in, pre_act.at[side], pull.at[side], hidden.at[half], grad_pre.at[half],
            in_sums,
        )
        if place > 0:
            leave_step(place - 1)
        if block == 0 and chunk > 0:
            finish_chunk(chunk - 1)
        advance(*after_block.get((chunk, block), ()))
    leave_step(len(steps) - 1)
    finish_chunk(CHUNKS - 1)
    advance(2)
    advance(0)
    first = 0
    for last, which in ((8, (0,)), (14, (2, 1))):
        after_mlp(
            first, last, branch, grad_xn, cot_masked, padded, centred, inv_std, mask, scale, gain, mixed,
            grad_conv, sums,
        )
        for chunk in which:
            advance(chunk)
        first = last
    store(mixed, mixed_out)
    collect_vectors(sums, in_sums, small)
    first = 0
    for last, which in ((7, (0,)), (14, (2, 1)), (21, (2,))):
        conv_grad(first, last, padded, grad_conv, tap_sums)
        for chunk in which:
            advance(chunk)
        first = last
    collect_taps(tap_sums, small)
    for chunk in (3, 2, 1, 3, 0, 2, 1, 3, 1, 2, 3):
        advance(chunk)
    while any(item.phase < item.phases for item in running):
        advance(2)
        advance(3)
        advance(1)
        advance(0)
    for made in copies:
        made.wait()
    for made in halves:
        made.wait_send()


def run_block(*operands):
    scratch = work_scratch()
    spaces = [pltpu.VMEM] * len(operands)
    spaces[1] = spaces[7] = spaces[9] = pl.ANY
    spaces[2] = pltpu.SMEM
    for item in plan():
        scratch += item.scratch()
    return pl.pallas_call(
        block_kernel,
        out_shape=(
            jax.ShapeDtypeStruct((ROWS, BREADTH, C), jnp.bfloat16),
            jax.ShapeDtypeStruct((CHUNKS, 2, 1536, LANES), jnp.bfloat16),
            jax.ShapeDtypeStruct((2 * LANES, LANES), jnp.float32),
        ),
        in_specs=[pl.BlockSpec(memory_space=space) for space in spaces],
        out_specs=(pl.BlockSpec(memory_space=pl.ANY),) * 3,
        scratch_shapes=scratch,
        compiler_params=pltpu.CompilerParams(
            collective_id=0, has_side_effects=True, vmem_limit_bytes=60 * 1024 * 1024
        ),
    )(*operands)


def finish_kernel(
    mixed_in, large_in, small_in, mixed, dw, dwb, ln_gain, ln_bias, w1_out, b1, w2_out, b2, scale,
    large, small, w1, w2, held, in_sems, out_sems
):
    arrive = pltpu.make_async_copy(mixed_in, held, in_sems.at[2 * CHUNKS + 1])
    leave = pltpu.make_async_copy(held, mixed, out_sems.at[2 * CHUNKS])
    little = pltpu.make_async_copy(small_in, small, in_sems.at[2 * CHUNKS])
    pieces = [(chunk, half) for chunk in range(CHUNKS) for half in range(2)]
    loads = [
        pltpu.make_async_copy(large_in.at[piece], large.at[piece], in_sems.at[index])
        for index, piece in enumerate(pieces)
    ]
    for made in [little, arrive] + loads:
        made.start()
    little.wait()

    def row(place):
        return small[place : place + 1, :]

    for group in range(GROUPS):
        for tap in range(K * K):
            dw[tap // K, tap % K : tap % K + 1, lanes(group)] = row(group * K * K + tap)
    for index, target in enumerate((b2, scale, ln_gain, ln_bias, dwb)):
        for group in range(GROUPS):
            target[lanes(group)] = row(147 + index * GROUPS + group).reshape(LANES)
    for group in range(HID // LANES):
        b1[lanes(group)] = row(162 + group).reshape(LANES)

    arrive.wait()
    leave.start()
    stores = []
    for index, (chunk, half) in enumerate(pieces):
        loads[index].wait()
        units = slice(chunk * CHUNK, (chunk + 1) * CHUNK)
        if half == 0:
            for group in range(CHUNK // LANES):
                first = chunk * CHUNK + group * LANES
                w1[:, first : first + LANES] = large[
                    chunk, 0, group * C : (group + 1) * C, :
                ].astype(jnp.float32)
            made = pltpu.make_async_copy(w1.at[:, units], w1_out.at[:, units], out_sems.at[index])
        else:
            for group in range(GROUPS):
                w2[units, lanes(group)] = large[
                    chunk, 1, group * CHUNK : (group + 1) * CHUNK, :
                ].astype(jnp.float32)
            made = pltpu.make_async_copy(w2.at[units, :], w2_out.at[units, :], out_sems.at[index])
        made.start()
        stores.append(made)
    for made in stores + [leave]:
        made.wait()


def finish(mixed, large, small):
    def f32(*shape):
        return jax.ShapeDtypeStruct(shape, jnp.float32)

    vector = f32(C)
    spaces = [pltpu.VMEM] * 10
    spaces[0] = spaces[5] = spaces[7] = pl.ANY
    return pl.pallas_call(
        finish_kernel,
        out_shape=(
            jax.ShapeDtypeStruct(mixed.shape, mixed.dtype), f32(K, K, C), vector, vector, vector,
            f32(C, HID), f32(HID), f32(HID, C), vector, vector,
        ),
        in_specs=[pl.BlockSpec(memory_space=pl.ANY)] * 3,
        out_specs=tuple(pl.BlockSpec(memory_space=space) for space in spaces),
        scratch_shapes=[
            pltpu.VMEM(large.shape, large.dtype),
            pltpu.VMEM(small.shape, small.dtype),
            pltpu.VMEM((C, HID), jnp.float32),
            pltpu.VMEM((HID, C), jnp.float32),
            pltpu.VMEM(mixed.shape, mixed.dtype),
            pltpu.SemaphoreType.DMA((2 * CHUNKS + 2,)),
            pltpu.SemaphoreType.DMA((2 * CHUNKS + 1,)),
        ],
        compiler_params=pltpu.CompilerParams(vmem_limit_bytes=60 * 1024 * 1024),
    )(mixed, large, small)


def local(
    features,
    cotangent,
    owner_slot,
    dw_weight,
    dw_bias,
    ln_gain,
    ln_bias,
    w_in,
    b_in,
    w_out,
    b_out,
    layer_scale,
):
    mixed, large, small = run_block(
        features[0],
        cotangent[0],
        owner_slot.transpose(2, 0, 1),
        dw_weight,
        dw_bias,
        ln_gain,
        ln_bias,
        w_in,
        b_in,
        w_out,
        b_out,
        layer_scale,
    )
    outs = finish(mixed, large, small)
    return (outs[0][None],) + tuple(outs[1:])


def solution(mesh):
    placed = (
        P("slide", "tile", None, None),
        P("slide", "tile", None, None),
        P("slide", None, None),
        P(),
        P(),
        P(),
        P(),
        P(),
        P(),
        P(),
        P(),
        P(),
    )
    return jax.shard_map(
        local,
        mesh=mesh,
        in_specs=placed,
        out_specs=(P("slide", "tile", None, None), P(), P(), P(), P(), P(), P(), P(), P(), P()),
        check_vma=False,
    )
```

```python
import math

import jax
import jax.numpy as jnp
from jax import lax
from jax.experimental import pallas as pl
from jax.experimental.pallas import tpu as pltpu
from jax.sharding import PartitionSpec as P

C = 384
HID = 1536
K = 7
TP = 7
COLS = 14
OWN = 16
ROWS = 14
BREADTH = 98
WIDE = 104
CELLS = ROWS * WIDE
PADDED = 1536
REACH = 3
CHUNK = 512
CHUNKS = HID // CHUNK
PAIR = 2 * WIDE
BLOCKS = CELLS // PAIR
NORM_ROWS = 112
STRIP = 16
GROUPS = C // 128
LOSS_SCALE = 1.0 / math.sqrt(8 * 32 * OWN * TP * TP)

CORES = 2
SIZES = {"x": 4, "y": 4, "z": 8}
LANES = 128
MESH = pl.DeviceIdType.MESH


def coordinates():
    tile = lax.axis_index("tile")
    return {
        "z": lax.axis_index("slide"),
        "y": tile // 8,
        "x": (tile // 2) % 4,
        "core": tile % 2,
    }


def device_at(where):
    return (where["z"], where["y"] * 8 + where["x"] * 2 + where["core"])


def peer_along(where, axis, distance):
    size = SIZES[axis]
    position = (where[axis] + distance) % size
    return position, device_at({**where, axis: position})


def stack_peer(where, distance):
    place = (where["z"] * 2 + where["core"] + distance) % 16
    return place, device_at({**where, "z": place // 2, "core": place % 2})


def plane_peer(where, distance):
    place = (where["y"] * 4 + where["x"] + distance) % 16
    return place, device_at({**where, "y": place // 4, "x": place % 4})


def enter(where):
    tile = lax.axis_index("tile")
    peers = [(where["z"], (tile + step) % 32) for step in (1, 31)]
    for step in range(1, 16):
        peers += [stack_peer(where, step)[1], plane_peer(where, step)[1]]
    barrier = pltpu.get_barrier_semaphore()
    for peer in peers:
        pl.semaphore_signal(barrier, inc=1, device_id=peer, device_id_type=MESH)
    return barrier, len(peers)


class Sum:
    def __init__(self, rows, dtype, scatter, exchange):
        self.rows, self.dtype = rows, dtype
        self.scatter, self.exchange = scatter, exchange
        self.heights = [rows]
        for axis in scatter:
            self.heights.append(self.heights[-1] // SIZES[axis])
        self.phases = 2 * len(scatter) + len(exchange) + 3

    def scratch(self):
        shapes = [pltpu.VMEM((self.rows, LANES), jnp.float32)]
        for axis, before, after in zip(self.scatter, self.heights, self.heights[1:]):
            shapes.append(pltpu.VMEM((before, LANES), jnp.float32))
            shapes.append(pltpu.VMEM((before, LANES), self.dtype))
            shapes.append(pltpu.VMEM((SIZES[axis] - 1, after, LANES), self.dtype))
        for axis in self.exchange:
            shapes.append(pltpu.VMEM((SIZES[axis], self.heights[-1], LANES), self.dtype))
        shapes.append(pltpu.SemaphoreType.DMA((self.phases,)))
        shapes.append(pltpu.SemaphoreType.DMA((self.phases,)))
        return shapes

    def bind(self, where, keep, send, result, refs):
        refs = list(refs)
        self.where, self.keep, self.send, self.result = where, keep, send, result
        self.landed = refs.pop(0)
        self.levels = [tuple(refs.pop(0) for _ in range(3)) for _ in self.scatter]
        self.slots = [refs.pop(0) for _ in self.exchange]
        self.send_sems, self.recv_sems = refs
        self.flying = []
        self.done = []
        self.phase = 0
        offset = 0
        self.offsets = [offset]
        for axis, height in zip(self.scatter, self.heights[1:]):
            offset = offset + where[axis] * height
            self.offsets.append(offset)
        return self

    def copy(self, source, target, device, start=True):
        made = pltpu.make_async_remote_copy(
            src_ref=source,
            dst_ref=target,
            send_sem=self.send_sems.at[self.phase],
            recv_sem=self.recv_sems.at[self.phase],
            device_id=device,
            device_id_type=MESH,
        )
        if start:
            made.start()
        return made

    def fly(self, everything, device):
        self.flying.append(self.copy(everything, everything, device, start=False))

    def land(self):
        for made in self.flying:
            made.wait_recv()
        self.done += self.flying
        self.flying = []

    def rows_at(self, level):
        return pl.ds(pl.multiple_of(self.offsets[level], 16), self.heights[level])

    def start_core(self):
        other = device_at({**self.where, "core": 1 - self.where["core"]})
        self.copy(self.send, self.landed, other)
        self.fly(self.landed, other)

    def start_scatter(self, index, total):
        axis, height = self.scatter[index], self.heights[index + 1]
        held, outgoing, incoming = self.levels[index]
        held[...] = total
        outgoing[...] = total.astype(self.dtype)
        for step in range(1, SIZES[axis]):
            position, device = peer_along(self.where, axis, step)
            self.copy(
                outgoing.at[pl.ds(pl.multiple_of(position * height, 16), height), :],
                incoming.at[step - 1],
                device,
            )
        self.fly(incoming, device)

    def finish_scatter(self, index):
        axis, height = self.scatter[index], self.heights[index + 1]
        held, _, incoming = self.levels[index]
        total = held[pl.ds(pl.multiple_of(self.where[axis] * height, 16), height), :]
        for step in range(SIZES[axis] - 1):
            total = total + incoming[step].astype(jnp.float32)
        return total

    def start_exchange(self, index, total):
        axis, slots = self.exchange[index], self.slots[index]
        me = self.where[axis]
        slots[me] = total.astype(self.dtype)
        for step in range(1, SIZES[axis]):
            _, device = peer_along(self.where, axis, step)
            self.copy(slots.at[me], slots.at[me], device)
        self.fly(slots.at[pl.ds(0, SIZES[axis] - 1)], device)

    def finish_exchange(self, index):
        axis, slots = self.exchange[index], self.slots[index]
        total = slots[0].astype(jnp.float32)
        for place in range(1, SIZES[axis]):
            total = total + slots[place].astype(jnp.float32)
        return total

    def start_gather(self, index):
        axis, core = self.scatter[index], self.where["core"]
        block = self.result.at[core, self.rows_at(index + 1), :]
        for step in range(1, SIZES[axis]):
            _, device = peer_along(self.where, axis, step)
            self.copy(block, block, device)
        count = (SIZES[axis] - 1) * self.heights[index + 1]
        self.fly(self.result.at[core, pl.ds(0, count), :], device)

    def advance(self):
        phase, core = self.phase, self.where["core"]
        deep, wide = len(self.scatter), len(self.exchange)
        if phase >= self.phases:
            return False
        self.land()
        more = self.step(phase, deep, wide, core)
        self.phase += 1
        return more

    def step(self, phase, deep, wide, core):
        if phase == 0:
            self.start_core()
            return True
        if phase == 1:
            total = self.keep[...] + self.landed[...]
            self.start_scatter(0, total)
            return True
        if phase <= deep + wide:
            if phase <= deep:
                total = self.finish_scatter(phase - 2)
                self.start_scatter(phase - 1, total)
                return True
            index = phase - deep - 1
            total = self.finish_scatter(deep - 1) if index == 0 else self.finish_exchange(index - 1)
            self.start_exchange(index, total)
            return True
        step = phase - deep - wide - 1
        if step == 0:
            total = self.finish_exchange(wide - 1)
            self.result[core, self.rows_at(deep), :] = total.astype(self.dtype)
        if step < deep:
            self.start_gather(deep - 1 - step)
            return True
        if step == deep:
            other = device_at({**self.where, "core": 1 - core})
            self.copy(self.result.at[core], self.result.at[core], other)
            self.fly(self.result.at[core], other)
            return True
        for made in self.done:
            made.wait_send()
        return False


class Spread:
    ROWS = 16
    phases = 4

    def scratch(self):
        return [
            pltpu.VMEM((15, self.ROWS, LANES), jnp.float32),
            pltpu.VMEM((16, self.ROWS, LANES), jnp.float32),
            pltpu.SemaphoreType.DMA((3,)),
            pltpu.SemaphoreType.DMA((3,)),
        ]

    def bind(self, where, source, result, refs):
        self.where, self.source, self.result = where, source, result
        self.landed, self.slots, self.send_sems, self.recv_sems = refs
        self.phase = 0
        self.flying, self.done = [], []
        return self

    copy = Sum.copy
    fly = Sum.fly
    land = Sum.land

    def advance(self):
        phase, where, rows = self.phase, self.where, self.ROWS
        if phase >= self.phases:
            return False
        self.land()
        more = self.step(phase, where, rows)
        self.phase += 1
        return more

    def step(self, phase, where, rows):
        place, flat = where["z"] * 2 + where["core"], where["y"] * 4 + where["x"]
        mine = pl.ds(pl.multiple_of(place * rows, rows), rows)
        if phase == 0:
            for step in range(1, 16):
                other, device = stack_peer(where, step)
                block = self.source.at[pl.ds(pl.multiple_of(other * rows, rows), rows), :]
                self.copy(block, self.landed.at[step - 1], device)
            self.fly(self.landed, device)
        elif phase == 1:
            total = self.source[mine, :]
            for step in range(15):
                total = total + self.landed[step]
            self.slots[flat] = total
            for step in range(1, 16):
                _, device = plane_peer(where, step)
                self.copy(self.slots.at[flat], self.slots.at[flat], device)
            self.fly(self.slots.at[pl.ds(0, 15)], device)
        elif phase == 2:
            total = self.slots[0]
            for index in range(1, 16):
                total = total + self.slots[index]
            self.result[mine, :] = total
            block = self.result.at[mine, :]
            for step in range(1, 16):
                _, device = stack_peer(where, step)
                self.copy(block, block, device)
            self.fly(self.result.at[pl.ds(0, 15 * rows), :], device)
        else:
            for made in self.done:
                made.wait_send()
            return False
        return True


def lanes(group):
    return slice(group * LANES, (group + 1) * LANES)


def line(vector, group):
    return vector[lanes(group)].reshape(1, LANES)


def by_eight(value):
    return jnp.sum(value.reshape(-1, 8, LANES), axis=0)


def gelu_parts(pre_act):
    density = jnp.exp(-0.5 * pre_act * pre_act) * 0.3989422804014327
    t = pl.reciprocal(1.0 + 0.2316419 * jnp.abs(pre_act), approx=False)
    series = 1.781477937 + t * (-1.821255978 + t * 1.330274429)
    series = t * (0.319381530 + t * (-0.356563782 + t * series))
    tail = density * series
    mass = jnp.where(pre_act >= 0.0, 1.0 - tail, tail)
    return pre_act * mass, mass + pre_act * density


def spread_tissue(table, mask):
    tile = lax.axis_index("tile")
    mask[:, 96:WIDE, :] = jnp.zeros((4, WIDE - 96, LANES), jnp.float32)
    for place in range(4):
        row = jnp.clip(2 * tile - 1 + place, 0, 63)
        inside = 1.0
        if place == 0:
            inside = jnp.where(tile > 0, 1.0, 0.0)
        if place == 3:
            inside = jnp.where(tile < 31, 1.0, 0.0)
        for column in range(COLS):
            live = jnp.where(table[column, 0, row] >= 0, 1.0, 0.0) * inside
            mask[place, column * TP : (column + 1) * TP, :] = jnp.full((TP, LANES), live, jnp.float32)


def fill(feat, cot, mask, padded, cot_masked):
    edge = jnp.zeros((3, ROWS + 2 * REACH, 8, LANES), jnp.float32)
    padded[:, :, 0:8, :] = edge
    padded[:, :, 104:112, :] = edge
    padded[:, :, 112:120, :] = edge

    def row(i, carry):
        live = mask[1 + i // TP][:BREADTH]
        cells = feat[i].astype(jnp.float32)
        pull = cot[i].astype(jnp.float32)
        for group in range(GROUPS):
            padded[group, i + REACH, 8 : 8 + BREADTH, :] = cells[:, lanes(group)] * live
            end = pl.ds(pl.multiple_of(i * WIDE + WIDE - 8, 8), 8)
            cot_masked[group, end, :] = jnp.zeros((8, LANES), jnp.float32)
            place = pl.ds(pl.multiple_of(i * WIDE, 8), BREADTH)
            cot_masked[group, place, :] = pull[:, lanes(group)] * live
        return carry

    lax.fori_loop(0, ROWS, row, 0)


def fill_halo(halo, mask, padded):
    def row(i, carry):
        for side in range(2):
            live = mask[3 * side][:BREADTH]
            cells = halo[side, i].astype(jnp.float32)
            for group in range(GROUPS):
                padded[group, i + side * (ROWS + REACH), 8 : 8 + BREADTH, :] = (
                    cells[:, lanes(group)] * live
                )
        return carry

    lax.fori_loop(0, REACH, row, 0)


def spread_taps(weight, taps, bias, bias_rows):
    for group in range(GROUPS):
        bias_rows[group] = jnp.broadcast_to(line(bias, group), (8, LANES))
    for tap in range(K * K):
        for group in range(GROUPS):
            taps[group, tap] = jnp.broadcast_to(weight[tap // K, tap % K : tap % K + 1, lanes(group)], (8, LANES))


def conv(padded, taps, bias_rows, conv_out):
    def tile(step, carry):
        group, column = step // 13, step % 13
        total = jnp.zeros((ROWS, 8, LANES), jnp.float32) + bias_rows[group]
        for col_tap in range(K):
            window = padded[group, :, pl.ds(8 * column + 5 + col_tap, 8), :]
            for row_tap in range(K):
                total = total + window[row_tap : row_tap + ROWS] * taps[group, row_tap * K + col_tap]
        for i in range(ROWS):
            conv_out[group, pl.ds(pl.multiple_of(i * WIDE + 8 * column, 8), 8), :] = total[i]
        return carry

    lax.fori_loop(0, GROUPS * 13, tile, 0)


def conv_grad(first, last, padded, grad_conv, tap_sums):
    def unit(step, carry):
        group, col_tap = step // K, step % K
        totals = [jnp.zeros((8, LANES), jnp.float32)] * K
        for column in range(13):
            pull = jnp.stack(
                [
                    grad_conv[group, i * WIDE + 8 * column : i * WIDE + 8 * column + 8, :]
                    for i in range(ROWS)
                ]
            )
            window = padded[group, :, pl.ds(8 * column + 5 + col_tap, 8), :]
            for row_tap in range(K):
                totals[row_tap] = totals[row_tap] + jnp.sum(
                    window[row_tap : row_tap + ROWS] * pull, axis=0
                )
        for row_tap in range(K):
            tap_sums[group, row_tap * K + col_tap] = totals[row_tap]
        return carry

    lax.fori_loop(first, last, unit, 0)


def norm(conv_out, inv_std, gain, offset, normed):
    def block(step, carry):
        place = pl.ds(pl.multiple_of(step * NORM_ROWS, 16), NORM_ROWS)
        held = [conv_out[group, place, :] for group in range(GROUPS)]
        mean = jnp.sum(held[0] + held[1] + held[2], axis=-1, keepdims=True) * (1.0 / C)
        held = [item - mean for item in held]
        squares = held[0] * held[0] + held[1] * held[1] + held[2] * held[2]
        var = jnp.sum(squares, axis=-1, keepdims=True) * (1.0 / C)
        inv = jnp.broadcast_to(lax.rsqrt(var + 1e-06), (NORM_ROWS, LANES))
        inv_std[place, :] = inv
        for group in range(GROUPS):
            centred = held[group] * inv
            conv_out[group, place, :] = centred
            normed[place, lanes(group)] = (
                centred * line(gain, group) + line(offset, group)
            ).astype(jnp.bfloat16)
        return carry

    lax.fori_loop(0, CELLS // NORM_ROWS, block, 0)


def branch_grad(cot_masked, scale, grad_branch, sums):
    def block(step, carry):
        place = pl.ds(pl.multiple_of(step * NORM_ROWS, 16), NORM_ROWS)
        for group in range(GROUPS):
            pull = cot_masked[group, place, :] * (line(scale, group) * LOSS_SCALE)
            grad_branch[place, lanes(group)] = pull.astype(jnp.bfloat16)
            sums[group] += by_eight(pull)
        return carry

    lax.fori_loop(0, CELLS // NORM_ROWS, block, 0)


def turn(index, rows, turned):
    place = slice(index * LANES, (index + 1) * LANES)
    turned[:, place] = rows[place, :].T


def nt(left, right):
    return lax.dot_general(
        left, right, (((1,), (1,)), ((), ())), preferred_element_type=jnp.float32
    )


def rows_of(block):
    return slice(block * PAIR, (block + 1) * PAIR)


def mlp_enter(chunk, block, normed, grad_branch, w_in, w_out, pre_act, pull):
    units = slice(chunk * CHUNK, (chunk + 1) * CHUNK)
    place = rows_of(block)
    pre_act[...] = jnp.dot(normed[place, :], w_in[:, units], preferred_element_type=jnp.float32)
    pull[...] = nt(grad_branch[place, :], w_out[units, :])


def mlp_strips(chunk, block, b_in, pre_act, pull, hidden, grad_pre, in_sums):
    units = slice(chunk * CHUNK, (chunk + 1) * CHUNK)
    bias = b_in[units].reshape(1, CHUNK)
    total = in_sums[:, units]
    for first in range(0, PAIR, STRIP):
        strip = slice(first, first + STRIP)
        place = slice(block * PAIR + first, block * PAIR + first + STRIP)
        activ, slope = gelu_parts(pre_act[strip, :] + bias)
        hidden[place, :] = activ.astype(jnp.bfloat16)
        back = pull[strip, :] * slope
        total = total + back[:8] + back[8:]
        grad_pre[place, :] = back.astype(jnp.bfloat16)
    in_sums[:, units] = total


def mlp_leave(chunk, block, hidden, grad_pre, w_in, w_out, b_out, branch, grad_xn):
    units = slice(chunk * CHUNK, (chunk + 1) * CHUNK)
    place = rows_of(block)
    out = jnp.dot(hidden[place, :], w_out[units, :], preferred_element_type=jnp.float32)
    back = nt(grad_pre[place, :], w_in[:, units])
    if chunk == 0:
        branch[place, :] = out + b_out[...].reshape(1, C)
        grad_xn[place, :] = back
    else:
        branch[place, :] += out
        grad_xn[place, :] += back


def weight_grads(chunk, normed_t, grad_branch_t, hidden, grad_pre, large):
    first = jnp.dot(normed_t[...], grad_pre[...], preferred_element_type=jnp.float32)
    for group in range(CHUNK // LANES):
        large[chunk, 0, group * C : (group + 1) * C, :] = first[:, lanes(group)]
    second = jnp.dot(grad_branch_t[...], hidden[...], preferred_element_type=jnp.float32).T
    for group in range(GROUPS):
        large[chunk, 1, group * CHUNK : (group + 1) * CHUNK, :] = second[:, lanes(group)]


def after_mlp(first, last, branch, grad_xn, cot_masked, padded, centred, inv_std, mask, scale, gain, mixed, grad_conv, sums):
    def part(i, start, size, totals):
        totals = list(totals)
        place = pl.ds(pl.multiple_of(i * WIDE + start, 8), size)
        live = mask[1 + i // TP, start : start + size]
        used = min(BREADTH - start, size)
        kept = []
        for group in range(GROUPS):
            out = branch[place, lanes(group)].astype(jnp.bfloat16).astype(jnp.float32)
            totals[group] = totals[group] + by_eight(cot_masked[group, place, :] * out)
            cells = padded[group, i + REACH, 8 + start : 8 + start + size, :]
            cells = cells + live * (line(scale, group) * out)
            kept.append(cells[:used].astype(jnp.bfloat16))
        pulls, held = [], []
        for group in range(GROUPS):
            pull = grad_xn[place, lanes(group)].astype(jnp.bfloat16).astype(jnp.float32)
            cen = centred[group, place, :]
            totals[3 + group] = totals[3 + group] + by_eight(pull * cen)
            totals[6 + group] = totals[6 + group] + by_eight(pull)
            pulls.append(pull * line(gain, group))
            held.append(cen)
        mean = jnp.sum(pulls[0] + pulls[1] + pulls[2], axis=-1, keepdims=True) * (1.0 / C)
        along = pulls[0] * held[0] + pulls[1] * held[1] + pulls[2] * held[2]
        along = jnp.sum(along, axis=-1, keepdims=True) * (1.0 / C)
        inv = inv_std[place, :]
        for group in range(GROUPS):
            pulls[group] = inv * (pulls[group] - mean - held[group] * along)
            totals[9 + group] = totals[9 + group] + by_eight(pulls[group])
        for group in range(GROUPS):
            mixed[i, start : start + used, lanes(group)] = kept[group]
            grad_conv[group, place, :] = pulls[group]
        return tuple(totals)

    def row(i, totals):
        return part(i, 48, 56, part(i, 0, 48, totals))

    totals = lax.fori_loop(first, last, row, tuple(sums[3 + index] for index in range(12)))
    for index in range(12):
        sums[3 + index] = totals[index]


def put(small, place, value):
    small[place : place + 1, :] = jnp.sum(value, axis=0, keepdims=True)


def collect_vectors(sums, in_sums, small):
    small[168:, :] = jnp.zeros((2 * LANES - 168, LANES), jnp.float32)
    for index in range(15):
        value = sums[index]
        put(small, 147 + index, value * LOSS_SCALE if 3 <= index < 6 else value)
    for group in range(HID // LANES):
        put(small, 162 + group, in_sums[:, lanes(group)])


def collect_taps(tap_sums, small):
    for group in range(GROUPS):
        for tap in range(K * K):
            put(small, group * K * K + tap, tap_sums[group, tap])


X_FIRST, Y_FIRST = (("x", "z"), ("y",)), (("y", "z"), ("x",))
Z_FIRST = (("z", "y"), ("x",))
PIECES = (
    (0, 0, 1024, X_FIRST),
    (0, 1024, 512, Y_FIRST),
    (1, 0, 1024, Y_FIRST),
    (1, 1024, 512, X_FIRST),
    (2, 0, 512, X_FIRST),
    (2, 512, 512, Y_FIRST),
    (2, 1024, 512, Z_FIRST),
)


def plan():
    return [Sum(rows, jnp.bfloat16, *order) for _, _, rows, order in PIECES] + [Spread()]


def work_scratch():
    def f32(*shape):
        return pltpu.VMEM(shape, jnp.float32)

    def b16(*shape):
        return pltpu.VMEM(shape, jnp.bfloat16)

    return [
        b16(2, REACH, BREADTH, C),
        pltpu.SemaphoreType.DMA((2,)),
        pltpu.SemaphoreType.DMA((2,)),
        f32(GROUPS, ROWS + 2 * REACH, 120, LANES),
        f32(GROUPS, CELLS, LANES),
        f32(GROUPS, K * K, 8, LANES),
        f32(GROUPS, CELLS, LANES),
        f32(CELLS, LANES),
        b16(PADDED, C),
        b16(PADDED, C),
        b16(C, PADDED),
        b16(C, PADDED),
        b16(2, PADDED, CHUNK),
        b16(2, PADDED, CHUNK),
        f32(CELLS, C),
        f32(CELLS, C),
        f32(8, HID),
        f32(15, 8, LANES),
        f32(GROUPS, K * K, 8, LANES),
        f32(GROUPS, CELLS, LANES),
        f32(CHUNKS, 2, 1536, LANES),
        f32(2 * LANES, LANES),
        b16(CHUNKS, 2, 1536, LANES),
        f32(2 * LANES, LANES),
        b16(ROWS, BREADTH, C),
        pltpu.SemaphoreType.DMA((len(PIECES) + 2,)),
        f32(4, WIDE, LANES),
        f32(GROUPS, 8, LANES),
        b16(ROWS, BREADTH, C),
        b16(C, HID),
        b16(HID, C),
        pltpu.SemaphoreType.DMA((3,)),
        f32(2, PAIR, CHUNK),
        f32(2, PAIR, CHUNK),
    ]


def block_kernel(
    feat, cot_in, table, dw_weight, dw_bias, gain, offset, w_in_in, b_in, w_out_in, b_out, scale,
    mixed_out, large_out, small_out, *refs
):
    refs = list(refs)
    own = len(work_scratch())
    (
        halo, halo_send, halo_recv, padded, cot_masked, taps, centred, inv_std, normed, grad_branch,
        normed_t, grad_branch_t, hidden, grad_pre, branch, grad_xn, in_sums, sums, tap_sums,
        grad_conv, large, small, large_held, small_held, mixed, out_sems,
        mask, bias_rows, cot, w_in, w_out, in_sems, pre_act, pull,
    ) = refs[:own]
    refs = refs[own:]
    where = coordinates()
    core, tile = where["core"], lax.axis_index("tile")
    loads = [
        pltpu.make_async_copy(source, target, in_sems.at[index])
        for index, (source, target) in enumerate(((cot_in, cot), (w_in_in, w_in), (w_out_in, w_out)))
    ]
    for made in loads:
        made.start()
    greeting = enter(where)
    spread_tissue(table, mask)
    spread_taps(dw_weight, taps, dw_bias, bias_rows)
    pl.semaphore_wait(*greeting)
    halves = []
    for side, step, first in ((0, 1, ROWS - REACH), (1, 31, 0)):
        made = pltpu.make_async_remote_copy(
            src_ref=feat.at[pl.ds(first, REACH)],
            dst_ref=halo.at[side],
            send_sem=halo_send.at[side],
            recv_sem=halo_recv.at[side],
            device_id=(where["z"], (tile + step) % 32),
            device_id_type=MESH,
        )
        made.start()
        halves.append(made)
    running = []
    for index, item in enumerate(plan()):
        count = len(item.scratch())
        mine, refs = refs[:count], refs[count:]
        if index < len(PIECES):
            chunk, start, rows, _ = PIECES[index]
            span = pl.ds(start, rows)
            keep, send = large.at[chunk, core, span, :], large.at[chunk, 1 - core, span, :]
            item.bind(where, keep, send, large_held.at[chunk, :, span, :], mine)
        else:
            item.bind(where, small, small_held, mine)
        running.append(item)

    copies = []

    def store(source, target):
        made = pltpu.make_async_copy(source, target, out_sems.at[len(copies)])
        made.start()
        copies.append(made)

    def advance(*which):
        for index, item in enumerate(running):
            chunk = PIECES[index][0] if index < len(PIECES) else CHUNKS
            before = item.phase
            if chunk in which and not item.advance() and item.phase > before:
                if chunk < CHUNKS:
                    _, start, rows, _ = PIECES[index]
                    span = pl.ds(start, rows)
                    store(large_held.at[chunk, :, span, :], large_out.at[chunk, :, span, :])
                else:
                    store(small_held, small_out)

    sums[...] = jnp.zeros(sums.shape, jnp.float32)
    in_sums[...] = jnp.zeros(in_sums.shape, jnp.float32)
    for rows in (normed, grad_branch, hidden.at[0], hidden.at[1], grad_pre.at[0], grad_pre.at[1]):
        rows[CELLS:, :] = jnp.zeros((PADDED - CELLS, rows.shape[1]), jnp.bfloat16)
    loads[0].wait()
    fill(feat, cot, mask, padded, cot_masked)
    branch_grad(cot_masked, scale, grad_branch, sums)
    for made in halves:
        made.wait_recv()
    fill_halo(halo, mask, padded)
    conv(padded, taps, bias_rows, centred)
    norm(centred, inv_std, gain, offset, normed)
    loads[1].wait()
    loads[2].wait()

    steps = [(chunk, block) for chunk in range(CHUNKS) for block in range(BLOCKS)]

    def enter_step(place):
        if place < len(steps):
            chunk, block = steps[place]
            side = place % 2
            mlp_enter(
                chunk, block, normed, grad_branch, w_in, w_out, pre_act.at[side], pull.at[side]
            )

    def leave_step(place):
        chunk, block = steps[place]
        half = chunk % 2
        mlp_leave(
            chunk, block, hidden.at[half], grad_pre.at[half], w_in, w_out, b_out, branch, grad_xn
        )

    def finish_chunk(chunk):
        half = chunk % 2
        weight_grads(chunk, normed_t, grad_branch_t, hidden.at[half], grad_pre.at[half], large)

    after_block = {(1, 0): (0,), (1, 4): (0,), (2, 0): (1,), (2, 3): (0,), (2, 4): (1,)}
    enter_step(0)
    for place, (chunk, block) in enumerate(steps):
        half, side = chunk % 2, place % 2
        enter_step(place + 1)
        mlp_strips(
            chunk, block, b_in, pre_act.at[side], pull.at[side], hidden.at[half], grad_pre.at[half],
            in_sums,
        )
        if place < 6:
            for index in (2 * place, 2 * place + 1):
                turn(index, normed, normed_t)
                turn(index, grad_branch, grad_branch_t)
        if place > 0:
            leave_step(place - 1)
        if block == 0 and chunk > 0:
            finish_chunk(chunk - 1)
        advance(*after_block.get((chunk, block), ()))
    leave_step(len(steps) - 1)
    finish_chunk(CHUNKS - 1)
    advance(2)
    advance(0)
    first = 0
    for last, which in ((8, (0,)), (11, (2,)), (14, (1,))):
        after_mlp(
            first, last, branch, grad_xn, cot_masked, padded, centred, inv_std, mask, scale, gain, mixed,
            grad_conv, sums,
        )
        for chunk in which:
            advance(chunk)
        first = last
    store(mixed, mixed_out)
    collect_vectors(sums, in_sums, small)
    first = 0
    for last, which in ((5, (0,)), (10, (2, 1)), (16, (2,)), (21, (2,))):
        conv_grad(first, last, padded, grad_conv, tap_sums)
        for chunk in which:
            advance(chunk)
        first = last
    collect_taps(tap_sums, small)
    for chunk in (3, 1, 0, 3, 2, 3, 1, 2, 3, 1, 2):
        advance(chunk)
    while any(item.phase < item.phases for item in running):
        advance(2)
        advance(3)
        advance(1)
        advance(0)
    for made in copies:
        made.wait()
    for made in halves:
        made.wait_send()


def run_block(*operands):
    scratch = work_scratch()
    spaces = [pltpu.VMEM] * len(operands)
    spaces[1] = spaces[7] = spaces[9] = pl.ANY
    spaces[2] = pltpu.SMEM
    for item in plan():
        scratch += item.scratch()
    return pl.pallas_call(
        block_kernel,
        out_shape=(
            jax.ShapeDtypeStruct((ROWS, BREADTH, C), jnp.bfloat16),
            jax.ShapeDtypeStruct((CHUNKS, 2, 1536, LANES), jnp.bfloat16),
            jax.ShapeDtypeStruct((2 * LANES, LANES), jnp.float32),
        ),
        in_specs=[pl.BlockSpec(memory_space=space) for space in spaces],
        out_specs=(pl.BlockSpec(memory_space=pl.ANY),) * 3,
        scratch_shapes=scratch,
        compiler_params=pltpu.CompilerParams(
            collective_id=0, has_side_effects=True, vmem_limit_bytes=60 * 1024 * 1024
        ),
    )(*operands)


def finish_kernel(
    mixed_in, large_in, small_in, mixed, dw, dwb, ln_gain, ln_bias, w1_out, b1, w2_out, b2, scale,
    large, small, w1, w2, held, in_sems, out_sems
):
    arrive = pltpu.make_async_copy(mixed_in, held, in_sems.at[2 * CHUNKS + 1])
    leave = pltpu.make_async_copy(held, mixed, out_sems.at[2 * CHUNKS])
    little = pltpu.make_async_copy(small_in, small, in_sems.at[2 * CHUNKS])
    pieces = [(chunk, half) for chunk in range(CHUNKS) for half in range(2)]
    loads = [
        pltpu.make_async_copy(large_in.at[piece], large.at[piece], in_sems.at[index])
        for index, piece in enumerate(pieces)
    ]
    for made in [little, arrive] + loads:
        made.start()
    little.wait()

    def row(place):
        return small[place : place + 1, :]

    for group in range(GROUPS):
        for tap in range(K * K):
            dw[tap // K, tap % K : tap % K + 1, lanes(group)] = row(group * K * K + tap)
    for index, target in enumerate((b2, scale, ln_gain, ln_bias, dwb)):
        for group in range(GROUPS):
            target[lanes(group)] = row(147 + index * GROUPS + group).reshape(LANES)
    for group in range(HID // LANES):
        b1[lanes(group)] = row(162 + group).reshape(LANES)

    arrive.wait()
    leave.start()
    stores = []
    for index, (chunk, half) in enumerate(pieces):
        loads[index].wait()
        units = slice(chunk * CHUNK, (chunk + 1) * CHUNK)
        if half == 0:
            for group in range(CHUNK // LANES):
                first = chunk * CHUNK + group * LANES
                w1[:, first : first + LANES] = large[
                    chunk, 0, group * C : (group + 1) * C, :
                ].astype(jnp.float32)
            made = pltpu.make_async_copy(w1.at[:, units], w1_out.at[:, units], out_sems.at[index])
        else:
            for group in range(GROUPS):
                w2[units, lanes(group)] = large[
                    chunk, 1, group * CHUNK : (group + 1) * CHUNK, :
                ].astype(jnp.float32)
            made = pltpu.make_async_copy(w2.at[units, :], w2_out.at[units, :], out_sems.at[index])
        made.start()
        stores.append(made)
    for made in stores + [leave]:
        made.wait()


def finish(mixed, large, small):
    def f32(*shape):
        return jax.ShapeDtypeStruct(shape, jnp.float32)

    vector = f32(C)
    spaces = [pltpu.VMEM] * 10
    spaces[0] = spaces[5] = spaces[7] = pl.ANY
    return pl.pallas_call(
        finish_kernel,
        out_shape=(
            jax.ShapeDtypeStruct(mixed.shape, mixed.dtype), f32(K, K, C), vector, vector, vector,
            f32(C, HID), f32(HID), f32(HID, C), vector, vector,
        ),
        in_specs=[pl.BlockSpec(memory_space=pl.ANY)] * 3,
        out_specs=tuple(pl.BlockSpec(memory_space=space) for space in spaces),
        scratch_shapes=[
            pltpu.VMEM(large.shape, large.dtype),
            pltpu.VMEM(small.shape, small.dtype),
            pltpu.VMEM((C, HID), jnp.float32),
            pltpu.VMEM((HID, C), jnp.float32),
            pltpu.VMEM(mixed.shape, mixed.dtype),
            pltpu.SemaphoreType.DMA((2 * CHUNKS + 2,)),
            pltpu.SemaphoreType.DMA((2 * CHUNKS + 1,)),
        ],
        compiler_params=pltpu.CompilerParams(vmem_limit_bytes=60 * 1024 * 1024),
    )(mixed, large, small)


def local(
    features,
    cotangent,
    owner_slot,
    dw_weight,
    dw_bias,
    ln_gain,
    ln_bias,
    w_in,
    b_in,
    w_out,
    b_out,
    layer_scale,
):
    mixed, large, small = run_block(
        features[0],
        cotangent[0],
        owner_slot.transpose(2, 0, 1),
        dw_weight,
        dw_bias,
        ln_gain,
        ln_bias,
        w_in,
        b_in,
        w_out,
        b_out,
        layer_scale,
    )
    outs = finish(mixed, large, small)
    return (outs[0][None],) + tuple(outs[1:])


def solution(mesh):
    placed = (
        P("slide", "tile", None, None),
        P("slide", "tile", None, None),
        P("slide", None, None),
        P(),
        P(),
        P(),
        P(),
        P(),
        P(),
        P(),
        P(),
        P(),
    )
    return jax.shard_map(
        local,
        mesh=mesh,
        in_specs=placed,
        out_specs=(P("slide", "tile", None, None), P(), P(), P(), P(), P(), P(), P(), P(), P()),
        check_vma=False,
    )
```

```python
import math

import jax
import jax.numpy as jnp
from jax import lax
from jax.experimental import pallas as pl
from jax.experimental.pallas import tpu as pltpu
from jax.sharding import PartitionSpec as P

C = 384
HID = 1536
K = 7
TP = 7
COLS = 14
OWN = 16
ROWS = 14
BREADTH = 98
WIDE = 104
CELLS = ROWS * WIDE
PADDED = 1536
REACH = 3
CHUNK = 512
CHUNKS = HID // CHUNK
PAIR = 2 * WIDE
BLOCKS = CELLS // PAIR
NORM_ROWS = 112
STRIP = 16
GROUPS = C // 128
LOSS_SCALE = 1.0 / math.sqrt(8 * 32 * OWN * TP * TP)

CORES = 2
SIZES = {"x": 4, "y": 4, "z": 8}
LANES = 128
MESH = pl.DeviceIdType.MESH


def coordinates():
    tile = lax.axis_index("tile")
    return {
        "z": lax.axis_index("slide"),
        "y": tile // 8,
        "x": (tile // 2) % 4,
        "core": tile % 2,
    }


def device_at(where):
    return (where["z"], where["y"] * 8 + where["x"] * 2 + where["core"])


def peer_along(where, axis, distance):
    size = SIZES[axis]
    position = (where[axis] + distance) % size
    return position, device_at({**where, axis: position})


def stack_peer(where, distance):
    place = (where["z"] * 2 + where["core"] + distance) % 16
    return place, device_at({**where, "z": place // 2, "core": place % 2})


def plane_peer(where, distance):
    place = (where["y"] * 4 + where["x"] + distance) % 16
    return place, device_at({**where, "y": place // 4, "x": place % 4})


def enter(where):
    tile = lax.axis_index("tile")
    peers = [(where["z"], (tile + step) % 32) for step in (1, 31)]
    for step in range(1, 16):
        peers += [stack_peer(where, step)[1], plane_peer(where, step)[1]]
    barrier = pltpu.get_barrier_semaphore()
    for peer in peers:
        pl.semaphore_signal(barrier, inc=1, device_id=peer, device_id_type=MESH)
    return barrier, len(peers)


class Sum:
    def __init__(self, rows, dtype, scatter, exchange):
        self.rows, self.dtype = rows, dtype
        self.scatter, self.exchange = scatter, exchange
        self.heights = [rows]
        for axis in scatter:
            self.heights.append(self.heights[-1] // SIZES[axis])
        self.phases = 2 * len(scatter) + len(exchange) + 3

    def scratch(self):
        shapes = [pltpu.VMEM((self.rows, LANES), jnp.float32)]
        for axis, before, after in zip(self.scatter, self.heights, self.heights[1:]):
            shapes.append(pltpu.VMEM((before, LANES), jnp.float32))
            shapes.append(pltpu.VMEM((before, LANES), self.dtype))
            shapes.append(pltpu.VMEM((SIZES[axis] - 1, after, LANES), self.dtype))
        for axis in self.exchange:
            shapes.append(pltpu.VMEM((SIZES[axis], self.heights[-1], LANES), self.dtype))
        shapes.append(pltpu.SemaphoreType.DMA((self.phases,)))
        shapes.append(pltpu.SemaphoreType.DMA((self.phases,)))
        return shapes

    def bind(self, where, keep, send, result, refs):
        refs = list(refs)
        self.where, self.keep, self.send, self.result = where, keep, send, result
        self.landed = refs.pop(0)
        self.levels = [tuple(refs.pop(0) for _ in range(3)) for _ in self.scatter]
        self.slots = [refs.pop(0) for _ in self.exchange]
        self.send_sems, self.recv_sems = refs
        self.flying = []
        self.done = []
        self.phase = 0
        offset = 0
        self.offsets = [offset]
        for axis, height in zip(self.scatter, self.heights[1:]):
            offset = offset + where[axis] * height
            self.offsets.append(offset)
        return self

    def copy(self, source, target, device, start=True):
        made = pltpu.make_async_remote_copy(
            src_ref=source,
            dst_ref=target,
            send_sem=self.send_sems.at[self.phase],
            recv_sem=self.recv_sems.at[self.phase],
            device_id=device,
            device_id_type=MESH,
        )
        if start:
            made.start()
        return made

    def fly(self, everything, device):
        self.flying.append(self.copy(everything, everything, device, start=False))

    def land(self):
        for made in self.flying:
            made.wait_recv()
        self.done += self.flying
        self.flying = []

    def rows_at(self, level):
        return pl.ds(pl.multiple_of(self.offsets[level], 16), self.heights[level])

    def start_core(self):
        other = device_at({**self.where, "core": 1 - self.where["core"]})
        self.copy(self.send, self.landed, other)
        self.fly(self.landed, other)

    def start_scatter(self, index, total):
        axis, height = self.scatter[index], self.heights[index + 1]
        held, outgoing, incoming = self.levels[index]
        held[...] = total
        outgoing[...] = total.astype(self.dtype)
        for step in range(1, SIZES[axis]):
            position, device = peer_along(self.where, axis, step)
            self.copy(
                outgoing.at[pl.ds(pl.multiple_of(position * height, 16), height), :],
                incoming.at[step - 1],
                device,
            )
        self.fly(incoming, device)

    def finish_scatter(self, index):
        axis, height = self.scatter[index], self.heights[index + 1]
        held, _, incoming = self.levels[index]
        total = held[pl.ds(pl.multiple_of(self.where[axis] * height, 16), height), :]
        for step in range(SIZES[axis] - 1):
            total = total + incoming[step].astype(jnp.float32)
        return total

    def start_exchange(self, index, total):
        axis, slots = self.exchange[index], self.slots[index]
        me = self.where[axis]
        slots[me] = total.astype(self.dtype)
        for step in range(1, SIZES[axis]):
            _, device = peer_along(self.where, axis, step)
            self.copy(slots.at[me], slots.at[me], device)
        self.fly(slots.at[pl.ds(0, SIZES[axis] - 1)], device)

    def finish_exchange(self, index):
        axis, slots = self.exchange[index], self.slots[index]
        total = slots[0].astype(jnp.float32)
        for place in range(1, SIZES[axis]):
            total = total + slots[place].astype(jnp.float32)
        return total

    def start_gather(self, index):
        axis, core = self.scatter[index], self.where["core"]
        block = self.result.at[core, self.rows_at(index + 1), :]
        for step in range(1, SIZES[axis]):
            _, device = peer_along(self.where, axis, step)
            self.copy(block, block, device)
        count = (SIZES[axis] - 1) * self.heights[index + 1]
        self.fly(self.result.at[core, pl.ds(0, count), :], device)

    def advance(self):
        phase, core = self.phase, self.where["core"]
        deep, wide = len(self.scatter), len(self.exchange)
        if phase >= self.phases:
            return False
        self.land()
        more = self.step(phase, deep, wide, core)
        self.phase += 1
        return more

    def step(self, phase, deep, wide, core):
        if phase == 0:
            self.start_core()
            return True
        if phase == 1:
            total = self.keep[...] + self.landed[...]
            self.start_scatter(0, total)
            return True
        if phase <= deep + wide:
            if phase <= deep:
                total = self.finish_scatter(phase - 2)
                self.start_scatter(phase - 1, total)
                return True
            index = phase - deep - 1
            total = self.finish_scatter(deep - 1) if index == 0 else self.finish_exchange(index - 1)
            self.start_exchange(index, total)
            return True
        step = phase - deep - wide - 1
        if step == 0:
            total = self.finish_exchange(wide - 1)
            self.result[core, self.rows_at(deep), :] = total.astype(self.dtype)
        if step < deep:
            self.start_gather(deep - 1 - step)
            return True
        if step == deep:
            other = device_at({**self.where, "core": 1 - core})
            self.copy(self.result.at[core], self.result.at[core], other)
            self.fly(self.result.at[core], other)
            return True
        for made in self.done:
            made.wait_send()
        return False


class Spread:
    ROWS = 16
    phases = 4

    def scratch(self):
        return [
            pltpu.VMEM((15, self.ROWS, LANES), jnp.float32),
            pltpu.VMEM((16, self.ROWS, LANES), jnp.float32),
            pltpu.SemaphoreType.DMA((3,)),
            pltpu.SemaphoreType.DMA((3,)),
        ]

    def bind(self, where, source, result, refs):
        self.where, self.source, self.result = where, source, result
        self.landed, self.slots, self.send_sems, self.recv_sems = refs
        self.phase = 0
        self.flying, self.done = [], []
        return self

    copy = Sum.copy
    fly = Sum.fly
    land = Sum.land

    def advance(self):
        phase, where, rows = self.phase, self.where, self.ROWS
        if phase >= self.phases:
            return False
        self.land()
        more = self.step(phase, where, rows)
        self.phase += 1
        return more

    def step(self, phase, where, rows):
        place, flat = where["z"] * 2 + where["core"], where["y"] * 4 + where["x"]
        mine = pl.ds(pl.multiple_of(place * rows, rows), rows)
        if phase == 0:
            for step in range(1, 16):
                other, device = stack_peer(where, step)
                block = self.source.at[pl.ds(pl.multiple_of(other * rows, rows), rows), :]
                self.copy(block, self.landed.at[step - 1], device)
            self.fly(self.landed, device)
        elif phase == 1:
            total = self.source[mine, :]
            for step in range(15):
                total = total + self.landed[step]
            self.slots[flat] = total
            for step in range(1, 16):
                _, device = plane_peer(where, step)
                self.copy(self.slots.at[flat], self.slots.at[flat], device)
            self.fly(self.slots.at[pl.ds(0, 15)], device)
        elif phase == 2:
            total = self.slots[0]
            for index in range(1, 16):
                total = total + self.slots[index]
            self.result[mine, :] = total
            block = self.result.at[mine, :]
            for step in range(1, 16):
                _, device = stack_peer(where, step)
                self.copy(block, block, device)
            self.fly(self.result.at[pl.ds(0, 15 * rows), :], device)
        else:
            for made in self.done:
                made.wait_send()
            return False
        return True


def lanes(group):
    return slice(group * LANES, (group + 1) * LANES)


def line(vector, group):
    return vector[lanes(group)].reshape(1, LANES)


def by_eight(value):
    return jnp.sum(value.reshape(-1, 8, LANES), axis=0)


def gelu_parts(pre_act):
    density = jnp.exp(-0.5 * pre_act * pre_act) * 0.3989422804014327
    t = pl.reciprocal(1.0 + 0.2316419 * jnp.abs(pre_act), approx=False)
    series = 1.781477937 + t * (-1.821255978 + t * 1.330274429)
    series = t * (0.319381530 + t * (-0.356563782 + t * series))
    tail = density * series
    mass = jnp.where(pre_act >= 0.0, 1.0 - tail, tail)
    return pre_act * mass, mass + pre_act * density


def spread_tissue(table, mask):
    tile = lax.axis_index("tile")
    mask[:, 96:WIDE, :] = jnp.zeros((4, WIDE - 96, LANES), jnp.float32)
    for place in range(4):
        row = jnp.clip(2 * tile - 1 + place, 0, 63)
        inside = 1.0
        if place == 0:
            inside = jnp.where(tile > 0, 1.0, 0.0)
        if place == 3:
            inside = jnp.where(tile < 31, 1.0, 0.0)
        for column in range(COLS):
            live = jnp.where(table[column, 0, row] >= 0, 1.0, 0.0) * inside
            mask[place, column * TP : (column + 1) * TP, :] = jnp.full((TP, LANES), live, jnp.float32)


def fill(feat, cot, mask, padded, cot_masked):
    edge = jnp.zeros((3, ROWS + 2 * REACH, 8, LANES), jnp.float32)
    padded[:, :, 0:8, :] = edge
    padded[:, :, 104:112, :] = edge
    padded[:, :, 112:120, :] = edge

    def row(i, carry):
        live = mask[1 + i // TP][:BREADTH]
        cells = feat[i].astype(jnp.float32)
        pull = cot[i].astype(jnp.float32)
        for group in range(GROUPS):
            padded[group, i + REACH, 8 : 8 + BREADTH, :] = cells[:, lanes(group)] * live
            end = pl.ds(pl.multiple_of(i * WIDE + WIDE - 8, 8), 8)
            cot_masked[group, end, :] = jnp.zeros((8, LANES), jnp.float32)
            place = pl.ds(pl.multiple_of(i * WIDE, 8), BREADTH)
            cot_masked[group, place, :] = pull[:, lanes(group)] * live
        return carry

    lax.fori_loop(0, ROWS, row, 0)


def fill_halo(halo, mask, padded):
    def row(i, carry):
        for side in range(2):
            live = mask[3 * side][:BREADTH]
            cells = halo[side, i].astype(jnp.float32)
            for group in range(GROUPS):
                padded[group, i + side * (ROWS + REACH), 8 : 8 + BREADTH, :] = (
                    cells[:, lanes(group)] * live
                )
        return carry

    lax.fori_loop(0, REACH, row, 0)


def spread_taps(weight, taps, bias, bias_rows):
    for group in range(GROUPS):
        bias_rows[group] = jnp.broadcast_to(line(bias, group), (8, LANES))
    for tap in range(K * K):
        for group in range(GROUPS):
            taps[group, tap] = jnp.broadcast_to(weight[tap // K, tap % K : tap % K + 1, lanes(group)], (8, LANES))


def conv(padded, taps, bias_rows, conv_out):
    def one(group, carry):
        for column in range(13):
            total = jnp.zeros((ROWS, 8, LANES), jnp.float32) + bias_rows[group]
            for col_tap in range(K):
                window = padded[group, :, 8 * column + 5 + col_tap : 8 * column + 13 + col_tap, :]
                for row_tap in range(K):
                    tap = row_tap * K + col_tap
                    total = total + window[row_tap : row_tap + ROWS] * taps[group, tap]
            for i in range(ROWS):
                conv_out[group, i * WIDE + 8 * column : i * WIDE + 8 * column + 8, :] = total[i]
        return carry

    lax.fori_loop(0, GROUPS, one, 0)


def conv_grad(first, last, padded, grad_conv, tap_sums):
    def unit(step, carry):
        group, col_tap = step // K, step % K
        totals = [jnp.zeros((8, LANES), jnp.float32)] * K
        for column in range(13):
            pull = jnp.stack(
                [
                    grad_conv[group, i * WIDE + 8 * column : i * WIDE + 8 * column + 8, :]
                    for i in range(ROWS)
                ]
            )
            window = padded[group, :, pl.ds(8 * column + 5 + col_tap, 8), :]
            for row_tap in range(K):
                totals[row_tap] = totals[row_tap] + jnp.sum(
                    window[row_tap : row_tap + ROWS] * pull, axis=0
                )
        for row_tap in range(K):
            tap_sums[group, row_tap * K + col_tap] = totals[row_tap]
        return carry

    lax.fori_loop(first, last, unit, 0)


def norm(conv_out, inv_std, gain, offset, normed):
    def block(step, carry):
        place = pl.ds(pl.multiple_of(step * NORM_ROWS, 16), NORM_ROWS)
        held = [conv_out[group, place, :] for group in range(GROUPS)]
        mean = jnp.sum(held[0] + held[1] + held[2], axis=-1, keepdims=True) * (1.0 / C)
        held = [item - mean for item in held]
        squares = held[0] * held[0] + held[1] * held[1] + held[2] * held[2]
        var = jnp.sum(squares, axis=-1, keepdims=True) * (1.0 / C)
        inv = jnp.broadcast_to(lax.rsqrt(var + 1e-06), (NORM_ROWS, LANES))
        inv_std[place, :] = inv
        for group in range(GROUPS):
            centred = held[group] * inv
            conv_out[group, place, :] = centred
            normed[place, lanes(group)] = (
                centred * line(gain, group) + line(offset, group)
            ).astype(jnp.bfloat16)
        return carry

    lax.fori_loop(0, CELLS // NORM_ROWS, block, 0)


def branch_grad(cot_masked, scale, grad_branch, sums):
    def block(step, carry):
        place = pl.ds(pl.multiple_of(step * NORM_ROWS, 16), NORM_ROWS)
        for group in range(GROUPS):
            pull = cot_masked[group, place, :] * (line(scale, group) * LOSS_SCALE)
            grad_branch[place, lanes(group)] = pull.astype(jnp.bfloat16)
            sums[group] += by_eight(pull)
        return carry

    lax.fori_loop(0, CELLS // NORM_ROWS, block, 0)


def turn(rows, turned):
    def block(step, carry):
        place = pl.ds(pl.multiple_of(step * LANES, LANES), LANES)
        turned[:, place] = rows[place, :].T
        return carry

    lax.fori_loop(0, PADDED // LANES, block, 0)


def nt(left, right):
    return lax.dot_general(
        left, right, (((1,), (1,)), ((), ())), preferred_element_type=jnp.float32
    )


def rows_of(block):
    return slice(block * PAIR, (block + 1) * PAIR)


def mlp_enter(chunk, block, normed, grad_branch, w_in, w_out, pre_act, pull):
    units = slice(chunk * CHUNK, (chunk + 1) * CHUNK)
    place = rows_of(block)
    pre_act[...] = jnp.dot(normed[place, :], w_in[:, units], preferred_element_type=jnp.float32)
    pull[...] = nt(grad_branch[place, :], w_out[units, :])


def mlp_strips(chunk, block, b_in, pre_act, pull, hidden, grad_pre, in_sums):
    units = slice(chunk * CHUNK, (chunk + 1) * CHUNK)
    bias = b_in[units].reshape(1, CHUNK)
    total = in_sums[:, units]
    for first in range(0, PAIR, STRIP):
        strip = slice(first, first + STRIP)
        place = slice(block * PAIR + first, block * PAIR + first + STRIP)
        activ, slope = gelu_parts(pre_act[strip, :] + bias)
        hidden[place, :] = activ.astype(jnp.bfloat16)
        back = pull[strip, :] * slope
        total = total + back[:8] + back[8:]
        grad_pre[place, :] = back.astype(jnp.bfloat16)
    in_sums[:, units] = total


def mlp_leave(chunk, block, hidden, grad_pre, w_in, w_out, b_out, branch, grad_xn):
    units = slice(chunk * CHUNK, (chunk + 1) * CHUNK)
    place = rows_of(block)
    out = jnp.dot(hidden[place, :], w_out[units, :], preferred_element_type=jnp.float32)
    back = nt(grad_pre[place, :], w_in[:, units])
    if chunk == 0:
        branch[place, :] = out + b_out[...].reshape(1, C)
        grad_xn[place, :] = back
    else:
        branch[place, :] += out
        grad_xn[place, :] += back


def weight_grads(chunk, normed_t, grad_branch_t, hidden, grad_pre, large):
    first = jnp.dot(normed_t[...], grad_pre[...], preferred_element_type=jnp.float32)
    for group in range(CHUNK // LANES):
        large[chunk, 0, group * C : (group + 1) * C, :] = first[:, lanes(group)]
    second = jnp.dot(grad_branch_t[...], hidden[...], preferred_element_type=jnp.float32).T
    for group in range(GROUPS):
        large[chunk, 1, group * CHUNK : (group + 1) * CHUNK, :] = second[:, lanes(group)]


def after_mlp(first, last, branch, grad_xn, cot_masked, padded, centred, inv_std, mask, scale, gain, mixed, grad_conv, sums):
    def part(i, start, size, totals):
        totals = list(totals)
        place = pl.ds(pl.multiple_of(i * WIDE + start, 8), size)
        live = mask[1 + i // TP, start : start + size]
        used = min(BREADTH - start, size)
        kept = []
        for group in range(GROUPS):
            out = branch[place, lanes(group)].astype(jnp.bfloat16).astype(jnp.float32)
            totals[group] = totals[group] + by_eight(cot_masked[group, place, :] * out)
            cells = padded[group, i + REACH, 8 + start : 8 + start + size, :]
            cells = cells + live * (line(scale, group) * out)
            kept.append(cells[:used].astype(jnp.bfloat16))
        pulls, held = [], []
        for group in range(GROUPS):
            pull = grad_xn[place, lanes(group)].astype(jnp.bfloat16).astype(jnp.float32)
            cen = centred[group, place, :]
            totals[3 + group] = totals[3 + group] + by_eight(pull * cen)
            totals[6 + group] = totals[6 + group] + by_eight(pull)
            pulls.append(pull * line(gain, group))
            held.append(cen)
        mean = jnp.sum(pulls[0] + pulls[1] + pulls[2], axis=-1, keepdims=True) * (1.0 / C)
        along = pulls[0] * held[0] + pulls[1] * held[1] + pulls[2] * held[2]
        along = jnp.sum(along, axis=-1, keepdims=True) * (1.0 / C)
        inv = inv_std[place, :]
        for group in range(GROUPS):
            pulls[group] = inv * (pulls[group] - mean - held[group] * along)
            totals[9 + group] = totals[9 + group] + by_eight(pulls[group])
        for group in range(GROUPS):
            mixed[i, start : start + used, lanes(group)] = kept[group]
            grad_conv[group, place, :] = pulls[group]
        return tuple(totals)

    def row(i, totals):
        return part(i, 48, 56, part(i, 0, 48, totals))

    totals = lax.fori_loop(first, last, row, tuple(sums[3 + index] for index in range(12)))
    for index in range(12):
        sums[3 + index] = totals[index]


def put(small, place, value):
    small[place : place + 1, :] = jnp.sum(value, axis=0, keepdims=True)


def collect_vectors(sums, in_sums, small):
    small[168:, :] = jnp.zeros((2 * LANES - 168, LANES), jnp.float32)
    for index in range(15):
        value = sums[index]
        put(small, 147 + index, value * LOSS_SCALE if 3 <= index < 6 else value)
    for group in range(HID // LANES):
        put(small, 162 + group, in_sums[:, lanes(group)])


def collect_taps(tap_sums, small):
    for group in range(GROUPS):
        for tap in range(K * K):
            put(small, group * K * K + tap, tap_sums[group, tap])


X_FIRST, Y_FIRST = (("x", "z"), ("y",)), (("y", "z"), ("x",))
PIECES = (
    (0, 0, 1024, X_FIRST),
    (0, 1024, 512, Y_FIRST),
    (1, 0, 1024, Y_FIRST),
    (1, 1024, 512, X_FIRST),
    (2, 0, 1024, X_FIRST),
    (2, 1024, 512, Y_FIRST),
)


def plan():
    return [Sum(rows, jnp.bfloat16, *order) for _, _, rows, order in PIECES] + [Spread()]


def work_scratch():
    def f32(*shape):
        return pltpu.VMEM(shape, jnp.float32)

    def b16(*shape):
        return pltpu.VMEM(shape, jnp.bfloat16)

    return [
        b16(2, REACH, BREADTH, C),
        pltpu.SemaphoreType.DMA((2,)),
        pltpu.SemaphoreType.DMA((2,)),
        f32(GROUPS, ROWS + 2 * REACH, 120, LANES),
        f32(GROUPS, CELLS, LANES),
        f32(GROUPS, K * K, 8, LANES),
        f32(GROUPS, CELLS, LANES),
        f32(CELLS, LANES),
        b16(PADDED, C),
        b16(PADDED, C),
        b16(C, PADDED),
        b16(C, PADDED),
        b16(2, PADDED, CHUNK),
        b16(2, PADDED, CHUNK),
        f32(CELLS, C),
        f32(CELLS, C),
        f32(8, HID),
        f32(15, 8, LANES),
        f32(GROUPS, K * K, 8, LANES),
        f32(GROUPS, CELLS, LANES),
        f32(CHUNKS, 2, 1536, LANES),
        f32(2 * LANES, LANES),
        b16(CHUNKS, 2, 1536, LANES),
        f32(2 * LANES, LANES),
        b16(ROWS, BREADTH, C),
        pltpu.SemaphoreType.DMA((len(PIECES) + 2,)),
        f32(4, WIDE, LANES),
        f32(GROUPS, 8, LANES),
        b16(ROWS, BREADTH, C),
        b16(C, HID),
        b16(HID, C),
        pltpu.SemaphoreType.DMA((3,)),
        f32(2, PAIR, CHUNK),
        f32(2, PAIR, CHUNK),
    ]


def block_kernel(
    feat, cot_in, table, dw_weight, dw_bias, gain, offset, w_in_in, b_in, w_out_in, b_out, scale,
    mixed_out, large_out, small_out, *refs
):
    refs = list(refs)
    own = len(work_scratch())
    (
        halo, halo_send, halo_recv, padded, cot_masked, taps, centred, inv_std, normed, grad_branch,
        normed_t, grad_branch_t, hidden, grad_pre, branch, grad_xn, in_sums, sums, tap_sums,
        grad_conv, large, small, large_held, small_held, mixed, out_sems,
        mask, bias_rows, cot, w_in, w_out, in_sems, pre_act, pull,
    ) = refs[:own]
    refs = refs[own:]
    where = coordinates()
    core, tile = where["core"], lax.axis_index("tile")
    loads = [
        pltpu.make_async_copy(source, target, in_sems.at[index])
        for index, (source, target) in enumerate(((cot_in, cot), (w_in_in, w_in), (w_out_in, w_out)))
    ]
    for made in loads:
        made.start()
    greeting = enter(where)
    spread_tissue(table, mask)
    spread_taps(dw_weight, taps, dw_bias, bias_rows)
    pl.semaphore_wait(*greeting)
    halves = []
    for side, step, first in ((0, 1, ROWS - REACH), (1, 31, 0)):
        made = pltpu.make_async_remote_copy(
            src_ref=feat.at[pl.ds(first, REACH)],
            dst_ref=halo.at[side],
            send_sem=halo_send.at[side],
            recv_sem=halo_recv.at[side],
            device_id=(where["z"], (tile + step) % 32),
            device_id_type=MESH,
        )
        made.start()
        halves.append(made)
    running = []
    for index, item in enumerate(plan()):
        count = len(item.scratch())
        mine, refs = refs[:count], refs[count:]
        if index < len(PIECES):
            chunk, start, rows, _ = PIECES[index]
            span = pl.ds(start, rows)
            keep, send = large.at[chunk, core, span, :], large.at[chunk, 1 - core, span, :]
            item.bind(where, keep, send, large_held.at[chunk, :, span, :], mine)
        else:
            item.bind(where, small, small_held, mine)
        running.append(item)

    copies = []

    def store(source, target):
        made = pltpu.make_async_copy(source, target, out_sems.at[len(copies)])
        made.start()
        copies.append(made)

    def advance(*which):
        for index, item in enumerate(running):
            chunk = PIECES[index][0] if index < len(PIECES) else CHUNKS
            before = item.phase
            if chunk in which and not item.advance() and item.phase > before:
                if chunk < CHUNKS:
                    _, start, rows, _ = PIECES[index]
                    span = pl.ds(start, rows)
                    store(large_held.at[chunk, :, span, :], large_out.at[chunk, :, span, :])
                else:
                    store(small_held, small_out)

    sums[...] = jnp.zeros(sums.shape, jnp.float32)
    in_sums[...] = jnp.zeros(in_sums.shape, jnp.float32)
    for rows in (normed, grad_branch, hidden.at[0], hidden.at[1], grad_pre.at[0], grad_pre.at[1]):
        rows[CELLS:, :] = jnp.zeros((PADDED - CELLS, rows.shape[1]), jnp.bfloat16)
    loads[0].wait()
    fill(feat, cot, mask, padded, cot_masked)
    branch_grad(cot_masked, scale, grad_branch, sums)
    turn(grad_branch, grad_branch_t)
    for made in halves:
        made.wait_recv()
    fill_halo(halo, mask, padded)
    conv(padded, taps, bias_rows, centred)
    norm(centred, inv_std, gain, offset, normed)
    turn(normed, normed_t)
    loads[1].wait()
    loads[2].wait()

    steps = [(chunk, block) for chunk in range(CHUNKS) for block in range(BLOCKS)]

    def enter_step(place):
        if place < len(steps):
            chunk, block = steps[place]
            side = place % 2
            mlp_enter(
                chunk, block, normed, grad_branch, w_in, w_out, pre_act.at[side], pull.at[side]
            )

    def leave_step(place):
        chunk, block = steps[place]
        half = chunk % 2
        mlp_leave(
            chunk, block, hidden.at[half], grad_pre.at[half], w_in, w_out, b_out, branch, grad_xn
        )

    def finish_chunk(chunk):
        half = chunk % 2
        weight_grads(chunk, normed_t, grad_branch_t, hidden.at[half], grad_pre.at[half], large)

    after_block = {(1, 0): (0,), (1, 4): (0,), (2, 0): (1,), (2, 3): (0,), (2, 4): (1,)}
    enter_step(0)
    for place, (chunk, block) in enumerate(steps):
        half, side = chunk % 2, place % 2
        enter_step(place + 1)
        mlp_strips(
            chunk, block, b_in, pre_act.at[side], pull.at[side], hidden.at[half], grad_pre.at[half],
            in_sums,
        )
        if place > 0:
            leave_step(place - 1)
        if block == 0 and chunk > 0:
            finish_chunk(chunk - 1)
        advance(*after_block.get((chunk, block), ()))
    leave_step(len(steps) - 1)
    finish_chunk(CHUNKS - 1)
    advance(2)
    advance(0)
    first = 0
    for last, which in ((8, (0,)), (14, (2, 1))):
        after_mlp(
            first, last, branch, grad_xn, cot_masked, padded, centred, inv_std, mask, scale, gain, mixed,
            grad_conv, sums,
        )
        for chunk in which:
            advance(chunk)
        first = last
    store(mixed, mixed_out)
    collect_vectors(sums, in_sums, small)
    first = 0
    for last, which in ((7, (0,)), (14, (2, 1)), (21, (2,))):
        conv_grad(first, last, padded, grad_conv, tap_sums)
        for chunk in which:
            advance(chunk)
        first = last
    collect_taps(tap_sums, small)
    for chunk in (3, 2, 1, 3, 0, 2, 1, 3, 1, 2, 3):
        advance(chunk)
    while any(item.phase < item.phases for item in running):
        advance(2)
        advance(3)
        advance(1)
        advance(0)
    for made in copies:
        made.wait()
    for made in halves:
        made.wait_send()


def run_block(*operands):
    scratch = work_scratch()
    spaces = [pltpu.VMEM] * len(operands)
    spaces[1] = spaces[7] = spaces[9] = pl.ANY
    spaces[2] = pltpu.SMEM
    for item in plan():
        scratch += item.scratch()
    return pl.pallas_call(
        block_kernel,
        out_shape=(
            jax.ShapeDtypeStruct((ROWS, BREADTH, C), jnp.bfloat16),
            jax.ShapeDtypeStruct((CHUNKS, 2, 1536, LANES), jnp.bfloat16),
            jax.ShapeDtypeStruct((2 * LANES, LANES), jnp.float32),
        ),
        in_specs=[pl.BlockSpec(memory_space=space) for space in spaces],
        out_specs=(pl.BlockSpec(memory_space=pl.ANY),) * 3,
        scratch_shapes=scratch,
        compiler_params=pltpu.CompilerParams(
            collective_id=0, has_side_effects=True, vmem_limit_bytes=60 * 1024 * 1024
        ),
    )(*operands)


def finish_kernel(
    mixed_in, large_in, small_in, mixed, dw, dwb, ln_gain, ln_bias, w1_out, b1, w2_out, b2, scale,
    large, small, w1, w2, held, in_sems, out_sems
):
    arrive = pltpu.make_async_copy(mixed_in, held, in_sems.at[2 * CHUNKS + 1])
    leave = pltpu.make_async_copy(held, mixed, out_sems.at[2 * CHUNKS])
    little = pltpu.make_async_copy(small_in, small, in_sems.at[2 * CHUNKS])
    pieces = [(chunk, half) for chunk in range(CHUNKS) for half in range(2)]
    loads = [
        pltpu.make_async_copy(large_in.at[piece], large.at[piece], in_sems.at[index])
        for index, piece in enumerate(pieces)
    ]
    for made in [little, arrive] + loads:
        made.start()
    arrive.wait()
    leave.start()
    stores = []
    for index, (chunk, half) in enumerate(pieces):
        loads[index].wait()
        units = slice(chunk * CHUNK, (chunk + 1) * CHUNK)
        if half == 0:
            for group in range(CHUNK // LANES):
                first = chunk * CHUNK + group * LANES
                w1[:, first : first + LANES] = large[
                    chunk, 0, group * C : (group + 1) * C, :
                ].astype(jnp.float32)
            made = pltpu.make_async_copy(w1.at[:, units], w1_out.at[:, units], out_sems.at[index])
        else:
            for group in range(GROUPS):
                w2[units, lanes(group)] = large[
                    chunk, 1, group * CHUNK : (group + 1) * CHUNK, :
                ].astype(jnp.float32)
            made = pltpu.make_async_copy(w2.at[units, :], w2_out.at[units, :], out_sems.at[index])
        made.start()
        stores.append(made)
    little.wait()

    def row(place):
        return small[place : place + 1, :]

    for group in range(GROUPS):
        for tap in range(K * K):
            dw[tap // K, tap % K : tap % K + 1, lanes(group)] = row(group * K * K + tap)
    for index, target in enumerate((b2, scale, ln_gain, ln_bias, dwb)):
        for group in range(GROUPS):
            target[lanes(group)] = row(147 + index * GROUPS + group).reshape(LANES)
    for group in range(HID // LANES):
        b1[lanes(group)] = row(162 + group).reshape(LANES)
    for made in stores + [leave]:
        made.wait()


def finish(mixed, large, small):
    def f32(*shape):
        return jax.ShapeDtypeStruct(shape, jnp.float32)

    vector = f32(C)
    spaces = [pltpu.VMEM] * 10
    spaces[0] = spaces[5] = spaces[7] = pl.ANY
    return pl.pallas_call(
        finish_kernel,
        out_shape=(
            jax.ShapeDtypeStruct(mixed.shape, mixed.dtype), f32(K, K, C), vector, vector, vector,
            f32(C, HID), f32(HID), f32(HID, C), vector, vector,
        ),
        in_specs=[pl.BlockSpec(memory_space=pl.ANY)] * 3,
        out_specs=tuple(pl.BlockSpec(memory_space=space) for space in spaces),
        scratch_shapes=[
            pltpu.VMEM(large.shape, large.dtype),
            pltpu.VMEM(small.shape, small.dtype),
            pltpu.VMEM((C, HID), jnp.float32),
            pltpu.VMEM((HID, C), jnp.float32),
            pltpu.VMEM(mixed.shape, mixed.dtype),
            pltpu.SemaphoreType.DMA((2 * CHUNKS + 2,)),
            pltpu.SemaphoreType.DMA((2 * CHUNKS + 1,)),
        ],
        compiler_params=pltpu.CompilerParams(vmem_limit_bytes=60 * 1024 * 1024),
    )(mixed, large, small)


def local(
    features,
    cotangent,
    owner_slot,
    dw_weight,
    dw_bias,
    ln_gain,
    ln_bias,
    w_in,
    b_in,
    w_out,
    b_out,
    layer_scale,
):
    mixed, large, small = run_block(
        features[0],
        cotangent[0],
        owner_slot.transpose(2, 0, 1),
        dw_weight,
        dw_bias,
        ln_gain,
        ln_bias,
        w_in,
        b_in,
        w_out,
        b_out,
        layer_scale,
    )
    outs = finish(mixed, large, small)
    return (outs[0][None],) + tuple(outs[1:])


def solution(mesh):
    placed = (
        P("slide", "tile", None, None),
        P("slide", "tile", None, None),
        P("slide", None, None),
        P(),
        P(),
        P(),
        P(),
        P(),
        P(),
        P(),
        P(),
        P(),
    )
    return jax.shard_map(
        local,
        mesh=mesh,
        in_specs=placed,
        out_specs=(P("slide", "tile", None, None), P(), P(), P(), P(), P(), P(), P(), P(), P()),
        check_vma=False,
    )
```
